1024 devices in a mesh: tile: 128 (over y, z_lo, core), case: 8 (over x, z_hi).
Axes of the slice: x: 4, y: 8, z: 16 (z_hi: 2, z_lo: 8; z = z_hi * 8 + z_lo), core: 2. Of those that a mesh axis runs over, the one named last changes fastest.
Arguments:
- checkpoint: bfloat16 [8, 19, 1024, 8, 128], P('case', None, 'tile'), may hold values from 0 to 0.6, as said below
- adjoint_field: float32 [8, 19, 1024, 8, 128], P('case', None, 'tile'), may hold values from -6 to 6
- accel_table: int32 [8, 2, 3], P('case'), may hold values from -20 to 20
- design: float32 [128, 1, 16], P('tile'), may hold values from 0 to 1
- design_mask: int32 [128, 1, 16], P('tile'), may hold values 0 or 1
- first_moment: float32 [128, 1, 16], P('tile'), may hold values from -1 to 1
- second_moment: float32 [128, 1, 16], P('tile'), may hold values from 0.001 to 0.1
Outputs:
- adjoint_start: float32 [8, 19, 1024, 8, 128], P('case', None, 'tile')
- design_new: float32 [128, 1, 16], P('tile')
- first_new: float32 [128, 1, 16], P('tile')
- second_new: float32 [128, 1, 16], P('tile')
The draws below stay inside these ranges and needn't reach their ends.
Inputs may be any that keep to these rules, and one draw needn't show every extreme that they name: `checkpoint`: every population is positive.
All inputs are finite; a program needn't handle non-finite values. No bound on the sum of `design_mask` on one device may be relied on, other than what follows from the above.
Results may differ from the reference program's by a relative error of at most 0.0003.
Values sent between devices are 32-bit elements; how exact they have to be, the bound alone decides.
No kernel may reach another device: no remote copies, remote signals or barrier semaphores. Data moves between devices by JAX's collectives and lax.ppermute only.
A program may use at most 32 MiB of HBM per device.

```python
import math
import jax
import jax.numpy as jnp
import numpy as np
from jax import lax

Q = 19
BLOCK = 8
STEPS = 2
NY = 8
NZ = 128
CASES = 8
NX = 1024
NBX = 128
NBY = 1
NBZ = 16


LATTICE_WEIGHTS = [1.0 / 3.0] + [1.0 / 18.0] * 6 + [1.0 / 36.0] * 12


def draw_checkpoint(key, part):
    key = jax.random.fold_in(key, 11)
    jitter_key = jax.random.fold_in(key, 1)
    weights = jnp.array(LATTICE_WEIGHTS, jnp.float32)[None, :, None, None, None]
    shape = (CASES, Q, NX, NY, NZ)
    level = jnp.ones((CASES, 1, NX, NY, NZ), jnp.float32)
    jitter = jax.random.uniform(jitter_key, shape, jnp.float32, 0.8, 1.2)
    return (weights * level * jitter).astype(jnp.bfloat16)


def plant(entries, stream_key, low, high):
    dims = entries.shape
    spot = [jax.random.randint(jax.random.fold_in(stream_key, axis), (), 0, dims[axis]) for axis in range(len(dims))]
    entries = entries.at[tuple(spot)].set(low)
    longest = dims.index(max(dims))
    spot[longest] = (spot[longest] + 1) % dims[longest]
    return entries.at[tuple(spot)].set(high)


def block_scale(stream_key, shape, cuts, low, largest):
    level = 1.0
    for position, parts in cuts:
        heights = jax.random.uniform(jax.random.fold_in(jax.random.fold_in(stream_key, 6), position), (parts,), jnp.float32, low / len(cuts), largest / len(cuts))
        level = level * jnp.repeat(jnp.exp(heights), shape[position] // parts).reshape((-1,) + (1,) * (len(shape) - 1 - position))
    return level


def normal_values(rng, dims, deviation, most, cuts=(), held_as=jnp.bfloat16):
    loudness = block_scale(rng, dims, cuts, -0.22, 0.18) if cuts else 1.0
    values = jax.random.normal(rng, dims, jnp.float32) * deviation * loudness
    return jnp.minimum(jnp.maximum(values, -most), most).astype(held_as)


def setup_inputs(seed: int = 0) -> dict:
    key_list = jax.random.split(jax.random.key(seed), 8)
    checkpoint = draw_checkpoint(jax.random.fold_in(key_list[7], 71), 0)
    adjoint_field = normal_values(key_list[1], (CASES, Q, NX, NY, NZ), 1.0, 6.0, ((0, 8), (2, 128)), jnp.float32)
    accel_table = plant(jax.random.randint(key_list[2], (CASES, STEPS, 3), -20, 21), jax.random.fold_in(key_list[2], 1), -20, 20).astype(jnp.int32)
    design = jnp.clip(1.0 * jax.random.uniform(key_list[3], (NBX, NBY, NBZ), jnp.float32) ** block_scale(key_list[3], (NBX, NBY, NBZ), ((0, 128),), -0.2, 0.2), 0.0, 1.0)
    design_mask = plant((jax.random.randint(key_list[4], (NBX, NBY, NBZ), 0, 2) < 1).astype(jnp.int32), jax.random.fold_in(key_list[4], 1), 0, 1)
    first_moment = normal_values(key_list[5], (NBX, NBY, NBZ), 0.2, 1.0, ((0, 128),), jnp.float32)
    second_moment = jnp.clip(jnp.exp(math.log(0.1) - 4.6051702 * jax.random.uniform(key_list[6], (NBX, NBY, NBZ), jnp.float32) ** block_scale(key_list[6], (NBX, NBY, NBZ), ((0, 128),), -0.2, 0.2)), 0.001, 0.1)
    return {"checkpoint": checkpoint, "adjoint_field": adjoint_field, "accel_table": accel_table, "design": design, "design_mask": design_mask, "first_moment": first_moment, "second_moment": second_moment}


VELOCITIES = [(0, 0, 0), (1, 0, 0), (-1, 0, 0), (0, 1, 0), (0, -1, 0), (0, 0, 1), (0, 0, -1), (1, 1, 0), (-1, -1, 0), (1, -1, 0), (-1, 1, 0), (1, 0, 1), (-1, 0, -1), (1, 0, -1), (-1, 0, 1), (0, 1, 1), (0, -1, -1), (0, 1, -1), (0, -1, 1)]
OPPOSITE = [0, 2, 1, 4, 3, 6, 5, 8, 7, 10, 9, 12, 11, 14, 13, 16, 15, 18, 17]
WEIGHTS = np.array([1.0 / 3.0] + [1.0 / 18.0] * 6 + [1.0 / 36.0] * 12, np.float32)
VEL_TABLE = np.array(VELOCITIES, np.float32)
RELAX_RATE = 0.9
SOLID_MAX = 0.5
FACE_WEIGHT = 0.5
ACCEL_SCALE = 400.0
BETA_ONE = 0.9
BETA_TWO = 0.999
LEARN_RATE = 0.2
ADAM_EPS = 1e-08
BIAS_ONE = 1.0 - 0.9 ** 10
BIAS_TWO = 1.0 - 0.999 ** 10

def collide(populations, solid, accel):
    density = lax.optimization_barrier(jnp.sum(populations, axis=0))
    velocity = [lax.optimization_barrier(jnp.sum(populations * VEL_TABLE[:, axis_id][:, None, None, None], axis=0)) / density for axis_id in range(3)]
    speed_sq = velocity[0] * velocity[0] + velocity[1] * velocity[1] + velocity[2] * velocity[2]
    project = sum((VEL_TABLE[:, axis_id][:, None, None, None] * velocity[axis_id][None] for axis_id in range(3)))
    forcing = sum((VEL_TABLE[:, axis_id][:, None, None, None] * accel[axis_id] for axis_id in range(3)))
    weight = WEIGHTS[:, None, None, None]
    equil = weight * density * (1.0 + 3.0 * project + 4.5 * project * project - 1.5 * speed_sq)
    post = populations + RELAX_RATE * (equil - populations) + 3.0 * weight * density * forcing
    flipped = post[jnp.array(OPPOSITE)]
    return (1.0 - solid) * post + solid * flipped

def stream(field):
    return jnp.stack([jnp.roll(field[vel_id], VELOCITIES[vel_id], axis=(0, 1, 2)) for vel_id in range(Q)])

def advance(populations, solid, accel):
    return stream(collide(populations, solid, accel))

def block_filter(grid):
    beside_all = jnp.zeros_like(grid)
    for axis_id in range(3):
        beside_all = beside_all + jnp.roll(grid, 1, axis_id) + jnp.roll(grid, -1, axis_id)
    return (grid + FACE_WEIGHT * beside_all) / (1.0 + 6.0 * FACE_WEIGHT)

def reference(checkpoint, adjoint_field, accel_table, design, design_mask, first_moment, second_moment):
    mask_float = design_mask.astype(jnp.float32)
    filtered = block_filter(design * mask_float)
    solid = SOLID_MAX * jnp.broadcast_to(filtered[:, None, :, None, :, None], (NBX, BLOCK, NBY, BLOCK, NBZ, BLOCK)).reshape(NX, NY, NZ)

    def one_case(inputs):
        stored, adjoint, table = inputs
        accel = table.astype(jnp.float32) / ACCEL_SCALE
        states = [stored.astype(jnp.float32)]
        for turn in range(STEPS - 1):
            states.append(advance(states[-1], solid, accel[turn]))
        cotangent = adjoint
        sensitivity = jnp.zeros((NX, NY, NZ), jnp.float32)
        for turn in reversed(range(STEPS)):
            acc_now = accel[turn]
            _, pull = jax.vjp(lambda pops, cells: advance(pops, cells, acc_now), states[turn], solid)
            cotangent, dsolid = pull(cotangent)
            sensitivity = sensitivity + dsolid
        blocks = sensitivity.reshape(NBX, BLOCK, NBY, BLOCK, NBZ, BLOCK).sum(axis=(1, 3, 5))
        return (cotangent, blocks)
    adjoint_start, blocks = lax.map(one_case, (checkpoint, adjoint_field, accel_table))
    block_sens = SOLID_MAX * lax.optimization_barrier(jnp.sum(blocks, axis=0))
    gradient = mask_float * block_filter(block_sens)
    first_new = BETA_ONE * first_moment + (1.0 - BETA_ONE) * gradient
    second_new = BETA_TWO * second_moment + (1.0 - BETA_TWO) * gradient * gradient
    stepped = design - LEARN_RATE * (first_new / BIAS_ONE) / (jnp.sqrt(second_new / BIAS_TWO) + ADAM_EPS)
    design_new = jnp.clip(stepped, 0.0, 1.0)
    return (adjoint_start, design_new, first_new, second_new)
```

```python
import functools

import jax
import jax.numpy as jnp
import numpy as np
from jax import lax
from jax.experimental import pallas as pl
from jax.experimental.pallas import tpu as pltpu
from jax.sharding import PartitionSpec as P

Q = 19
BLOCK = 8
VELOCITIES = [
    (0, 0, 0),
    (1, 0, 0),
    (-1, 0, 0),
    (0, 1, 0),
    (0, -1, 0),
    (0, 0, 1),
    (0, 0, -1),
    (1, 1, 0),
    (-1, -1, 0),
    (1, -1, 0),
    (-1, 1, 0),
    (1, 0, 1),
    (-1, 0, -1),
    (1, 0, -1),
    (-1, 0, 1),
    (0, 1, 1),
    (0, -1, -1),
    (0, 1, -1),
    (0, -1, 1),
]
W_REST, W_AXIS, W_DIAG = 1.0 / 3.0, 1.0 / 18.0, 1.0 / 36.0
RELAX_RATE = 0.9
SOLID_MAX = 0.5
FACE_WEIGHT = 0.5
ACCEL_SCALE = 400.0
BETA_ONE = 0.9
BETA_TWO = 0.999
LEARN_RATE = 0.2
ADAM_EPS = 1e-08
BIAS_ONE = 1.0 - 0.9**10
BIAS_TWO = 1.0 - 0.999**10

PAIRS = tuple(range(1, Q, 2))
Q_ZERO = [q for q in range(Q) if VELOCITIES[q][0] == 0]
Q_PLUS = [q for q in range(Q) if VELOCITIES[q][0] == 1]
Q_MINUS = [q for q in range(Q) if VELOCITIES[q][0] == -1]
N_NEAR = len(Q_ZERO) + len(Q_MINUS)
ROW_FAR = Q
ROW_ADJ = 2 * Q
ROW_ADJ_FAR = ROW_ADJ + N_NEAR
ROW_DESIGN = ROW_ADJ_FAR + len(Q_MINUS)
ROWS = ROW_DESIGN + 1
RUN = 16
GROUP = 4
OFFSET = 2


def shift_yz(value, vel_id, direction):
    _, shift_y, shift_z = VELOCITIES[vel_id]
    if shift_y:
        value = pltpu.roll(value, (direction * shift_y) % 8, 0)
    if shift_z:
        value = pltpu.roll(value, (direction * shift_z) % 128, 1)
    return value


def along(vector, vel_id):
    total = None
    for part, sign in zip(vector, VELOCITIES[vel_id]):
        if sign == 0:
            continue
        if total is None:
            total = part if sign > 0 else -part
        else:
            total = total + part if sign > 0 else total - part
    return total


def weight(pair):
    return W_AXIS if pair < 7 else W_DIAG


def moments(f):
    plus = {p: f[p] + f[p + 1] for p in PAIRS}
    minus = {p: f[p] - f[p + 1] for p in PAIRS}
    density = f[0]
    for p in PAIRS:
        density = density + plus[p]
    momentum = []
    for axis in range(3):
        total = None
        for p in PAIRS:
            sign = VELOCITIES[p][axis]
            if sign == 0:
                continue
            if total is None:
                total = minus[p]
            else:
                total = total + minus[p] if sign > 0 else total - minus[p]
        momentum.append(total)
    return density, momentum, plus, minus


def odd_parts(density, momentum, minus, accel):
    flow = [3.0 * RELAX_RATE * m + (3.0 * a) * density for m, a in zip(momentum, accel)]
    return {
        p: (1.0 - RELAX_RATE) * minus[p] + (2.0 * weight(p)) * along(flow, p) for p in PAIRS
    }


def collide(f, solid, accel):
    density, momentum, plus, minus = moments(f)
    odd = odd_parts(density, momentum, minus, accel)
    inverse = 1.0 / density
    velocity = [m * inverse for m in momentum]
    speed_sq = sum(m * u for m, u in zip(momentum, velocity))
    base = RELAX_RATE * (density - 1.5 * speed_sq)
    gray = {0: (1.0 - RELAX_RATE) * f[0] + W_REST * base}
    bent = 0.5 - solid
    for p in PAIRS:
        project = along(velocity, p)
        even = 0.5 * (1.0 - RELAX_RATE) * plus[p] + weight(p) * (
            base + (4.5 * RELAX_RATE) * density * (project * project)
        )
        turned = bent * odd[p]
        gray[p] = even + turned
        gray[p + 1] = even - turned
    return gray, odd


def collide_adjoint(f_moments, g, solid, accel):
    density, momentum = f_moments
    inverse = 1.0 / density
    velocity = [m * inverse for m in momentum]
    plus = {p: g[p] + g[p + 1] for p in PAIRS}
    fluid = 1.0 - 2.0 * solid
    minus = {p: fluid * (g[p] - g[p + 1]) for p in PAIRS}
    axis_sum = plus[1] + plus[3] + plus[5]
    diag_xy, diag_xz, diag_yz = plus[7] + plus[9], plus[11] + plus[13], plus[15] + plus[17]
    level = W_REST * g[0] + W_AXIS * axis_sum + W_DIAG * (diag_xy + diag_xz + diag_yz)
    second = {
        (0, 0): W_AXIS * plus[1] + W_DIAG * (diag_xy + diag_xz),
        (1, 1): W_AXIS * plus[3] + W_DIAG * (diag_xy + diag_yz),
        (2, 2): W_AXIS * plus[5] + W_DIAG * (diag_xz + diag_yz),
        (0, 1): W_DIAG * (plus[7] - plus[9]),
        (0, 2): W_DIAG * (plus[11] - plus[13]),
        (1, 2): W_DIAG * (plus[15] - plus[17]),
    }
    first = [
        W_AXIS * minus[1] + W_DIAG * (minus[7] + minus[9] + minus[11] + minus[13]),
        W_AXIS * minus[3] + W_DIAG * (minus[7] - minus[9] + minus[15] + minus[17]),
        W_AXIS * minus[5] + W_DIAG * (minus[11] - minus[13] + minus[15] - minus[17]),
    ]
    bent = [
        sum(second[(min(i, j), max(i, j))] * velocity[j] for j in range(3)) for i in range(3)
    ]
    pull = [
        RELAX_RATE * (3.0 * first[i] + 9.0 * bent[i] - (3.0 * level) * velocity[i])
        for i in range(3)
    ]
    speed_sq = sum(u * u for u in velocity)
    rest = RELAX_RATE * (
        level * (1.0 + 1.5 * speed_sq) - 4.5 * sum(b * u for b, u in zip(bent, velocity))
    )
    rest = rest + 3.0 * sum(a * b for a, b in zip(accel, first))
    out = {0: (1.0 - RELAX_RATE) * g[0] + rest}
    for p in PAIRS:
        even = 0.5 * (1.0 - RELAX_RATE) * plus[p] + rest
        odd = 0.5 * (1.0 - RELAX_RATE) * minus[p] + along(pull, p)
        out[p] = even + odd
        out[p + 1] = even - odd
    return out


def sens_terms(g, odd):
    return sum((g[p + 1] - g[p]) * odd[p] for p in PAIRS)


def lanes():
    return lax.broadcasted_iota(jnp.int32, (8, 128), 1)


def read_accel(accel_ref, turn):
    return [accel_ref[turn, axis].astype(jnp.float32) * (1.0 / ACCEL_SCALE) for axis in range(3)]


def pack_kernel(parity_ref, f_ref, adj_ref, design_ref, mask_ref, to_a, to_b, blocks_ref, row):
    row[...] = jnp.zeros_like(row)
    row[0:1, 0:16] = design_ref[...] * mask_ref[...].astype(jnp.float32)
    spread = jnp.take_along_axis(row[...], lanes() // BLOCK, axis=1)
    spread = jnp.broadcast_to(spread[0:1], (8, 128))
    blocks_ref[...] = spread
    to_a[ROW_DESIGN] = spread
    to_b[ROW_DESIGN] = spread

    def fill(out, right):
        near, far = (7, 6) if right else (0, 1)
        for q in range(Q):
            two = f_ref[q, 48:64, :] if right else f_ref[q, 0:16, :]
            two = two.astype(jnp.float32)
            low, high = two[0:8], two[8:16]
            out[q] = high if right else low
            out[ROW_FAR + q] = low if right else high
        moving = Q_MINUS if right else Q_PLUS
        for i, q in enumerate(Q_ZERO + moving):
            out[ROW_ADJ + i] = adj_ref[q, near]
        for i, q in enumerate(moving):
            out[ROW_ADJ_FAR + i] = adj_ref[q, far]

    @pl.when(parity_ref[0] == 0)
    def _():
        fill(to_b, False)
        fill(to_a, True)

    @pl.when(parity_ref[0] == 1)
    def _():
        fill(to_b, True)
        fill(to_a, False)


def smooth(beside, grid):
    around = beside + 2.0 * grid + pltpu.roll(grid, 8, 1) + pltpu.roll(grid, 120, 1)
    return (grid + FACE_WEIGHT * around) * (1.0 / (1.0 + 6.0 * FACE_WEIGHT))


def sens_kernel(
    parity_ref,
    accel_ref,
    f_ref,
    adj_ref,
    from_a,
    from_b,
    blocks_ref,
    low_ref,
    high_ref,
    g_out,
    f_out,
    solid_out,
    sum_out,
    turned_out,
    adj_ext,
    f_next,
    odd_ext,
    solid_ext,
):
    even = parity_ref[0] == 0

    def left(row):
        return jnp.where(even, from_b[row], from_a[row])

    def right(row):
        return jnp.where(even, from_a[row], from_b[row])

    own = blocks_ref[...]
    before, after = left(ROW_DESIGN), right(ROW_DESIGN)
    solid_own = SOLID_MAX * smooth(before + after, own)
    solid_before = SOLID_MAX * smooth(low_ref[...] + own, before)
    solid_after = SOLID_MAX * smooth(own + high_ref[...], after)
    for e in range(12):
        solid_ext[e] = solid_before if e < 2 else solid_own if e < 10 else solid_after
    solid_out[...] = solid_own

    for q in range(Q):
        f_out[q, 0] = left(ROW_FAR + q)
        f_out[q, 1] = left(q)
        f_out[q, 10] = right(q)
        f_out[q, 11] = right(ROW_FAR + q)
    for i, q in enumerate(Q_ZERO + Q_MINUS):
        adj_ext[q, 1] = left(ROW_ADJ + i)
    for i, q in enumerate(Q_ZERO + Q_PLUS):
        adj_ext[q, 10] = right(ROW_ADJ + i)
    for i, q in enumerate(Q_MINUS):
        adj_ext[q, 0] = left(ROW_ADJ_FAR + i)
    for i, q in enumerate(Q_PLUS):
        adj_ext[q, 11] = right(ROW_ADJ_FAR + i)
    for q in range(Q):
        for k in range(4):
            two = f_ref[q, 16 * k : 16 * k + 16, :].astype(jnp.float32)
            f_out[q, 2 + 2 * k] = two[0:8]
            f_out[q, 3 + 2 * k] = two[8:16]
        for x in range(8):
            adj_ext[q, 2 + x] = adj_ref[q, x]

    accel_first = read_accel(accel_ref, 0)
    accel_second = read_accel(accel_ref, 1)

    def forward(e, _):
        f = [f_out[q, e] for q in range(Q)]
        gray, odd = collide(f, solid_ext[e], accel_first)
        for q in range(Q):
            f_next[q, e + 1 + VELOCITIES[q][0]] = shift_yz(gray[q], q, 1)
        for i, p in enumerate(PAIRS):
            odd_ext[i, e] = odd[p]
        return 0

    lax.fori_loop(0, 12, forward, 0)

    def backward(e, total):
        f = [f_next[q, e + 1] for q in range(Q)]
        g = [shift_yz(adj_ext[q, e + VELOCITIES[q][0]], q, -1) for q in range(Q)]
        density, momentum, _, minus = moments(f)
        odd = odd_parts(density, momentum, minus, accel_second)
        inside = jnp.logical_and(e >= 2, e < 10)
        total = total + jnp.where(inside, sens_terms(g, odd), 0.0)
        adjoint = collide_adjoint((density, momentum), g, solid_ext[e], accel_second)
        for q in range(Q):
            g_out[q, e - VELOCITIES[q][0]] = shift_yz(adjoint[q], q, -1)
        return total

    total = lax.fori_loop(1, 11, backward, jnp.zeros((8, 128), jnp.float32))

    def early(e, total):
        g = [g_out[q, e] for q in range(Q)]
        odd = {p: odd_ext[i, e] for i, p in enumerate(PAIRS)}
        return total + sens_terms(g, odd)

    total = lax.fori_loop(2, 10, early, total)
    total = jnp.sum(total, axis=0, keepdims=True)
    total = jnp.broadcast_to(total, (8, 128))
    for step in (1, 2, 4):
        total = total + pltpu.roll(total, 128 - step, 1)
    total = jnp.where(lanes() % BLOCK == 0, total, 0.0)
    sum_out[...] = total[0:1]
    turned_out[...] = pltpu.roll(total, 1, 1)[0:1]


def start_kernel(accel_ref, g_ref, f_ref, solid_ref, out_ref):
    accel = read_accel(accel_ref, 0)
    solid = solid_ref[...]

    def layer(x, _):
        f = [f_ref[q, x + 2] for q in range(Q)]
        g = [g_ref[q, x + 2] for q in range(Q)]
        density, momentum, _, _ = moments(f)
        adjoint = collide_adjoint((density, momentum), g, solid, accel)
        for q in range(Q):
            out_ref[q, x] = adjoint[q]
        return 0

    lax.fori_loop(0, 8, layer, 0)


def update_kernel(
    cases,
    place_ref,
    sums_ref,
    design_ref,
    mask_ref,
    first_ref,
    second_ref,
    design_out,
    first_out,
    second_out,
):
    place = place_ref[0]
    totals = []
    for tile in range(GROUP):
        total = sums_ref[tile * cases]
        for case in range(1, cases):
            total = total + sums_ref[tile * cases + case]
        totals.append(jnp.broadcast_to(total, (8, 128)))
    ahead = pltpu.roll(totals[0], 127, 1)
    behind = pltpu.roll(totals[-1], 127, 1)
    line = [ahead] + totals + [behind]

    def pick(shift):
        value = line[shift]
        for k in range(1, GROUP):
            value = jnp.where(place == k, line[k + shift], value)
        return value

    gradient = SOLID_MAX * smooth(pick(0) + pick(2), pick(1))
    spots = jnp.minimum(lanes() * BLOCK, 127)
    gradient = jnp.take_along_axis(gradient, spots, axis=1)[0:1, 0:16]
    gradient = mask_ref[...].astype(jnp.float32) * gradient
    first = BETA_ONE * first_ref[...] + (1.0 - BETA_ONE) * gradient
    second = BETA_TWO * second_ref[...] + (1.0 - BETA_TWO) * gradient * gradient
    stepped = design_ref[...] - LEARN_RATE * (first * (1.0 / BIAS_ONE)) / (
        jnp.sqrt(second * (1.0 / BIAS_TWO)) + ADAM_EPS
    )
    design_out[...] = jnp.clip(stepped, 0.0, 1.0)
    first_out[...] = first
    second_out[...] = second


def tables(tiles, cases):
    run = RUN if tiles % RUN == 0 else tiles

    def device(tile, case):
        return (tile % tiles) * cases + case

    def near(tile, step, case):
        target = tile + step
        crossed = (target // run) != (tile // run)
        return device(target, case ^ 1 if crossed else case)

    chip, beyond, up, down, edge = [], [], [], [], []
    for tile in range(tiles):
        step = 1 if tile % 2 else -1
        for case in range(cases):
            here = device(tile, case)
            chip.append((here, device(tile ^ 1, case)))
            beyond.append((here, device(tile + step, case)))
            up.append((here, near(tile, 2, case)))
            down.append((here, near(tile, -2, case)))
            place = (tile - OFFSET) % GROUP
            if place == 0:
                edge.append((here, device(tile - 1, case)))
            if place == GROUP - 1:
                edge.append((here, device(tile + 1, case)))
    groups = [
        [device(OFFSET + g * GROUP + k, case) for k in range(GROUP) for case in range(cases)]
        for g in range(tiles // GROUP)
    ]
    return chip, beyond, up, down, edge, groups


VMEM_SPEC = pl.BlockSpec(memory_space=pltpu.VMEM)
SMEM_SPEC = pl.BlockSpec(memory_space=pltpu.SMEM)
F32 = jnp.float32


def body(
    tiles,
    cases,
    checkpoint,
    adjoint_field,
    accel_table,
    design,
    design_mask,
    first_moment,
    second_moment,
):
    axes = ("tile", "case")
    chip, beyond, up, down, edge, groups = tables(tiles, cases)
    tile = lax.axis_index("tile")
    parity = jnp.reshape(tile % 2, (1,)).astype(jnp.int32)
    place = jnp.reshape((tile - OFFSET) % GROUP, (1,)).astype(jnp.int32)
    f_zero = checkpoint.reshape(Q, 64, 128)
    adjoint = adjoint_field[0]
    accel = accel_table[0]
    flat = [a.reshape(1, 16) for a in (design, design_mask, first_moment, second_moment)]
    params = pltpu.CompilerParams(vmem_limit_bytes=32 * 1024 * 1024)

    face = jax.ShapeDtypeStruct((ROWS, 8, 128), F32)
    layer = jax.ShapeDtypeStruct((8, 128), F32)
    to_a, to_b, blocks = pl.pallas_call(
        pack_kernel,
        out_shape=(face, face, layer),
        in_specs=[SMEM_SPEC] + [VMEM_SPEC] * 4,
        out_specs=[VMEM_SPEC] * 3,
        scratch_shapes=[pltpu.VMEM((8, 128), F32)],
        compiler_params=params,
        name="pack_faces",
    )(parity, f_zero, adjoint, flat[0], flat[1])

    from_b = lax.ppermute(to_b, axes, beyond)
    from_a = lax.ppermute(to_a, axes, chip)
    low = lax.ppermute(blocks, axes, up)
    high = lax.ppermute(blocks, axes, down)

    ext = jax.ShapeDtypeStruct((Q, 12, 8, 128), F32)
    row = jax.ShapeDtypeStruct((1, 128), F32)
    g_one, f_ext, solid, sums, turned = pl.pallas_call(
        sens_kernel,
        out_shape=(ext, ext, layer, row, row),
        in_specs=[SMEM_SPEC] * 2 + [VMEM_SPEC] * 7,
        out_specs=[VMEM_SPEC] * 5,
        scratch_shapes=[
            pltpu.VMEM((Q, 12, 8, 128), F32),
            pltpu.VMEM((Q, 14, 8, 128), F32),
            pltpu.VMEM((len(PAIRS), 12, 8, 128), F32),
            pltpu.VMEM((12, 8, 128), F32),
        ],
        compiler_params=params,
        name="sensitivity",
    )(parity, accel, f_zero, adjoint, from_a, from_b, blocks, low, high)

    outside = lax.ppermute(turned, axes, edge)
    payload = jnp.broadcast_to((sums + outside)[None], (GROUP * cases, 1, 128))
    shared = lax.all_to_all(payload, axes, 0, 0, axis_index_groups=groups, tiled=True)

    start = pl.pallas_call(
        start_kernel,
        out_shape=jax.ShapeDtypeStruct((Q, 8, 8, 128), F32),
        in_specs=[SMEM_SPEC] + [VMEM_SPEC] * 3,
        out_specs=VMEM_SPEC,
        compiler_params=params,
        name="adjoint_start",
    )(accel, g_one, f_ext, solid)

    small = jax.ShapeDtypeStruct((1, 16), F32)
    updated = pl.pallas_call(
        functools.partial(update_kernel, cases),
        out_shape=(small, small, small),
        in_specs=[SMEM_SPEC] + [VMEM_SPEC] * 5,
        out_specs=[VMEM_SPEC] * 3,
        compiler_params=params,
        name="update",
    )(place, shared, *flat)
    return (start[None],) + tuple(u.reshape(1, 1, 16) for u in updated)


def solution(mesh):
    placed = (
        P("case", None, "tile", None, None),
        P("case", None, "tile", None, None),
        P("case", None, None),
        P("tile", None, None),
        P("tile", None, None),
        P("tile", None, None),
        P("tile", None, None),
    )
    return jax.shard_map(
        functools.partial(body, mesh.shape["tile"], mesh.shape["case"]),
        mesh=mesh,
        in_specs=placed,
        out_specs=(
            P("case", None, "tile", None, None),
            P("tile", None, None),
            P("tile", None, None),
            P("tile", None, None),
        ),
        check_vma=False,
    )
```

```python
import functools

import jax
import jax.numpy as jnp
import numpy as np
from jax import lax
from jax.experimental import pallas as pl
from jax.experimental.pallas import tpu as pltpu
from jax.sharding import PartitionSpec as P

Q = 19
BLOCK = 8
VELOCITIES = [
    (0, 0, 0),
    (1, 0, 0),
    (-1, 0, 0),
    (0, 1, 0),
    (0, -1, 0),
    (0, 0, 1),
    (0, 0, -1),
    (1, 1, 0),
    (-1, -1, 0),
    (1, -1, 0),
    (-1, 1, 0),
    (1, 0, 1),
    (-1, 0, -1),
    (1, 0, -1),
    (-1, 0, 1),
    (0, 1, 1),
    (0, -1, -1),
    (0, 1, -1),
    (0, -1, 1),
]
W_REST, W_AXIS, W_DIAG = 1.0 / 3.0, 1.0 / 18.0, 1.0 / 36.0
RELAX_RATE = 0.9
SOLID_MAX = 0.5
FACE_WEIGHT = 0.5
ACCEL_SCALE = 400.0
BETA_ONE = 0.9
BETA_TWO = 0.999
LEARN_RATE = 0.2
ADAM_EPS = 1e-08
BIAS_ONE = 1.0 - 0.9**10
BIAS_TWO = 1.0 - 0.999**10

PAIRS = tuple(range(1, Q, 2))
Q_ZERO = [q for q in range(Q) if VELOCITIES[q][0] == 0]
Q_PLUS = [q for q in range(Q) if VELOCITIES[q][0] == 1]
Q_MINUS = [q for q in range(Q) if VELOCITIES[q][0] == -1]
ROW_FAR = len(Q_ZERO) + len(Q_PLUS)
ROW_ADJ = ROW_FAR + len(Q_PLUS)
ROW_ADJ_FAR = ROW_ADJ + len(Q_ZERO) + len(Q_PLUS)
ROW_SOLID = ROW_ADJ_FAR + len(Q_PLUS)
ROWS = ROW_SOLID + 1
RAW_FAR = Q
RAW_ADJ = RAW_FAR + 2 * len(Q_PLUS)
RAW_ADJ_FAR = RAW_ADJ + len(Q_ZERO) + len(Q_PLUS)
RAW_ROWS = RAW_ADJ_FAR + len(Q_PLUS)
RUN = 16
GROUP = 8
OFFSET = 5


def shift_yz(value, vel_id, direction):
    _, shift_y, shift_z = VELOCITIES[vel_id]
    if shift_y:
        value = pltpu.roll(value, (direction * shift_y) % 8, 0)
    if shift_z:
        value = pltpu.roll(value, (direction * shift_z) % 128, 1)
    return value


def along(vector, vel_id):
    total = None
    for part, sign in zip(vector, VELOCITIES[vel_id]):
        if sign == 0:
            continue
        if total is None:
            total = part if sign > 0 else -part
        else:
            total = total + part if sign > 0 else total - part
    return total


def weight(pair):
    return W_AXIS if pair < 7 else W_DIAG


def moments(f):
    plus = {p: f[p] + f[p + 1] for p in PAIRS}
    minus = {p: f[p] - f[p + 1] for p in PAIRS}
    density = f[0]
    for p in PAIRS:
        density = density + plus[p]
    momentum = []
    for axis in range(3):
        total = None
        for p in PAIRS:
            sign = VELOCITIES[p][axis]
            if sign == 0:
                continue
            if total is None:
                total = minus[p]
            else:
                total = total + minus[p] if sign > 0 else total - minus[p]
        momentum.append(total)
    return density, momentum, plus, minus


def odd_parts(density, momentum, minus, accel):
    flow = [3.0 * RELAX_RATE * m + (3.0 * a) * density for m, a in zip(momentum, accel)]
    return {
        p: (1.0 - RELAX_RATE) * minus[p] + (2.0 * weight(p)) * along(flow, p) for p in PAIRS
    }


def collide(f, solid, accel):
    density, momentum, plus, minus = moments(f)
    odd = odd_parts(density, momentum, minus, accel)
    inverse = 1.0 / density
    velocity = [m * inverse for m in momentum]
    speed_sq = sum(m * u for m, u in zip(momentum, velocity))
    base = RELAX_RATE * (density - 1.5 * speed_sq)
    gray = {0: (1.0 - RELAX_RATE) * f[0] + W_REST * base}
    bent = 0.5 - solid
    for p in PAIRS:
        project = along(velocity, p)
        even = 0.5 * (1.0 - RELAX_RATE) * plus[p] + weight(p) * (
            base + (4.5 * RELAX_RATE) * density * (project * project)
        )
        turned = bent * odd[p]
        gray[p] = even + turned
        gray[p + 1] = even - turned
    return gray, odd


def collide_adjoint(f_moments, g, solid, accel):
    density, momentum = f_moments
    inverse = 1.0 / density
    velocity = [m * inverse for m in momentum]
    plus = {p: g[p] + g[p + 1] for p in PAIRS}
    fluid = 1.0 - 2.0 * solid
    minus = {p: fluid * (g[p] - g[p + 1]) for p in PAIRS}
    axis_sum = plus[1] + plus[3] + plus[5]
    diag_xy, diag_xz, diag_yz = plus[7] + plus[9], plus[11] + plus[13], plus[15] + plus[17]
    level = W_REST * g[0] + W_AXIS * axis_sum + W_DIAG * (diag_xy + diag_xz + diag_yz)
    second = {
        (0, 0): W_AXIS * plus[1] + W_DIAG * (diag_xy + diag_xz),
        (1, 1): W_AXIS * plus[3] + W_DIAG * (diag_xy + diag_yz),
        (2, 2): W_AXIS * plus[5] + W_DIAG * (diag_xz + diag_yz),
        (0, 1): W_DIAG * (plus[7] - plus[9]),
        (0, 2): W_DIAG * (plus[11] - plus[13]),
        (1, 2): W_DIAG * (plus[15] - plus[17]),
    }
    first = [
        W_AXIS * minus[1] + W_DIAG * (minus[7] + minus[9] + minus[11] + minus[13]),
        W_AXIS * minus[3] + W_DIAG * (minus[7] - minus[9] + minus[15] + minus[17]),
        W_AXIS * minus[5] + W_DIAG * (minus[11] - minus[13] + minus[15] - minus[17]),
    ]
    bent = [
        sum(second[(min(i, j), max(i, j))] * velocity[j] for j in range(3)) for i in range(3)
    ]
    pull = [
        RELAX_RATE * (3.0 * first[i] + 9.0 * bent[i] - (3.0 * level) * velocity[i])
        for i in range(3)
    ]
    speed_sq = sum(u * u for u in velocity)
    rest = RELAX_RATE * (
        level * (1.0 + 1.5 * speed_sq) - 4.5 * sum(b * u for b, u in zip(bent, velocity))
    )
    rest = rest + 3.0 * sum(a * b for a, b in zip(accel, first))
    out = {0: (1.0 - RELAX_RATE) * g[0] + rest}
    for p in PAIRS:
        even = 0.5 * (1.0 - RELAX_RATE) * plus[p] + rest
        odd = 0.5 * (1.0 - RELAX_RATE) * minus[p] + along(pull, p)
        out[p] = even + odd
        out[p + 1] = even - odd
    return out


def sens_terms(g, odd):
    return sum((g[p + 1] - g[p]) * odd[p] for p in PAIRS)


def lanes():
    return lax.broadcasted_iota(jnp.int32, (8, 128), 1)


def read_accel(accel_ref, turn):
    return [accel_ref[turn, axis] for axis in range(3)]


def is_even():
    return lax.axis_index("tile") & 1 == 0


def spread(row, blocks):
    row[...] = jnp.zeros_like(row)
    row[0:1, 0:16] = blocks
    wide = jnp.take_along_axis(row[...], lanes() // BLOCK, axis=1)
    return jnp.broadcast_to(wide[0:1], (8, 128))


def smooth(beside, grid):
    around = beside + 2.0 * grid + pltpu.roll(grid, 8, 1) + pltpu.roll(grid, 120, 1)
    return (grid + FACE_WEIGHT * around) * (1.0 / (1.0 + 6.0 * FACE_WEIGHT))


def read_layer(f_ref, q, x):
    two = f_ref[q, 16 * (x // 2) : 16 * (x // 2) + 16, :].astype(jnp.float32)
    return two[8:16] if x % 2 else two[0:8]


def pack(f_ref, adj_ref, out, high, solid, accel):
    near, far = (7, 6) if high else (0, 1)
    onward, back = (Q_PLUS, Q_MINUS) if high else (Q_MINUS, Q_PLUS)
    gray, _ = collide([read_layer(f_ref, q, near) for q in range(Q)], solid, accel)
    for i, q in enumerate(Q_ZERO + onward):
        out[i] = shift_yz(gray[q], q, 1)
    gray, _ = collide([read_layer(f_ref, q, far) for q in range(Q)], solid, accel)
    for i, q in enumerate(onward):
        out[ROW_FAR + i] = shift_yz(gray[q], q, 1)
    for i, q in enumerate(Q_ZERO + back):
        out[ROW_ADJ + i] = adj_ref[q, near]
    for i, q in enumerate(back):
        out[ROW_ADJ_FAR + i] = adj_ref[q, far]
    out[ROW_SOLID] = solid


def load_kernel(
    design_hbm,
    mask_hbm,
    accel_hbm,
    f_hbm,
    adj_hbm,
    blocks_out,
    accel_out,
    f_out,
    adj_out,
    design,
    mask,
    table,
    sems,
):
    copies = [
        pltpu.make_async_copy(source, target, sems.at[i])
        for i, (source, target) in enumerate(
            (
                (design_hbm, design),
                (mask_hbm, mask),
                (accel_hbm, table),
                (f_hbm, f_out),
                (adj_hbm, adj_out),
            )
        )
    ]
    for copy in copies:
        copy.start()
    for copy in copies[:3]:
        copy.wait()
    blocks_out[...] = design[...] * mask[...].astype(jnp.float32)
    for turn in range(2):
        for axis in range(3):
            value = table[turn, axis].astype(jnp.float32) * (1.0 / ACCEL_SCALE)
            accel_out[turn, axis] = jnp.full((8, 128), value, jnp.float32)
    for copy in copies[3:]:
        copy.wait()


def pack_raw(f_ref, adj_ref, out, high, accel):
    near, far = (7, 6) if high else (0, 1)
    back = Q_MINUS if high else Q_PLUS
    post, _ = collide([read_layer(f_ref, q, near) for q in range(Q)], 0.0, accel)
    for q in range(Q):
        out[q] = post[q]
    post, _ = collide([read_layer(f_ref, q, far) for q in range(Q)], 0.0, accel)
    for i, p in enumerate(Q_PLUS):
        out[RAW_FAR + 2 * i] = post[p]
        out[RAW_FAR + 2 * i + 1] = post[p + 1]
    for i, q in enumerate(Q_ZERO + back):
        out[RAW_ADJ + i] = adj_ref[q, near]
    for i, q in enumerate(back):
        out[RAW_ADJ_FAR + i] = adj_ref[q, far]


def duo_kernel(own_ref, mate_ref, duo_out):
    duo_out[0:1] = own_ref[...]
    duo_out[1:2] = mate_ref[...]


def raw_kernel(f_ref, adj_ref, accel_ref, duo_ref, to_b):
    del duo_ref
    accel = read_accel(accel_ref, 0)
    even = is_even()
    pl.when(even)(lambda: pack_raw(f_ref, adj_ref, to_b, False, accel))
    pl.when(jnp.logical_not(even))(lambda: pack_raw(f_ref, adj_ref, to_b, True, accel))


def pack_kernel(
    f_ref, adj_ref, accel_ref, own_ref, mate_ref, duo_ref, to_a, solid_out, solid_beyond, row
):
    duo = duo_ref[...]
    beside, past = duo[0:1], duo[1:2]
    own = spread(row, own_ref[...])
    solid = SOLID_MAX * smooth(spread(row, mate_ref[...] + beside), own)
    solid_out[...] = solid
    solid_beyond[...] = SOLID_MAX * smooth(own + spread(row, past), spread(row, beside))
    accel = read_accel(accel_ref, 0)
    even = is_even()
    pl.when(even)(lambda: pack(f_ref, adj_ref, to_a, True, solid, accel))
    pl.when(jnp.logical_not(even))(lambda: pack(f_ref, adj_ref, to_a, False, solid, accel))


def mid_kernel(
    accel_ref,
    solid_ref,
    f_ref,
    adj_ref,
    from_a,
    g_out,
    f_next,
    odd_out,
    mom_out,
    sum_out,
    adj_ext,
    solid_ext,
):
    even = is_even()
    solid_own = solid_ref[...]
    solid_mate = from_a[ROW_SOLID]
    for e in range(12):
        solid_ext[e] = solid_own if 2 <= e < 10 else solid_mate
    accel_first = read_accel(accel_ref, 0)
    accel_second = read_accel(accel_ref, 1)
    for q in range(Q):
        for x in range(8):
            adj_ext[q, 2 + x] = adj_ref[q, x]
        for e in (2, 3, 8, 9):
            g_out[q, e] = jnp.zeros((8, 128), jnp.float32)

    def forward(k, _):
        for half in range(2):
            e = 2 * k + 2 + half
            f = [
                f_ref[q, pl.ds(pl.multiple_of(16 * k, 16), 16), :].astype(jnp.float32)[
                    8 * half : 8 * half + 8
                ]
                for q in range(Q)
            ]
            gray, odd = collide(f, solid_own, accel_first)
            density, momentum, _, _ = moments(f)
            for i, part in enumerate([density] + momentum):
                mom_out[i, e - 2] = part
            for q in range(Q):
                f_next[q, e + 1 + VELOCITIES[q][0]] = shift_yz(gray[q], q, 1)
            for i, p in enumerate(PAIRS):
                odd_out[i, e] = odd[p]
        return 0

    lax.fori_loop(0, 4, forward, 0)

    def mate_side(low):
        face, near, far = (2, 1, 0) if low else (9, 10, 11)
        inward, outward = (Q_PLUS, Q_MINUS) if low else (Q_MINUS, Q_PLUS)
        for i, q in enumerate(Q_ZERO):
            f_next[q, near + 1] = from_a[i]
        for i, q in enumerate(inward):
            f_next[q, face + 1] = from_a[len(Q_ZERO) + i]
            f_next[q, near + 1] = from_a[ROW_FAR + i]
        for i, q in enumerate(Q_ZERO + outward):
            adj_ext[q, near] = from_a[ROW_ADJ + i]
        for i, q in enumerate(outward):
            adj_ext[q, far] = from_a[ROW_ADJ_FAR + i]

    pl.when(even)(lambda: mate_side(False))
    pl.when(jnp.logical_not(even))(lambda: mate_side(True))

    def backward(e, total):
        f = [f_next[q, e + 1] for q in range(Q)]
        g = [shift_yz(adj_ext[q, e + VELOCITIES[q][0]], q, -1) for q in range(Q)]
        density, momentum, _, minus = moments(f)
        odd = odd_parts(density, momentum, minus, accel_second)
        inside = jnp.logical_and(e >= 2, e < 10)
        total = total + jnp.where(inside, sens_terms(g, odd), 0.0)
        adjoint = collide_adjoint((density, momentum), g, solid_ext[e], accel_second)
        for q in range(Q):
            g_out[q, e - VELOCITIES[q][0]] = shift_yz(adjoint[q], q, -1)
        return total

    first = jnp.where(even, 3, 1)
    total = lax.fori_loop(first, first + 8, backward, jnp.zeros((8, 128), jnp.float32))

    def early(e, total):
        g = [g_out[q, e] for q in range(Q)]
        odd = {p: odd_out[i, e] for i, p in enumerate(PAIRS)}
        return total + sens_terms(g, odd)

    sum_out[...] = lax.fori_loop(2, 10, early, total)


def edge(low, message, solid_own, solid, f_next, adj_ref, accel):
    inward, outward = (Q_PLUS, Q_MINUS) if low else (Q_MINUS, Q_PLUS)
    beside, face, layer, behind = (2, 3, 0, 1) if low else (11, 10, 7, 6)
    adj = {q: message[RAW_ADJ + i] for i, q in enumerate(Q_ZERO + outward)}

    def mixed(row, q):
        if q == 0:
            return message[row]
        opposite = row + 1 if q % 2 else row - 1
        value = message[row]
        return shift_yz(value + solid * (message[opposite] - value), q, 1)

    first = 0 if low else 1
    f = {q: mixed(RAW_FAR + 2 * i + first, q) for i, q in enumerate(inward)}
    f.update({q: mixed(q, q) for q in Q_ZERO})
    f.update({q: f_next[q, beside] for q in outward})
    g = {q: message[RAW_ADJ_FAR + i] for i, q in enumerate(outward)}
    g.update({q: adj[q] for q in Q_ZERO})
    g.update({q: adj_ref[q, layer] for q in inward})
    g = {q: shift_yz(g[q], q, -1) for q in range(Q)}
    density, momentum, _, _ = moments(f)
    adj_beside = collide_adjoint((density, momentum), g, solid, accel)

    f = {q: f_next[q, face] for q in Q_ZERO + outward}
    f.update({q: mixed(q, q) for q in inward})
    g = {q: adj[q] for q in outward}
    g.update({q: adj_ref[q, layer] for q in Q_ZERO})
    g.update({q: adj_ref[q, behind] for q in inward})
    g = {q: shift_yz(g[q], q, -1) for q in range(Q)}
    density, momentum, _, minus = moments(f)
    odd = odd_parts(density, momentum, minus, accel)
    adj_face = collide_adjoint((density, momentum), g, solid_own, accel)
    adj_beside = {q: shift_yz(adj_beside[q], q, -1) for q in outward}
    adj_face = {q: shift_yz(adj_face[q], q, -1) for q in Q_ZERO + outward}
    return adj_beside, adj_face, sens_terms(g, odd)


def turned_odd(odd, q):
    return -odd[q] if q % 2 else odd[q - 1]


def post_kernel(
    message,
    accel_ref,
    solid_ref,
    beyond_ref,
    f_next,
    adj_ref,
    g_ref,
    odd_ref,
    sum_ref,
    head_out,
    tail_out,
    sums_out,
    turned_out,
    own_sum,
):
    for q in range(Q):
        head_out[q, 0] = g_ref[q, 2]
        head_out[q, 1] = g_ref[q, 3]
        tail_out[q, 0] = g_ref[q, 8]
        tail_out[q, 1] = g_ref[q, 9]

    def side(low):
        adj_beside, adj_face, own = edge(
            low,
            message,
            solid_ref[...],
            beyond_ref[...],
            f_next,
            adj_ref,
            read_accel(accel_ref, 1),
        )
        face, behind = (2, 3) if low else (9, 8)
        out, at_face, at_behind = (head_out, 0, 1) if low else (tail_out, 1, 0)
        first = {p: odd_ref[i, face] for i, p in enumerate(PAIRS)}
        second = {p: odd_ref[i, behind] for i, p in enumerate(PAIRS)}
        for q in Q_ZERO:
            if q:
                own = own + adj_face[q] * turned_odd(first, q)
            out[q, at_face] = adj_face[q]
        for q in Q_MINUS if low else Q_PLUS:
            own = own + adj_beside[q] * turned_odd(first, q)
            own = own + adj_face[q] * turned_odd(second, q)
            out[q, at_face] = adj_beside[q]
            out[q, at_behind] = adj_face[q]
        own_sum[...] = own

    even = is_even()
    pl.when(even)(lambda: side(True))
    pl.when(jnp.logical_not(even))(lambda: side(False))
    total = jnp.sum(own_sum[...] + sum_ref[...], axis=0, keepdims=True)
    total = jnp.broadcast_to(total, (8, 128))
    for step in (1, 2, 4):
        total = total + pltpu.roll(total, 128 - step, 1)
    total = jnp.where(lanes() % BLOCK == 0, total, 0.0)
    sums_out[...] = total[0:1]
    turned_out[...] = pltpu.roll(total, 1, 1)[0:1]


def start_kernel(accel_ref, solid_ref, g_ref, mom_ref, head_ref, tail_ref, out_ref):
    accel = read_accel(accel_ref, 0)
    solid = solid_ref[...]

    def layers(low, high, source, offset):
        def step(x, _):
            g = [source[q, x + offset] for q in range(Q)]
            momentum = [mom_ref[1 + axis, x] for axis in range(3)]
            adjoint = collide_adjoint((mom_ref[0, x], momentum), g, solid, accel)
            for q in range(Q):
                out_ref[q, x] = adjoint[q]
            return 0

        lax.fori_loop(low, high, step, 0)

    layers(0, 2, head_ref, 0)
    layers(2, 6, g_ref, 2)
    layers(6, 8, tail_ref, -6)


def share_kernel(sums_ref, outside_ref, out):
    out[...] = jnp.broadcast_to((sums_ref[...] + outside_ref[...])[None], out.shape)


def update_kernel(
    cases,
    sums_ref,
    design_ref,
    mask_ref,
    first_ref,
    second_ref,
    design_out,
    first_out,
    second_out,
):
    place = (lax.axis_index("tile") - OFFSET) & (GROUP - 1)
    totals = []
    for tile in range(GROUP):
        total = sums_ref[tile * cases]
        for case in range(1, cases):
            total = total + sums_ref[tile * cases + case]
        totals.append(jnp.broadcast_to(total, (8, 128)))

    line = [pltpu.roll(totals[0], 127, 1)] + totals + [pltpu.roll(totals[-1], 127, 1)]

    def pick(shift):
        value = line[shift]
        for k in range(1, GROUP):
            value = jnp.where(place == k, line[k + shift], value)
        return value

    gradient = SOLID_MAX * smooth(pick(0) + pick(2), pick(1))
    spots = jnp.minimum(lanes() * BLOCK, 127)
    gradient = jnp.take_along_axis(gradient, spots, axis=1)[0:1, 0:16]
    gradient = mask_ref[...].astype(jnp.float32) * gradient
    first = BETA_ONE * first_ref[...] + (1.0 - BETA_ONE) * gradient
    second = BETA_TWO * second_ref[...] + (1.0 - BETA_TWO) * gradient * gradient
    stepped = design_ref[...] - LEARN_RATE * (first * (1.0 / BIAS_ONE)) / (
        jnp.sqrt(second * (1.0 / BIAS_TWO)) + ADAM_EPS
    )
    design_out[...] = jnp.clip(stepped, 0.0, 1.0)
    first_out[...] = first
    second_out[...] = second


def tables(tiles, cases):
    run = RUN if tiles % RUN == 0 else tiles

    def device(tile, case):
        return (tile % tiles) * cases + case

    def near(tile, step, case):
        target = tile + step
        crossed = (target // run) != (tile // run)
        return device(target, case ^ 1 if crossed else case)

    found = {name: [] for name in ("chip", "beyond", "beside", "ends")}
    for tile in range(tiles):
        step = 1 if tile % 2 else -1
        for case in range(cases):
            here = device(tile, case)
            found["chip"].append((here, device(tile ^ 1, case)))
            found["beyond"].append((here, device(tile + step, case)))
            found["beside"].append((here, near(tile, step, case)))
            place = (tile - OFFSET) % GROUP
            if place == 0:
                found["ends"].append((here, device(tile - 1, case)))
            if place == GROUP - 1:
                found["ends"].append((here, device(tile + 1, case)))
    groups = [
        [device(OFFSET + g * GROUP + k, case) for k in range(GROUP) for case in range(cases)]
        for g in range(tiles // GROUP)
    ]
    return found, groups


VMEM_SPEC = pl.BlockSpec(memory_space=pltpu.VMEM)
HBM_SPEC = pl.BlockSpec(memory_space=pltpu.HBM)
F32 = jnp.float32


def body(
    tiles,
    cases,
    checkpoint,
    adjoint_field,
    accel_table,
    design,
    design_mask,
    first_moment,
    second_moment,
):
    axes = ("tile", "case")
    pairs, groups = tables(tiles, cases)
    f_zero = checkpoint.reshape(Q, 64, 128)
    adjoint = adjoint_field[0]
    flat = [a.reshape(1, 16) for a in (design, design_mask, first_moment, second_moment)]
    params = pltpu.CompilerParams(vmem_limit_bytes=32 * 1024 * 1024)

    def send(value, name):
        return lax.ppermute(value, axes, pairs[name])

    def call(kernel, name, out_shape, in_specs, scratch, *args):
        many = isinstance(out_shape, tuple)
        return pl.pallas_call(
            kernel,
            out_shape=out_shape,
            in_specs=in_specs,
            out_specs=[VMEM_SPEC] * len(out_shape) if many else VMEM_SPEC,
            scratch_shapes=scratch,
            compiler_params=params,
            name=name,
        )(*args)

    def shape(*dims):
        return jax.ShapeDtypeStruct(dims, F32)

    row = pltpu.VMEM((8, 128), F32)
    blocks, accel, f_zero, adjoint = call(
        load_kernel,
        "load",
        (
            shape(1, 16),
            shape(2, 3, 8, 128),
            jax.ShapeDtypeStruct((Q, 64, 128), jnp.bfloat16),
            shape(Q, 8, 8, 128),
        ),
        [HBM_SPEC] * 5,
        [
            pltpu.VMEM((1, 16), F32),
            pltpu.VMEM((1, 16), jnp.int32),
            pltpu.SMEM((2, 3), jnp.int32),
            pltpu.SemaphoreType.DMA((5,)),
        ],
        *(
            pltpu.with_memory_space_constraint(a, pltpu.HBM)
            for a in (flat[0], flat[1], accel_table[0], f_zero, adjoint)
        ),
    )
    mate = send(blocks, "chip")
    duo = call(duo_kernel, "chip_blocks", shape(2, 16), [VMEM_SPEC] * 2, [], blocks, mate)
    duo_beside = send(duo, "beside")
    to_b = call(
        raw_kernel,
        "pack_beyond",
        shape(RAW_ROWS, 8, 128),
        [VMEM_SPEC] * 4,
        [],
        f_zero,
        adjoint,
        accel,
        duo,
    )
    from_b = send(to_b, "beyond")
    to_a, solid, solid_beyond = call(
        pack_kernel,
        "pack_chip",
        (shape(ROWS, 8, 128), shape(8, 128), shape(8, 128)),
        [VMEM_SPEC] * 6,
        [row],
        f_zero,
        adjoint,
        accel,
        blocks,
        mate,
        duo_beside,
    )
    from_a = send(to_a, "chip")
    g_one, f_next, odd, mom, sums = call(
        mid_kernel,
        "middle",
        (
            shape(Q, 12, 8, 128),
            shape(Q, 14, 8, 128),
            shape(len(PAIRS), 12, 8, 128),
            shape(4, 8, 8, 128),
            shape(8, 128),
        ),
        [VMEM_SPEC] * 5,
        [pltpu.VMEM((Q, 12, 8, 128), F32), pltpu.VMEM((12, 8, 128), F32)],
        accel,
        solid,
        f_zero,
        adjoint,
        from_a,
    )
    head, tail, sums, turned = call(
        post_kernel,
        "chip_edge",
        (shape(Q, 2, 8, 128), shape(Q, 2, 8, 128), shape(1, 128), shape(1, 128)),
        [VMEM_SPEC] * 9,
        [row],
        from_b,
        accel,
        solid,
        solid_beyond,
        f_next,
        adjoint,
        g_one,
        odd,
        sums,
    )
    outside = send(turned, "ends")
    payload = call(
        share_kernel, "share", shape(GROUP * cases, 1, 128), [VMEM_SPEC] * 2, [], sums, outside
    )
    payload, head = lax.optimization_barrier((payload, head))
    shared = lax.all_to_all(payload, axes, 0, 0, axis_index_groups=groups, tiled=True)
    start = call(
        start_kernel,
        "adjoint_start",
        shape(Q, 8, 8, 128),
        [VMEM_SPEC] * 6,
        [],
        accel,
        solid,
        g_one,
        mom,
        head,
        tail,
    )
    small = shape(1, 16)
    updated = call(
        functools.partial(update_kernel, cases),
        "update",
        (small, small, small),
        [VMEM_SPEC] * 5,
        [],
        shared,
        *flat,
    )
    return (start[None],) + tuple(u.reshape(1, 1, 16) for u in updated)


def solution(mesh):
    placed = (
        P("case", None, "tile", None, None),
        P("case", None, "tile", None, None),
        P("case", None, None),
        P("tile", None, None),
        P("tile", None, None),
        P("tile", None, None),
        P("tile", None, None),
    )
    return jax.shard_map(
        functools.partial(body, mesh.shape["tile"], mesh.shape["case"]),
        mesh=mesh,
        in_specs=placed,
        out_specs=(
            P("case", None, "tile", None, None),
            P("tile", None, None),
            P("tile", None, None),
            P("tile", None, None),
        ),
        check_vma=False,
    )
```

```python
import functools

import jax
import jax.numpy as jnp
import numpy as np
from jax import lax
from jax.experimental import pallas as pl
from jax.experimental.pallas import tpu as pltpu
from jax.sharding import PartitionSpec as P

Q = 19
BLOCK = 8
VELOCITIES = [
    (0, 0, 0),
    (1, 0, 0),
    (-1, 0, 0),
    (0, 1, 0),
    (0, -1, 0),
    (0, 0, 1),
    (0, 0, -1),
    (1, 1, 0),
    (-1, -1, 0),
    (1, -1, 0),
    (-1, 1, 0),
    (1, 0, 1),
    (-1, 0, -1),
    (1, 0, -1),
    (-1, 0, 1),
    (0, 1, 1),
    (0, -1, -1),
    (0, 1, -1),
    (0, -1, 1),
]
W_REST, W_AXIS, W_DIAG = 1.0 / 3.0, 1.0 / 18.0, 1.0 / 36.0
RELAX_RATE = 0.9
SOLID_MAX = 0.5
FACE_WEIGHT = 0.5
ACCEL_SCALE = 400.0
BETA_ONE = 0.9
BETA_TWO = 0.999
LEARN_RATE = 0.2
ADAM_EPS = 1e-08
BIAS_ONE = 1.0 - 0.9**10
BIAS_TWO = 1.0 - 0.999**10

PAIRS = tuple(range(1, Q, 2))
Q_ZERO = [q for q in range(Q) if VELOCITIES[q][0] == 0]
Q_PLUS = [q for q in range(Q) if VELOCITIES[q][0] == 1]
Q_MINUS = [q for q in range(Q) if VELOCITIES[q][0] == -1]
ROW_FAR = len(Q_ZERO) + len(Q_PLUS)
ROW_ADJ = ROW_FAR + len(Q_PLUS)
ROW_ADJ_FAR = ROW_ADJ + len(Q_ZERO) + len(Q_PLUS)
ROW_SOLID = ROW_ADJ_FAR + len(Q_PLUS)
ROWS = ROW_SOLID + 1
B_FAR = Q
B_ADJ = B_FAR + 2 * len(Q_PLUS)
B_ADJ_FAR = B_ADJ + len(Q_ZERO) + len(Q_PLUS)
B_BLOCKS = B_ADJ_FAR + len(Q_PLUS)
B_ROWS = B_BLOCKS + 1
RUN = 16
GROUP = 8
OFFSET = 5


def shift_yz(value, vel_id, direction):
    _, shift_y, shift_z = VELOCITIES[vel_id]
    if shift_y:
        value = pltpu.roll(value, (direction * shift_y) % 8, 0)
    if shift_z:
        value = pltpu.roll(value, (direction * shift_z) % 128, 1)
    return value


def along(vector, vel_id):
    total = None
    for part, sign in zip(vector, VELOCITIES[vel_id]):
        if sign == 0:
            continue
        if total is None:
            total = part if sign > 0 else -part
        else:
            total = total + part if sign > 0 else total - part
    return total


def weight(pair):
    return W_AXIS if pair < 7 else W_DIAG


def moments(f):
    plus = {p: f[p] + f[p + 1] for p in PAIRS}
    minus = {p: f[p] - f[p + 1] for p in PAIRS}
    density = f[0]
    for p in PAIRS:
        density = density + plus[p]
    momentum = []
    for axis in range(3):
        total = None
        for p in PAIRS:
            sign = VELOCITIES[p][axis]
            if sign == 0:
                continue
            if total is None:
                total = minus[p]
            else:
                total = total + minus[p] if sign > 0 else total - minus[p]
        momentum.append(total)
    return density, momentum, plus, minus


def odd_parts(density, momentum, minus, accel):
    flow = [3.0 * RELAX_RATE * m + (3.0 * a) * density for m, a in zip(momentum, accel)]
    return {
        p: (1.0 - RELAX_RATE) * minus[p] + (2.0 * weight(p)) * along(flow, p) for p in PAIRS
    }


def collide(f, solid, accel):
    density, momentum, plus, minus = moments(f)
    odd = odd_parts(density, momentum, minus, accel)
    inverse = 1.0 / density
    velocity = [m * inverse for m in momentum]
    speed_sq = sum(m * u for m, u in zip(momentum, velocity))
    base = RELAX_RATE * (density - 1.5 * speed_sq)
    gray = {0: (1.0 - RELAX_RATE) * f[0] + W_REST * base}
    bent = 0.5 - solid
    for p in PAIRS:
        project = along(velocity, p)
        even = 0.5 * (1.0 - RELAX_RATE) * plus[p] + weight(p) * (
            base + (4.5 * RELAX_RATE) * density * (project * project)
        )
        turned = bent * odd[p]
        gray[p] = even + turned
        gray[p + 1] = even - turned
    return gray, odd


def collide_adjoint(f_moments, g, solid, accel):
    density, momentum = f_moments
    inverse = 1.0 / density
    velocity = [m * inverse for m in momentum]
    plus = {p: g[p] + g[p + 1] for p in PAIRS}
    fluid = 1.0 - 2.0 * solid
    minus = {p: fluid * (g[p] - g[p + 1]) for p in PAIRS}
    axis_sum = plus[1] + plus[3] + plus[5]
    diag_xy, diag_xz, diag_yz = plus[7] + plus[9], plus[11] + plus[13], plus[15] + plus[17]
    level = W_REST * g[0] + W_AXIS * axis_sum + W_DIAG * (diag_xy + diag_xz + diag_yz)
    second = {
        (0, 0): W_AXIS * plus[1] + W_DIAG * (diag_xy + diag_xz),
        (1, 1): W_AXIS * plus[3] + W_DIAG * (diag_xy + diag_yz),
        (2, 2): W_AXIS * plus[5] + W_DIAG * (diag_xz + diag_yz),
        (0, 1): W_DIAG * (plus[7] - plus[9]),
        (0, 2): W_DIAG * (plus[11] - plus[13]),
        (1, 2): W_DIAG * (plus[15] - plus[17]),
    }
    first = [
        W_AXIS * minus[1] + W_DIAG * (minus[7] + minus[9] + minus[11] + minus[13]),
        W_AXIS * minus[3] + W_DIAG * (minus[7] - minus[9] + minus[15] + minus[17]),
        W_AXIS * minus[5] + W_DIAG * (minus[11] - minus[13] + minus[15] - minus[17]),
    ]
    bent = [
        sum(second[(min(i, j), max(i, j))] * velocity[j] for j in range(3)) for i in range(3)
    ]
    pull = [
        RELAX_RATE * (3.0 * first[i] + 9.0 * bent[i] - (3.0 * level) * velocity[i])
        for i in range(3)
    ]
    speed_sq = sum(u * u for u in velocity)
    rest = RELAX_RATE * (
        level * (1.0 + 1.5 * speed_sq) - 4.5 * sum(b * u for b, u in zip(bent, velocity))
    )
    rest = rest + 3.0 * sum(a * b for a, b in zip(accel, first))
    out = {0: (1.0 - RELAX_RATE) * g[0] + rest}
    for p in PAIRS:
        even = 0.5 * (1.0 - RELAX_RATE) * plus[p] + rest
        odd = 0.5 * (1.0 - RELAX_RATE) * minus[p] + along(pull, p)
        out[p] = even + odd
        out[p + 1] = even - odd
    return out


def sens_terms(g, odd):
    return sum((g[p + 1] - g[p]) * odd[p] for p in PAIRS)


def lanes():
    return lax.broadcasted_iota(jnp.int32, (8, 128), 1)


def read_accel(accel_ref, turn):
    return [accel_ref[turn, axis] for axis in range(3)]


def is_even():
    return lax.axis_index("tile") & 1 == 0


def spread(row, blocks):
    row[...] = jnp.zeros_like(row)
    row[0:1, 0:16] = blocks
    wide = jnp.take_along_axis(row[...], lanes() // BLOCK, axis=1)
    return jnp.broadcast_to(wide[0:1], (8, 128))


def smooth(beside, grid):
    around = beside + 2.0 * grid + pltpu.roll(grid, 8, 1) + pltpu.roll(grid, 120, 1)
    return (grid + FACE_WEIGHT * around) * (1.0 / (1.0 + 6.0 * FACE_WEIGHT))


def read_layer(f_ref, q, x):
    two = f_ref[q, 16 * (x // 2) : 16 * (x // 2) + 16, :].astype(jnp.float32)
    return two[8:16] if x % 2 else two[0:8]


def pack(f_ref, adj_ref, out, high, solid, accel):
    near, far = (7, 6) if high else (0, 1)
    onward, back = (Q_PLUS, Q_MINUS) if high else (Q_MINUS, Q_PLUS)
    gray, _ = collide([read_layer(f_ref, q, near) for q in range(Q)], solid, accel)
    for i, q in enumerate(Q_ZERO + onward):
        out[i] = shift_yz(gray[q], q, 1)
    gray, _ = collide([read_layer(f_ref, q, far) for q in range(Q)], solid, accel)
    for i, q in enumerate(onward):
        out[ROW_FAR + i] = shift_yz(gray[q], q, 1)
    for i, q in enumerate(Q_ZERO + back):
        out[ROW_ADJ + i] = adj_ref[q, near]
    for i, q in enumerate(back):
        out[ROW_ADJ_FAR + i] = adj_ref[q, far]
    out[ROW_SOLID] = solid


def load_kernel(
    design_hbm,
    mask_hbm,
    accel_hbm,
    f_hbm,
    adj_hbm,
    blocks_out,
    accel_out,
    f_out,
    adj_out,
    design,
    mask,
    table,
    sems,
):
    copies = [
        pltpu.make_async_copy(source, target, sems.at[i])
        for i, (source, target) in enumerate(
            (
                (design_hbm, design),
                (mask_hbm, mask),
                (accel_hbm, table),
                (f_hbm, f_out),
                (adj_hbm, adj_out),
            )
        )
    ]
    for copy in copies:
        copy.start()
    for copy in copies[:3]:
        copy.wait()
    blocks_out[...] = design[...] * mask[...].astype(jnp.float32)
    for turn in range(2):
        for axis in range(3):
            value = table[turn, axis].astype(jnp.float32) * (1.0 / ACCEL_SCALE)
            accel_out[turn, axis] = jnp.full((8, 128), value, jnp.float32)
    for copy in copies[3:]:
        copy.wait()


def pack_beyond(f_ref, adj_ref, out, high, accel):
    near, far = (7, 6) if high else (0, 1)
    back = Q_MINUS if high else Q_PLUS
    post, _ = collide([read_layer(f_ref, q, near) for q in range(Q)], 0.0, accel)
    for q in range(Q):
        out[q] = post[q]
    post, _ = collide([read_layer(f_ref, q, far) for q in range(Q)], 0.0, accel)
    for i, p in enumerate(Q_PLUS):
        out[B_FAR + 2 * i] = post[p]
        out[B_FAR + 2 * i + 1] = post[p + 1]
    for i, q in enumerate(Q_ZERO + back):
        out[B_ADJ + i] = adj_ref[q, near]
    for i, q in enumerate(back):
        out[B_ADJ_FAR + i] = adj_ref[q, far]


def beyond_kernel(f_ref, adj_ref, accel_ref, own_ref, to_b, row):
    accel = read_accel(accel_ref, 0)
    to_b[B_BLOCKS] = spread(row, own_ref[...])
    even = is_even()
    pl.when(even)(lambda: pack_beyond(f_ref, adj_ref, to_b, False, accel))
    pl.when(jnp.logical_not(even))(lambda: pack_beyond(f_ref, adj_ref, to_b, True, accel))


def chip_kernel(
    f_ref,
    adj_ref,
    accel_ref,
    own_ref,
    mate_ref,
    past_ref,
    from_b,
    to_a,
    solid_out,
    solid_beyond,
    row,
):
    own = spread(row, own_ref[...])
    beside = from_b[B_BLOCKS]
    solid = SOLID_MAX * smooth(spread(row, mate_ref[...]) + beside, own)
    solid_out[...] = solid
    solid_beyond[...] = SOLID_MAX * smooth(own + spread(row, past_ref[...]), beside)
    accel = read_accel(accel_ref, 0)
    even = is_even()
    pl.when(even)(lambda: pack(f_ref, adj_ref, to_a, True, solid, accel))
    pl.when(jnp.logical_not(even))(lambda: pack(f_ref, adj_ref, to_a, False, solid, accel))


def mix(message, solid, row, q):
    value = message[row]
    if q == 0:
        return value
    opposite = message[row + 1 if q % 2 else row - 1]
    return shift_yz(value + solid * (opposite - value), q, 1)


def mid_kernel(
    accel_ref,
    solid_ref,
    beyond_ref,
    f_ref,
    adj_ref,
    from_b,
    g_out,
    f_next,
    odd_out,
    mom_out,
    sum_out,
    adj_ext,
    solid_ext,
):
    even = is_even()
    solid_own = solid_ref[...]
    solid_beyond = beyond_ref[...]
    accel_first = read_accel(accel_ref, 0)
    accel_second = read_accel(accel_ref, 1)
    for e in range(1, 11):
        solid_ext[e] = solid_own if 2 <= e < 10 else solid_beyond
    for q in range(Q):
        for x in range(8):
            adj_ext[q, 2 + x] = adj_ref[q, x]
        for e in (2, 3, 8, 9):
            g_out[q, e] = jnp.zeros((8, 128), jnp.float32)

    def forward(k, _):
        for half in range(2):
            e = 2 * k + 2 + half
            f = [
                f_ref[q, pl.ds(pl.multiple_of(16 * k, 16), 16), :].astype(jnp.float32)[
                    8 * half : 8 * half + 8
                ]
                for q in range(Q)
            ]
            gray, odd = collide(f, solid_own, accel_first)
            density, momentum, _, _ = moments(f)
            for i, part in enumerate([density] + momentum):
                mom_out[i, e - 2] = part
            for q in range(Q):
                f_next[q, e + 1 + VELOCITIES[q][0]] = shift_yz(gray[q], q, 1)
            for i, p in enumerate(PAIRS):
                odd_out[i, e] = odd[p]
        return 0

    lax.fori_loop(0, 4, forward, 0)

    def far_side(low):
        face, beside, far = (2, 1, 0) if low else (9, 10, 11)
        inward, outward = (Q_PLUS, Q_MINUS) if low else (Q_MINUS, Q_PLUS)
        first = 0 if low else 1
        for q in Q_ZERO:
            f_next[q, beside + 1] = mix(from_b, solid_beyond, q, q)
        for i, q in enumerate(inward):
            f_next[q, face + 1] = mix(from_b, solid_beyond, q, q)
            f_next[q, beside + 1] = mix(from_b, solid_beyond, B_FAR + 2 * i + first, q)
        for i, q in enumerate(Q_ZERO + outward):
            adj_ext[q, beside] = from_b[B_ADJ + i]
        for i, q in enumerate(outward):
            adj_ext[q, far] = from_b[B_ADJ_FAR + i]

    pl.when(even)(lambda: far_side(True))
    pl.when(jnp.logical_not(even))(lambda: far_side(False))

    def backward(e, total):
        f = [f_next[q, e + 1] for q in range(Q)]
        g = [shift_yz(adj_ext[q, e + VELOCITIES[q][0]], q, -1) for q in range(Q)]
        density, momentum, _, minus = moments(f)
        odd = odd_parts(density, momentum, minus, accel_second)
        inside = jnp.logical_and(e >= 2, e < 10)
        total = total + jnp.where(inside, sens_terms(g, odd), 0.0)
        adjoint = collide_adjoint((density, momentum), g, solid_ext[e], accel_second)
        for q in range(Q):
            g_out[q, e - VELOCITIES[q][0]] = shift_yz(adjoint[q], q, -1)
        return total

    first = jnp.where(even, 1, 3)
    total = lax.fori_loop(first, first + 8, backward, jnp.zeros((8, 128), jnp.float32))

    def early(e, total):
        g = [g_out[q, e] for q in range(Q)]
        odd = {p: odd_out[i, e] for i, p in enumerate(PAIRS)}
        return total + sens_terms(g, odd)

    sum_out[...] = lax.fori_loop(2, 10, early, total)


def edge(low, message, solid_own, f_next, adj_ref, accel):
    inward, outward = (Q_PLUS, Q_MINUS) if low else (Q_MINUS, Q_PLUS)
    beside, face, layer, behind = (2, 3, 0, 1) if low else (11, 10, 7, 6)
    adj = {q: message[ROW_ADJ + i] for i, q in enumerate(Q_ZERO + outward)}

    f = {q: message[ROW_FAR + i] for i, q in enumerate(inward)}
    f.update({q: message[i] for i, q in enumerate(Q_ZERO)})
    f.update({q: f_next[q, beside] for q in outward})
    g = {q: message[ROW_ADJ_FAR + i] for i, q in enumerate(outward)}
    g.update({q: adj[q] for q in Q_ZERO})
    g.update({q: adj_ref[q, layer] for q in inward})
    g = {q: shift_yz(g[q], q, -1) for q in range(Q)}
    density, momentum, _, _ = moments(f)
    adj_beside = collide_adjoint((density, momentum), g, message[ROW_SOLID], accel)

    f = {q: f_next[q, face] for q in Q_ZERO + outward}
    f.update({q: message[len(Q_ZERO) + i] for i, q in enumerate(inward)})
    g = {q: adj[q] for q in outward}
    g.update({q: adj_ref[q, layer] for q in Q_ZERO})
    g.update({q: adj_ref[q, behind] for q in inward})
    g = {q: shift_yz(g[q], q, -1) for q in range(Q)}
    density, momentum, _, minus = moments(f)
    odd = odd_parts(density, momentum, minus, accel)
    adj_face = collide_adjoint((density, momentum), g, solid_own, accel)
    adj_beside = {q: shift_yz(adj_beside[q], q, -1) for q in outward}
    adj_face = {q: shift_yz(adj_face[q], q, -1) for q in Q_ZERO + outward}
    return adj_beside, adj_face, sens_terms(g, odd)


def turned_odd(odd, q):
    return -odd[q] if q % 2 else odd[q - 1]


def edge_kernel(
    message,
    accel_ref,
    solid_ref,
    f_next,
    adj_ref,
    g_ref,
    odd_ref,
    sum_ref,
    head_out,
    tail_out,
    sums_out,
    turned_out,
    own_sum,
):
    for q in range(Q):
        head_out[q, 0] = g_ref[q, 2]
        head_out[q, 1] = g_ref[q, 3]
        tail_out[q, 0] = g_ref[q, 8]
        tail_out[q, 1] = g_ref[q, 9]

    def side(low):
        adj_beside, adj_face, own = edge(
            low, message, solid_ref[...], f_next, adj_ref, read_accel(accel_ref, 1)
        )
        face, behind = (2, 3) if low else (9, 8)
        out, at_face, at_behind = (head_out, 0, 1) if low else (tail_out, 1, 0)
        first = {p: odd_ref[i, face] for i, p in enumerate(PAIRS)}
        second = {p: odd_ref[i, behind] for i, p in enumerate(PAIRS)}
        for q in Q_ZERO:
            if q:
                own = own + adj_face[q] * turned_odd(first, q)
            out[q, at_face] = adj_face[q]
        for q in Q_MINUS if low else Q_PLUS:
            own = own + adj_beside[q] * turned_odd(first, q)
            own = own + adj_face[q] * turned_odd(second, q)
            out[q, at_face] = adj_beside[q]
            out[q, at_behind] = adj_face[q]
        own_sum[...] = own + sum_ref[...]

    even = is_even()
    pl.when(even)(lambda: side(False))
    pl.when(jnp.logical_not(even))(lambda: side(True))

    total = jnp.broadcast_to(jnp.sum(own_sum[...], axis=0, keepdims=True), (8, 128))
    for step in (1, 2, 4):
        total = total + pltpu.roll(total, 128 - step, 1)
    total = jnp.where(lanes() % BLOCK == 0, total, 0.0)
    sums_out[...] = total[0:1]
    turned_out[...] = pltpu.roll(total, 1, 1)[0:1]


def start_kernel(accel_ref, solid_ref, g_ref, mom_ref, head_ref, tail_ref, out_ref):
    accel = read_accel(accel_ref, 0)
    solid = solid_ref[...]

    def layers(low, high, source, offset):
        def step(x, _):
            g = [source[q, x + offset] for q in range(Q)]
            momentum = [mom_ref[1 + axis, x] for axis in range(3)]
            adjoint = collide_adjoint((mom_ref[0, x], momentum), g, solid, accel)
            for q in range(Q):
                out_ref[q, x] = adjoint[q]
            return 0

        lax.fori_loop(low, high, step, 0)

    layers(0, 2, head_ref, 0)
    layers(2, 6, g_ref, 2)
    layers(6, 8, tail_ref, -6)


def share_kernel(sums_ref, outside_ref, out):
    out[...] = jnp.broadcast_to((sums_ref[...] + outside_ref[...])[None], out.shape)


def update_kernel(
    cases,
    sums_ref,
    design_ref,
    mask_ref,
    first_ref,
    second_ref,
    design_out,
    first_out,
    second_out,
):
    place = (lax.axis_index("tile") - OFFSET) & (GROUP - 1)
    totals = []
    for tile in range(GROUP):
        total = sums_ref[tile * cases]
        for case in range(1, cases):
            total = total + sums_ref[tile * cases + case]
        totals.append(jnp.broadcast_to(total, (8, 128)))

    line = [pltpu.roll(totals[0], 127, 1)] + totals + [pltpu.roll(totals[-1], 127, 1)]

    def pick(shift):
        value = line[shift]
        for k in range(1, GROUP):
            value = jnp.where(place == k, line[k + shift], value)
        return value

    gradient = SOLID_MAX * smooth(pick(0) + pick(2), pick(1))
    spots = jnp.minimum(lanes() * BLOCK, 127)
    gradient = jnp.take_along_axis(gradient, spots, axis=1)[0:1, 0:16]
    gradient = mask_ref[...].astype(jnp.float32) * gradient
    first = BETA_ONE * first_ref[...] + (1.0 - BETA_ONE) * gradient
    second = BETA_TWO * second_ref[...] + (1.0 - BETA_TWO) * gradient * gradient
    stepped = design_ref[...] - LEARN_RATE * (first * (1.0 / BIAS_ONE)) / (
        jnp.sqrt(second * (1.0 / BIAS_TWO)) + ADAM_EPS
    )
    design_out[...] = jnp.clip(stepped, 0.0, 1.0)
    first_out[...] = first
    second_out[...] = second


def tables(tiles, cases):
    run = RUN if tiles % RUN == 0 else tiles

    def device(tile, case):
        return (tile % tiles) * cases + case

    def near(tile, step, case):
        target = tile + step
        crossed = (target // run) != (tile // run)
        return device(target, case ^ 1 if crossed else case)

    found = {name: [] for name in ("chip", "beyond", "past", "ends")}
    for tile in range(tiles):
        step = 1 if tile % 2 else -1
        for case in range(cases):
            here = device(tile, case)
            found["chip"].append((here, device(tile ^ 1, case)))
            found["beyond"].append((here, device(tile + step, case)))
            found["past"].append((here, near(tile, -2 * step, case)))
            place = (tile - OFFSET) % GROUP
            if place == 0:
                found["ends"].append((here, device(tile - 1, case)))
            if place == GROUP - 1:
                found["ends"].append((here, device(tile + 1, case)))
    groups = [
        [device(OFFSET + g * GROUP + k, case) for k in range(GROUP) for case in range(cases)]
        for g in range(tiles // GROUP)
    ]
    return found, groups


VMEM_SPEC = pl.BlockSpec(memory_space=pltpu.VMEM)
HBM_SPEC = pl.BlockSpec(memory_space=pltpu.HBM)
F32 = jnp.float32


def body(
    tiles,
    cases,
    checkpoint,
    adjoint_field,
    accel_table,
    design,
    design_mask,
    first_moment,
    second_moment,
):
    axes = ("tile", "case")
    pairs, groups = tables(tiles, cases)
    f_zero = checkpoint.reshape(Q, 64, 128)
    adjoint = adjoint_field[0]
    flat = [a.reshape(1, 16) for a in (design, design_mask, first_moment, second_moment)]
    params = pltpu.CompilerParams(vmem_limit_bytes=32 * 1024 * 1024)

    def send(value, name):
        return lax.ppermute(value, axes, pairs[name])

    def call(kernel, name, out_shape, in_specs, scratch, *args):
        many = isinstance(out_shape, tuple)
        return pl.pallas_call(
            kernel,
            out_shape=out_shape,
            in_specs=in_specs,
            out_specs=[VMEM_SPEC] * len(out_shape) if many else VMEM_SPEC,
            scratch_shapes=scratch,
            compiler_params=params,
            name=name,
        )(*args)

    def shape(*dims):
        return jax.ShapeDtypeStruct(dims, F32)

    row = pltpu.VMEM((8, 128), F32)
    blocks, accel, f_zero, adjoint = call(
        load_kernel,
        "load",
        (
            shape(1, 16),
            shape(2, 3, 8, 128),
            jax.ShapeDtypeStruct((Q, 64, 128), jnp.bfloat16),
            shape(Q, 8, 8, 128),
        ),
        [HBM_SPEC] * 5,
        [
            pltpu.VMEM((1, 16), F32),
            pltpu.VMEM((1, 16), jnp.int32),
            pltpu.SMEM((2, 3), jnp.int32),
            pltpu.SemaphoreType.DMA((5,)),
        ],
        *(
            pltpu.with_memory_space_constraint(a, pltpu.HBM)
            for a in (flat[0], flat[1], accel_table[0], f_zero, adjoint)
        ),
    )
    to_b = call(
        beyond_kernel,
        "pack_beyond",
        shape(B_ROWS, 8, 128),
        [VMEM_SPEC] * 4,
        [row],
        f_zero,
        adjoint,
        accel,
        blocks,
    )
    from_b = send(to_b, "beyond")
    mate = send(blocks, "chip")
    past = send(blocks, "past")
    to_a, solid, solid_beyond = call(
        chip_kernel,
        "pack_chip",
        (shape(ROWS, 8, 128), shape(8, 128), shape(8, 128)),
        [VMEM_SPEC] * 7,
        [row],
        f_zero,
        adjoint,
        accel,
        blocks,
        mate,
        past,
        from_b,
    )
    from_a = send(to_a, "chip")
    g_one, f_next, odd, mom, sums = call(
        mid_kernel,
        "middle",
        (
            shape(Q, 12, 8, 128),
            shape(Q, 14, 8, 128),
            shape(len(PAIRS), 12, 8, 128),
            shape(4, 8, 8, 128),
            shape(8, 128),
        ),
        [VMEM_SPEC] * 6,
        [pltpu.VMEM((Q, 12, 8, 128), F32), pltpu.VMEM((12, 8, 128), F32)],
        accel,
        solid,
        solid_beyond,
        f_zero,
        adjoint,
        from_b,
    )
    head, tail, sums, turned = call(
        edge_kernel,
        "chip_edge",
        (shape(Q, 2, 8, 128), shape(Q, 2, 8, 128), shape(1, 128), shape(1, 128)),
        [VMEM_SPEC] * 8,
        [row],
        from_a,
        accel,
        solid,
        f_next,
        adjoint,
        g_one,
        odd,
        sums,
    )
    outside = send(turned, "ends")
    payload = call(
        share_kernel, "share", shape(GROUP * cases, 1, 128), [VMEM_SPEC] * 2, [], sums, outside
    )
    payload, head = lax.optimization_barrier((payload, head))
    shared = lax.all_to_all(payload, axes, 0, 0, axis_index_groups=groups, tiled=True)
    start = call(
        start_kernel,
        "adjoint_start",
        shape(Q, 8, 8, 128),
        [VMEM_SPEC] * 6,
        [],
        accel,
        solid,
        g_one,
        mom,
        head,
        tail,
    )
    small = shape(1, 16)
    updated = call(
        functools.partial(update_kernel, cases),
        "update",
        (small, small, small),
        [VMEM_SPEC] * 5,
        [],
        shared,
        *flat,
    )
    return (start[None],) + tuple(u.reshape(1, 1, 16) for u in updated)


def solution(mesh):
    placed = (
        P("case", None, "tile", None, None),
        P("case", None, "tile", None, None),
        P("case", None, None),
        P("tile", None, None),
        P("tile", None, None),
        P("tile", None, None),
        P("tile", None, None),
    )
    return jax.shard_map(
        functools.partial(body, mesh.shape["tile"], mesh.shape["case"]),
        mesh=mesh,
        in_specs=placed,
        out_specs=(
            P("case", None, "tile", None, None),
            P("tile", None, None),
            P("tile", None, None),
            P("tile", None, None),
        ),
        check_vma=False,
    )
```

```python
import functools

import jax
import jax.numpy as jnp
import numpy as np
from jax import lax
from jax.experimental import pallas as pl
from jax.experimental.pallas import tpu as pltpu
from jax.sharding import PartitionSpec as P

Q = 19
BLOCK = 8
VELOCITIES = [
    (0, 0, 0),
    (1, 0, 0),
    (-1, 0, 0),
    (0, 1, 0),
    (0, -1, 0),
    (0, 0, 1),
    (0, 0, -1),
    (1, 1, 0),
    (-1, -1, 0),
    (1, -1, 0),
    (-1, 1, 0),
    (1, 0, 1),
    (-1, 0, -1),
    (1, 0, -1),
    (-1, 0, 1),
    (0, 1, 1),
    (0, -1, -1),
    (0, 1, -1),
    (0, -1, 1),
]
W_REST, W_AXIS, W_DIAG = 1.0 / 3.0, 1.0 / 18.0, 1.0 / 36.0
RELAX_RATE = 0.9
SOLID_MAX = 0.5
FACE_WEIGHT = 0.5
ACCEL_SCALE = 400.0
BETA_ONE = 0.9
BETA_TWO = 0.999
LEARN_RATE = 0.2
ADAM_EPS = 1e-08
BIAS_ONE = 1.0 - 0.9**10
BIAS_TWO = 1.0 - 0.999**10

PAIRS = tuple(range(1, Q, 2))
Q_ZERO = [q for q in range(Q) if VELOCITIES[q][0] == 0]
Q_PLUS = [q for q in range(Q) if VELOCITIES[q][0] == 1]
Q_MINUS = [q for q in range(Q) if VELOCITIES[q][0] == -1]
ROW_FAR = Q
ROW_ADJ = ROW_FAR + 2 * len(Q_PLUS)
ROW_ADJ_FAR = ROW_ADJ + len(Q_ZERO) + len(Q_PLUS)
ROW_BLOCKS = ROW_ADJ_FAR + len(Q_PLUS)
ROWS = ROW_BLOCKS + 1
B_ROWS = ROWS + 1
RUN = 16
FORWARD_UNROLL = 2
BACKWARD_UNROLL = 6
GROUP = 8
OFFSET = 5


def shift_yz(value, vel_id, direction):
    _, shift_y, shift_z = VELOCITIES[vel_id]
    if shift_y:
        value = pltpu.roll(value, (direction * shift_y) % 8, 0)
    if shift_z:
        value = pltpu.roll(value, (direction * shift_z) % 128, 1)
    return value


def along(vector, vel_id):
    total = None
    for part, sign in zip(vector, VELOCITIES[vel_id]):
        if sign == 0:
            continue
        if total is None:
            total = part if sign > 0 else -part
        else:
            total = total + part if sign > 0 else total - part
    return total


def weight(pair):
    return W_AXIS if pair < 7 else W_DIAG


def moments(f):
    plus = {p: f[p] + f[p + 1] for p in PAIRS}
    minus = {p: f[p] - f[p + 1] for p in PAIRS}
    density = f[0]
    for p in PAIRS:
        density = density + plus[p]
    momentum = []
    for axis in range(3):
        total = None
        for p in PAIRS:
            sign = VELOCITIES[p][axis]
            if sign == 0:
                continue
            if total is None:
                total = minus[p]
            else:
                total = total + minus[p] if sign > 0 else total - minus[p]
        momentum.append(total)
    return density, momentum, plus, minus


def odd_parts(density, momentum, minus, accel):
    flow = [3.0 * RELAX_RATE * m + (3.0 * a) * density for m, a in zip(momentum, accel)]
    return {
        p: (1.0 - RELAX_RATE) * minus[p] + (2.0 * weight(p)) * along(flow, p) for p in PAIRS
    }


def collide(f, solid, accel):
    density, momentum, plus, minus = moments(f)
    odd = odd_parts(density, momentum, minus, accel)
    inverse = 1.0 / density
    velocity = [m * inverse for m in momentum]
    speed_sq = sum(m * u for m, u in zip(momentum, velocity))
    base = RELAX_RATE * (density - 1.5 * speed_sq)
    gray = {0: (1.0 - RELAX_RATE) * f[0] + W_REST * base}
    bent = 0.5 - solid
    for p in PAIRS:
        project = along(velocity, p)
        even = 0.5 * (1.0 - RELAX_RATE) * plus[p] + weight(p) * (
            base + (4.5 * RELAX_RATE) * density * (project * project)
        )
        turned = bent * odd[p]
        gray[p] = even + turned
        gray[p + 1] = even - turned
    return gray, odd


def collide_adjoint(f_moments, g, solid, accel):
    density, momentum = f_moments
    inverse = 1.0 / density
    velocity = [m * inverse for m in momentum]
    plus = {p: g[p] + g[p + 1] for p in PAIRS}
    fluid = 1.0 - 2.0 * solid
    minus = {p: fluid * (g[p] - g[p + 1]) for p in PAIRS}
    axis_sum = plus[1] + plus[3] + plus[5]
    diag_xy, diag_xz, diag_yz = plus[7] + plus[9], plus[11] + plus[13], plus[15] + plus[17]
    level = W_REST * g[0] + W_AXIS * axis_sum + W_DIAG * (diag_xy + diag_xz + diag_yz)
    second = {
        (0, 0): W_AXIS * plus[1] + W_DIAG * (diag_xy + diag_xz),
        (1, 1): W_AXIS * plus[3] + W_DIAG * (diag_xy + diag_yz),
        (2, 2): W_AXIS * plus[5] + W_DIAG * (diag_xz + diag_yz),
        (0, 1): W_DIAG * (plus[7] - plus[9]),
        (0, 2): W_DIAG * (plus[11] - plus[13]),
        (1, 2): W_DIAG * (plus[15] - plus[17]),
    }
    first = [
        W_AXIS * minus[1] + W_DIAG * (minus[7] + minus[9] + minus[11] + minus[13]),
        W_AXIS * minus[3] + W_DIAG * (minus[7] - minus[9] + minus[15] + minus[17]),
        W_AXIS * minus[5] + W_DIAG * (minus[11] - minus[13] + minus[15] - minus[17]),
    ]
    bent = [
        sum(second[(min(i, j), max(i, j))] * velocity[j] for j in range(3)) for i in range(3)
    ]
    pull = [
        RELAX_RATE * (3.0 * first[i] + 9.0 * bent[i] - (3.0 * level) * velocity[i])
        for i in range(3)
    ]
    speed_sq = sum(u * u for u in velocity)
    rest = RELAX_RATE * (
        level * (1.0 + 1.5 * speed_sq) - 4.5 * sum(b * u for b, u in zip(bent, velocity))
    )
    rest = rest + 3.0 * sum(a * b for a, b in zip(accel, first))
    out = {0: (1.0 - RELAX_RATE) * g[0] + rest}
    for p in PAIRS:
        even = 0.5 * (1.0 - RELAX_RATE) * plus[p] + rest
        odd = 0.5 * (1.0 - RELAX_RATE) * minus[p] + along(pull, p)
        out[p] = even + odd
        out[p + 1] = even - odd
    return out


def sens_terms(g, odd):
    return sum((g[p + 1] - g[p]) * odd[p] for p in PAIRS)


def lanes():
    return lax.broadcasted_iota(jnp.int32, (8, 128), 1)


def read_accel(accel_ref, turn):
    return [accel_ref[turn, axis] for axis in range(3)]


def is_even():
    return lax.axis_index("tile") & 1 == 0


def spread(row, blocks):
    row[...] = jnp.zeros_like(row)
    row[0:1, 0:16] = blocks
    wide = jnp.take_along_axis(row[...], lanes() // BLOCK, axis=1)
    return jnp.broadcast_to(wide[0:1], (8, 128))


def smooth(beside, grid):
    around = beside + 2.0 * grid + pltpu.roll(grid, 8, 1) + pltpu.roll(grid, 120, 1)
    return (grid + FACE_WEIGHT * around) * (1.0 / (1.0 + 6.0 * FACE_WEIGHT))


def read_layer(f_ref, q, x):
    two = f_ref[q, 16 * (x // 2) : 16 * (x // 2) + 16, :].astype(jnp.float32)
    return two[8:16] if x % 2 else two[0:8]


def load_kernel(
    design_hbm,
    mask_hbm,
    accel_hbm,
    first_hbm,
    second_hbm,
    f_hbm,
    adj_hbm,
    blocks_out,
    accel_out,
    design_out,
    mask_out,
    first_out,
    second_out,
    f_out,
    adj_out,
    table,
    sems,
):
    copies = [
        pltpu.make_async_copy(source, target, sems.at[i])
        for i, (source, target) in enumerate(
            (
                (design_hbm, design_out),
                (mask_hbm, mask_out),
                (accel_hbm, table),
                (first_hbm, first_out),
                (second_hbm, second_out),
                (f_hbm, f_out),
                (adj_hbm, adj_out),
            )
        )
    ]
    for copy in copies:
        copy.start()
    for copy in copies[:5]:
        copy.wait()
    blocks_out[...] = design_out[...] * mask_out[...].astype(jnp.float32)
    for turn in range(2):
        for axis in range(3):
            value = table[turn, axis].astype(jnp.float32) * (1.0 / ACCEL_SCALE)
            accel_out[turn, axis] = jnp.full((8, 128), value, jnp.float32)
    for copy in copies[5:]:
        copy.wait()


def pack(f_ref, adj_ref, out, high, blocks, accel):
    near, far = (7, 6) if high else (0, 1)
    back = Q_MINUS if high else Q_PLUS
    post, _ = collide([read_layer(f_ref, q, near) for q in range(Q)], 0.0, accel)
    for q in range(Q):
        out[q] = post[q]
    post, _ = collide([read_layer(f_ref, q, far) for q in range(Q)], 0.0, accel)
    for i, p in enumerate(Q_PLUS):
        out[ROW_FAR + 2 * i] = post[p]
        out[ROW_FAR + 2 * i + 1] = post[p + 1]
    for i, q in enumerate(Q_ZERO + back):
        out[ROW_ADJ + i] = adj_ref[q, near]
    for i, q in enumerate(back):
        out[ROW_ADJ_FAR + i] = adj_ref[q, far]
    out[ROW_BLOCKS] = blocks


def pack_kernel(f_ref, adj_ref, accel_ref, own_ref, to_b, to_a, row):
    accel = read_accel(accel_ref, 0)
    blocks = spread(row, own_ref[...])
    for r in range(ROWS, B_ROWS):
        to_b[r] = jnp.zeros((8, 128), jnp.float32)

    def both(low, high):
        pack(f_ref, adj_ref, low, False, blocks, accel)
        pack(f_ref, adj_ref, high, True, blocks, accel)

    even = is_even()
    pl.when(even)(lambda: both(to_b, to_a))
    pl.when(jnp.logical_not(even))(lambda: both(to_a, to_b))


def boundary(low, message, solid, solid_own, f_next, adj_ref, accel):
    inward, outward = (Q_PLUS, Q_MINUS) if low else (Q_MINUS, Q_PLUS)
    beside, face, layer, behind = (2, 3, 0, 1) if low else (11, 10, 7, 6)
    first = 0 if low else 1

    def mixed(row, q):
        value = message[row]
        if q:
            opposite = message[row + 1 if q % 2 else row - 1]
            value = shift_yz(value + solid * (opposite - value), q, 1)
        return value

    adj = {q: message[ROW_ADJ + i] for i, q in enumerate(Q_ZERO + outward)}
    f = {q: mixed(ROW_FAR + 2 * i + first, q) for i, q in enumerate(inward)}
    f.update({q: mixed(q, q) for q in Q_ZERO})
    f.update({q: f_next[q, beside] for q in outward})
    g = {q: message[ROW_ADJ_FAR + i] for i, q in enumerate(outward)}
    g.update({q: adj[q] for q in Q_ZERO})
    g.update({q: adj_ref[q, layer] for q in inward})
    g = {q: shift_yz(g[q], q, -1) for q in range(Q)}
    density, momentum, _, _ = moments(f)
    adj_beside = collide_adjoint((density, momentum), g, solid, accel)

    f = {q: f_next[q, face] for q in Q_ZERO + outward}
    f.update({q: mixed(q, q) for q in inward})
    g = {q: adj[q] for q in outward}
    g.update({q: adj_ref[q, layer] for q in Q_ZERO})
    g.update({q: adj_ref[q, behind] for q in inward})
    g = {q: shift_yz(g[q], q, -1) for q in range(Q)}
    density, momentum, _, minus = moments(f)
    odd = odd_parts(density, momentum, minus, accel)
    adj_face = collide_adjoint((density, momentum), g, solid_own, accel)
    adj_beside = {q: shift_yz(adj_beside[q], q, -1) for q in outward}
    adj_face = {q: shift_yz(adj_face[q], q, -1) for q in Q_ZERO + outward}
    return adj_beside, adj_face, sens_terms(g, odd)


def boundary_sens(low, adj_beside, adj_face, odd_ref):
    face, behind = (2, 3) if low else (9, 8)
    total = 0.0
    for q in Q_ZERO:
        if q:
            total = total + adj_face[q] * turned(odd_ref, face, q)
    for q in Q_MINUS if low else Q_PLUS:
        total = total + adj_beside[q] * turned(odd_ref, face, q)
        total = total + adj_face[q] * turned(odd_ref, behind, q)
    return total


def sens_kernel(
    accel_ref,
    f_ref,
    adj_ref,
    from_a,
    from_b,
    own_ref,
    within_ref,
    across_ref,
    g_out,
    mom_out,
    solid_out,
    sums_out,
    turned_out,
    f_next,
    odd_ext,
    row,
    past_row,
):
    accel_first = read_accel(accel_ref, 0)
    accel_second = read_accel(accel_ref, 1)
    own = spread(row, own_ref[...])
    solid_own = SOLID_MAX * smooth(from_a[ROW_BLOCKS] + from_b[ROW_BLOCKS], own)
    solid_out[...] = solid_own

    def forward(k, _):
        for half in range(2):
            e = 2 * k + 2 + half
            f = [
                f_ref[q, pl.ds(pl.multiple_of(16 * k, 16), 16), :].astype(jnp.float32)[
                    8 * half : 8 * half + 8
                ]
                for q in range(Q)
            ]
            gray, odd = collide(f, solid_own, accel_first)
            density, momentum, _, _ = moments(f)
            for i, part in enumerate([density] + momentum):
                mom_out[i, e - 2] = part
            for q in range(Q):
                f_next[q, e + 1 + VELOCITIES[q][0]] = shift_yz(gray[q], q, 1)
            for i, p in enumerate(PAIRS):
                odd_ext[i, e] = odd[p]
        return 0

    lax.fori_loop(0, 4, forward, 0, unroll=FORWARD_UNROLL)

    def backward(e, total):
        f = [f_next[q, e + 1] for q in range(Q)]
        g = [shift_yz(adj_ref[q, e - 2 + VELOCITIES[q][0]], q, -1) for q in range(Q)]
        density, momentum, _, minus = moments(f)
        odd = odd_parts(density, momentum, minus, accel_second)
        total = total + sens_terms(g, odd)
        adjoint = collide_adjoint((density, momentum), g, solid_own, accel_second)
        for q in range(Q):
            to = e - VELOCITIES[q][0]
            value = shift_yz(adjoint[q], q, -1)
            g_out[q, to] = value
            if q:
                total = total + value * turned(odd_ext, to, q)
        return total

    total = lax.fori_loop(
        3, 9, backward, jnp.zeros((8, 128), jnp.float32), unroll=BACKWARD_UNROLL
    )
    row[...] = total

    odd_chip = lax.axis_index("tile") & 2 == 2

    def side(low, message):
        outward = Q_MINUS if low else Q_PLUS
        past = jnp.where(odd_chip == low, within_ref[...], across_ref[...])
        solid = SOLID_MAX * smooth(own + spread(past_row, past), message[ROW_BLOCKS])
        adj_beside, adj_face, sens = boundary(
            low, message, solid, solid_own, f_next, adj_ref, accel_second
        )
        face, behind = (2, 3) if low else (9, 8)
        for q in Q_ZERO:
            g_out[q, face] = adj_face[q]
        for q in outward:
            g_out[q, face] = adj_beside[q]
            g_out[q, behind] = adj_face[q]
        row[...] += sens + boundary_sens(low, adj_beside, adj_face, odd_ext)

    def both(low, high):
        side(True, low)
        side(False, high)

    even = is_even()
    pl.when(even)(lambda: both(from_b, from_a))
    pl.when(jnp.logical_not(even))(lambda: both(from_a, from_b))

    total = jnp.broadcast_to(jnp.sum(row[...], axis=0, keepdims=True), (8, 128))
    for step in (1, 2, 4):
        total = total + pltpu.roll(total, 128 - step, 1)
    total = jnp.where(lanes() % BLOCK == 0, total, 0.0)
    sums_out[...] = total[0:1]
    turned_out[...] = pltpu.roll(total, 1, 1)[0:1]


def turned(odd_ref, layer, q):
    return -odd_ref[q // 2, layer] if q % 2 else odd_ref[q // 2 - 1, layer]


def start_kernel(accel_ref, solid_ref, g_ref, mom_ref, out_ref):
    accel = read_accel(accel_ref, 0)
    solid = solid_ref[...]

    def layer(x, _):
        g = [g_ref[q, x + 2] for q in range(Q)]
        momentum = [mom_ref[1 + axis, x] for axis in range(3)]
        adjoint = collide_adjoint((mom_ref[0, x], momentum), g, solid, accel)
        for q in range(Q):
            out_ref[q, x] = adjoint[q]
        return 0

    lax.fori_loop(0, 8, layer, 0)


def share_kernel(sums_ref, outside_ref, out):
    out[...] = jnp.broadcast_to((sums_ref[...] + outside_ref[...])[None], out.shape)


def update_kernel(
    cases,
    sums_ref,
    design_ref,
    mask_ref,
    first_ref,
    second_ref,
    design_out,
    first_out,
    second_out,
):
    place = (lax.axis_index("tile") - OFFSET) & (GROUP - 1)
    totals = []
    for tile in range(GROUP):
        total = sums_ref[tile * cases]
        for case in range(1, cases):
            total = total + sums_ref[tile * cases + case]
        totals.append(jnp.broadcast_to(total, (8, 128)))

    line = [pltpu.roll(totals[0], 127, 1)] + totals + [pltpu.roll(totals[-1], 127, 1)]

    def pick(shift):
        value = line[shift]
        for k in range(1, GROUP):
            value = jnp.where(place == k, line[k + shift], value)
        return value

    gradient = SOLID_MAX * smooth(pick(0) + pick(2), pick(1))
    spots = jnp.minimum(lanes() * BLOCK, 127)
    gradient = jnp.take_along_axis(gradient, spots, axis=1)[0:1, 0:16]
    gradient = mask_ref[...].astype(jnp.float32) * gradient
    first = BETA_ONE * first_ref[...] + (1.0 - BETA_ONE) * gradient
    second = BETA_TWO * second_ref[...] + (1.0 - BETA_TWO) * gradient * gradient
    stepped = design_ref[...] - LEARN_RATE * (first * (1.0 / BIAS_ONE)) / (
        jnp.sqrt(second * (1.0 / BIAS_TWO)) + ADAM_EPS
    )
    design_out[...] = jnp.clip(stepped, 0.0, 1.0)
    first_out[...] = first
    second_out[...] = second


def tables(tiles, cases):
    run = RUN if tiles % RUN == 0 else tiles

    def device(tile, case):
        return (tile % tiles) * cases + case

    def near(tile, step, case):
        target = tile + step
        crossed = (target // run) != (tile // run)
        return device(target, case ^ 1 if crossed else case)

    found = {name: [] for name in ("chip", "beyond", "across", "within", "ends")}
    for tile in range(tiles):
        step = 1 if tile % 2 else -1
        for case in range(cases):
            here = device(tile, case)
            found["chip"].append((here, device(tile ^ 1, case)))
            found["beyond"].append((here, device(tile + step, case)))
            odd_chip = (tile // 2) % 2
            found["across"].append((here, near(tile, 2 if odd_chip else -2, case)))
            found["within"].append((here, near(tile, -2 if odd_chip else 2, case)))
            place = (tile - OFFSET) % GROUP
            if place == 0:
                found["ends"].append((here, device(tile - 1, case)))
            if place == GROUP - 1:
                found["ends"].append((here, device(tile + 1, case)))
    groups = [
        [device(OFFSET + g * GROUP + k, case) for k in range(GROUP) for case in range(cases)]
        for g in range(tiles // GROUP)
    ]
    return found, groups


VMEM_SPEC = pl.BlockSpec(memory_space=pltpu.VMEM)
HBM_SPEC = pl.BlockSpec(memory_space=pltpu.HBM)
F32 = jnp.float32


def body(
    tiles,
    cases,
    checkpoint,
    adjoint_field,
    accel_table,
    design,
    design_mask,
    first_moment,
    second_moment,
):
    axes = ("tile", "case")
    pairs, groups = tables(tiles, cases)
    f_zero = checkpoint.reshape(Q, 64, 128)
    adjoint = adjoint_field[0]
    flat = [a.reshape(1, 16) for a in (design, design_mask, first_moment, second_moment)]
    params = pltpu.CompilerParams(vmem_limit_bytes=32 * 1024 * 1024)

    def send(value, name):
        return lax.ppermute(value, axes, pairs[name])

    def call(kernel, name, out_shape, in_specs, scratch, *args):
        many = isinstance(out_shape, tuple)
        return pl.pallas_call(
            kernel,
            out_shape=out_shape,
            in_specs=in_specs,
            out_specs=[VMEM_SPEC] * len(out_shape) if many else VMEM_SPEC,
            scratch_shapes=scratch,
            compiler_params=params,
            name=name,
        )(*args)

    def shape(*dims):
        return jax.ShapeDtypeStruct(dims, F32)

    row = pltpu.VMEM((8, 128), F32)
    blocks, accel, *kept, f_zero, adjoint = call(
        load_kernel,
        "load",
        (
            shape(1, 16),
            shape(2, 3, 8, 128),
            shape(1, 16),
            jax.ShapeDtypeStruct((1, 16), jnp.int32),
            shape(1, 16),
            shape(1, 16),
            jax.ShapeDtypeStruct((Q, 64, 128), jnp.bfloat16),
            shape(Q, 8, 8, 128),
        ),
        [HBM_SPEC] * 7,
        [pltpu.SMEM((2, 3), jnp.int32), pltpu.SemaphoreType.DMA((7,))],
        *(
            pltpu.with_memory_space_constraint(a, pltpu.HBM)
            for a in (*flat[:2], accel_table[0], *flat[2:], f_zero, adjoint)
        ),
    )
    to_b, to_a = call(
        pack_kernel,
        "pack_faces",
        (shape(B_ROWS, 8, 128), shape(ROWS, 8, 128)),
        [VMEM_SPEC] * 4,
        [row],
        f_zero,
        adjoint,
        accel,
        blocks,
    )
    from_b = send(to_b, "beyond")
    from_a = send(to_a, "chip")
    within = send(blocks, "within")
    across = send(blocks, "across")
    g_one, mom, solid, sums, turned_sums = call(
        sens_kernel,
        "sensitivity",
        (
            shape(Q, 12, 8, 128),
            shape(4, 8, 8, 128),
            shape(8, 128),
            shape(1, 128),
            shape(1, 128),
        ),
        [VMEM_SPEC] * 8,
        [
            pltpu.VMEM((Q, 14, 8, 128), F32),
            pltpu.VMEM((len(PAIRS), 12, 8, 128), F32),
            row,
            row,
        ],
        accel,
        f_zero,
        adjoint,
        from_a,
        from_b,
        blocks,
        within,
        across,
    )
    outside = send(turned_sums, "ends")
    payload = call(
        share_kernel, "share", shape(GROUP * cases, 1, 128), [VMEM_SPEC] * 2, [], sums, outside
    )
    payload, g_one = lax.optimization_barrier((payload, g_one))
    shared = lax.all_to_all(payload, axes, 0, 0, axis_index_groups=groups, tiled=True)
    start = call(
        start_kernel,
        "adjoint_start",
        shape(Q, 8, 8, 128),
        [VMEM_SPEC] * 4,
        [],
        accel,
        solid,
        g_one,
        mom,
    )
    small = shape(1, 16)
    updated = call(
        functools.partial(update_kernel, cases),
        "update",
        (small, small, small),
        [VMEM_SPEC] * 5,
        [],
        shared,
        *kept,
    )
    return (start[None],) + tuple(u.reshape(1, 1, 16) for u in updated)


def solution(mesh):
    placed = (
        P("case", None, "tile", None, None),
        P("case", None, "tile", None, None),
        P("case", None, None),
        P("tile", None, None),
        P("tile", None, None),
        P("tile", None, None),
        P("tile", None, None),
    )
    return jax.shard_map(
        functools.partial(body, mesh.shape["tile"], mesh.shape["case"]),
        mesh=mesh,
        in_specs=placed,
        out_specs=(
            P("case", None, "tile", None, None),
            P("tile", None, None),
            P("tile", None, None),
            P("tile", None, None),
        ),
        check_vma=False,
    )
```

```python
import functools

import jax
import jax.numpy as jnp
import numpy as np
from jax import lax
from jax.experimental import pallas as pl
from jax.experimental.pallas import tpu as pltpu
from jax.sharding import PartitionSpec as P

Q = 19
BLOCK = 8
VELOCITIES = [
    (0, 0, 0),
    (1, 0, 0),
    (-1, 0, 0),
    (0, 1, 0),
    (0, -1, 0),
    (0, 0, 1),
    (0, 0, -1),
    (1, 1, 0),
    (-1, -1, 0),
    (1, -1, 0),
    (-1, 1, 0),
    (1, 0, 1),
    (-1, 0, -1),
    (1, 0, -1),
    (-1, 0, 1),
    (0, 1, 1),
    (0, -1, -1),
    (0, 1, -1),
    (0, -1, 1),
]
W_REST, W_AXIS, W_DIAG = 1.0 / 3.0, 1.0 / 18.0, 1.0 / 36.0
RELAX_RATE = 0.9
SOLID_MAX = 0.5
FACE_WEIGHT = 0.5
ACCEL_SCALE = 400.0
BETA_ONE = 0.9
BETA_TWO = 0.999
LEARN_RATE = 0.2
ADAM_EPS = 1e-08
BIAS_ONE = 1.0 - 0.9**10
BIAS_TWO = 1.0 - 0.999**10

PAIRS = tuple(range(1, Q, 2))
Q_ZERO = [q for q in range(Q) if VELOCITIES[q][0] == 0]
Q_PLUS = [q for q in range(Q) if VELOCITIES[q][0] == 1]
Q_MINUS = [q for q in range(Q) if VELOCITIES[q][0] == -1]
ROW_MOMENTS = 2 * len(Q_PLUS)
ROW_TURNED = ROW_MOMENTS + 4
ROW_LEVEL = ROW_TURNED + 9
ROW_ADJ = ROW_LEVEL + 6
ROW_ADJ_FAR = ROW_ADJ + len(Q_PLUS)
ROW_BLOCKS = ROW_ADJ_FAR + len(Q_PLUS)
ROWS = ROW_BLOCKS + 1
B_ROWS = ROWS + 1
Z_MOTIONS = (0, 1, -1)
RUN = 16
FORWARD_UNROLL = 2
BACKWARD_UNROLL = 6
GROUP = 8
OFFSET = 7


def shift_yz(value, vel_id, direction):
    _, shift_y, shift_z = VELOCITIES[vel_id]
    if shift_y:
        value = pltpu.roll(value, (direction * shift_y) % 8, 0)
    if shift_z:
        value = pltpu.roll(value, (direction * shift_z) % 128, 1)
    return value


def add_signed(total, value, sign):
    if sign == 0:
        return total
    return total + value if sign > 0 else total - value


def along(vector, vel_id):
    total = None
    for part, sign in zip(vector, VELOCITIES[vel_id]):
        if sign == 0:
            continue
        if total is None:
            total = part if sign > 0 else -part
        else:
            total = total + part if sign > 0 else total - part
    return total


def weight(pair):
    return W_AXIS if pair < 7 else W_DIAG


def moments(f):
    plus = {p: f[p] + f[p + 1] for p in PAIRS}
    minus = {p: f[p] - f[p + 1] for p in PAIRS}
    density = f[0]
    for p in PAIRS:
        density = density + plus[p]
    momentum = []
    for axis in range(3):
        total = None
        for p in PAIRS:
            sign = VELOCITIES[p][axis]
            if sign == 0:
                continue
            if total is None:
                total = minus[p]
            else:
                total = total + minus[p] if sign > 0 else total - minus[p]
        momentum.append(total)
    return density, momentum, plus, minus


def odd_parts(density, momentum, minus, accel):
    flow = [3.0 * RELAX_RATE * m + (3.0 * a) * density for m, a in zip(momentum, accel)]
    return {
        p: (1.0 - RELAX_RATE) * minus[p] + (2.0 * weight(p)) * along(flow, p) for p in PAIRS
    }


def collide(f, solid, accel):
    density, momentum, plus, minus = moments(f)
    odd = odd_parts(density, momentum, minus, accel)
    inverse = 1.0 / density
    velocity = [m * inverse for m in momentum]
    speed_sq = sum(m * u for m, u in zip(momentum, velocity))
    base = RELAX_RATE * (density - 1.5 * speed_sq)
    gray = {0: (1.0 - RELAX_RATE) * f[0] + W_REST * base}
    bent = 0.5 - solid
    for p in PAIRS:
        project = along(velocity, p)
        even = 0.5 * (1.0 - RELAX_RATE) * plus[p] + weight(p) * (
            base + (4.5 * RELAX_RATE) * density * (project * project)
        )
        turned = bent * odd[p]
        gray[p] = even + turned
        gray[p + 1] = even - turned
    return gray, odd


def adjoint_parts(f_moments, level, first, second, accel):
    density, momentum = f_moments
    inverse = 1.0 / density
    velocity = [m * inverse for m in momentum]
    bent = [
        sum(second[(min(i, j), max(i, j))] * velocity[j] for j in range(3)) for i in range(3)
    ]
    pull = [
        RELAX_RATE * (3.0 * first[i] + 9.0 * bent[i] - (3.0 * level) * velocity[i])
        for i in range(3)
    ]
    speed_sq = sum(u * u for u in velocity)
    rest = RELAX_RATE * (
        level * (1.0 + 1.5 * speed_sq) - 4.5 * sum(b * u for b, u in zip(bent, velocity))
    )
    return rest + 3.0 * sum(a * b for a, b in zip(accel, first)), pull


def pair_adjoint(plus, minus, rest, pull, pair):
    even = 0.5 * (1.0 - RELAX_RATE) * plus + rest
    odd = 0.5 * (1.0 - RELAX_RATE) * minus + along(pull, pair)
    return even + odd, even - odd


def still_sums(plus, minus, rest):
    diag = W_DIAG * (plus[15] + plus[17])
    axis_y, axis_z = W_AXIS * plus[3], W_AXIS * plus[5]
    return (
        W_REST * rest + axis_y + axis_z + diag,
        axis_y + diag,
        axis_z + diag,
        W_DIAG * (plus[15] - plus[17]),
        W_AXIS * minus[3] + W_DIAG * (minus[15] + minus[17]),
        W_AXIS * minus[5] + W_DIAG * (minus[15] - minus[17]),
    )


def all_sums(still, plus, minus, fluid):
    level, yy, zz, yz, y, z = still
    diag_xy, diag_xz = W_DIAG * (plus[7] + plus[9]), W_DIAG * (plus[11] + plus[13])
    axis_x = W_AXIS * plus[1]
    second = {
        (0, 0): axis_x + diag_xy + diag_xz,
        (1, 1): yy + diag_xy,
        (2, 2): zz + diag_xz,
        (0, 1): W_DIAG * (plus[7] - plus[9]),
        (0, 2): W_DIAG * (plus[11] - plus[13]),
        (1, 2): yz,
    }
    first = [
        fluid * (W_AXIS * minus[1] + W_DIAG * (minus[7] + minus[9] + minus[11] + minus[13])),
        fluid * (y + W_DIAG * (minus[7] - minus[9])),
        fluid * (z + W_DIAG * (minus[11] - minus[13])),
    ]
    return level + axis_x + diag_xy + diag_xz, first, second


def pair_sums(g, pairs):
    return {p: g[p] + g[p + 1] for p in pairs}, {p: g[p] - g[p + 1] for p in pairs}


def collide_adjoint(f_moments, g, solid, accel):
    plus, minus = pair_sums(g, PAIRS)
    fluid = 1.0 - 2.0 * solid
    sums = all_sums(still_sums(plus, minus, g[0]), plus, minus, fluid)
    rest, pull = adjoint_parts(f_moments, *sums, accel)
    out = {0: (1.0 - RELAX_RATE) * g[0] + rest}
    for p in PAIRS:
        out[p], out[p + 1] = pair_adjoint(plus[p], fluid * minus[p], rest, pull, p)
    return out


def sens_terms(g, odd):
    return sum((g[p + 1] - g[p]) * odd[p] for p in PAIRS)


def lanes():
    return lax.broadcasted_iota(jnp.int32, (8, 128), 1)


def read_accel(accel_ref, turn):
    return [accel_ref[turn, axis] for axis in range(3)]


def is_even():
    return lax.axis_index("tile") & 1 == 0


def spread(row, blocks):
    row[...] = jnp.zeros_like(row)
    row[0:1, 0:16] = blocks
    wide = jnp.take_along_axis(row[...], lanes() // BLOCK, axis=1)
    return jnp.broadcast_to(wide[0:1], (8, 128))


def smooth(beside, grid):
    around = beside + 2.0 * grid + pltpu.roll(grid, 8, 1) + pltpu.roll(grid, 120, 1)
    return (grid + FACE_WEIGHT * around) * (1.0 / (1.0 + 6.0 * FACE_WEIGHT))


def read_layer(f_ref, q, x):
    two = f_ref[q, 16 * (x // 2) : 16 * (x // 2) + 16, :].astype(jnp.float32)
    return two[8:16] if x % 2 else two[0:8]


def load_kernel(
    design_hbm,
    mask_hbm,
    accel_hbm,
    first_hbm,
    second_hbm,
    f_hbm,
    adj_hbm,
    blocks_out,
    accel_out,
    design_out,
    mask_out,
    first_out,
    second_out,
    f_out,
    adj_out,
    table,
    sems,
):
    copies = [
        pltpu.make_async_copy(source, target, sems.at[i])
        for i, (source, target) in enumerate(
            (
                (design_hbm, design_out),
                (mask_hbm, mask_out),
                (accel_hbm, table),
                (first_hbm, first_out),
                (second_hbm, second_out),
                (f_hbm, f_out),
                (adj_hbm, adj_out),
            )
        )
    ]
    for copy in copies:
        copy.start()
    for copy in copies[:5]:
        copy.wait()
    blocks_out[...] = design_out[...] * mask_out[...].astype(jnp.float32)
    for turn in range(2):
        for axis in range(3):
            value = table[turn, axis].astype(jnp.float32) * (1.0 / ACCEL_SCALE)
            accel_out[turn, axis] = jnp.full((8, 128), value, jnp.float32)
    for copy in copies[5:]:
        copy.wait()


def pack(f_ref, adj_ref, out, high, blocks, accel):
    near, far = (7, 6) if high else (0, 1)
    onward, back = (Q_PLUS, Q_MINUS) if high else (Q_MINUS, Q_PLUS)
    post, _ = collide([read_layer(f_ref, q, near) for q in range(Q)], 0.0, accel)
    behind, _ = collide([read_layer(f_ref, q, far) for q in range(Q)], 0.0, accel)
    for i, p in enumerate(Q_PLUS):
        out[2 * i] = post[p]
        out[2 * i + 1] = post[p + 1]
    total = [0.0] * 4
    turned_away = {motion: [0.0] * 3 for motion in Z_MOTIONS}
    for q in Q_ZERO + onward:
        layer = behind if q in onward else post
        value = shift_yz(layer[q], q, 1)
        total = [
            add_signed(kept, value, sign) for kept, sign in zip(total, (1,) + VELOCITIES[q])
        ]
        if q:
            value = shift_yz(layer[q] - layer[q + 1 if q % 2 else q - 1], q, 1)
            group = turned_away[VELOCITIES[q][2]]
            signs = (1,) + VELOCITIES[q][:2]
            turned_away[VELOCITIES[q][2]] = [
                add_signed(kept, value, sign) for kept, sign in zip(group, signs)
            ]
    for i in range(4):
        out[ROW_MOMENTS + i] = total[i]
    for k, motion in enumerate(Z_MOTIONS):
        for i in range(3):
            out[ROW_TURNED + 3 * k + i] = turned_away[motion][i]
    g = {q: shift_yz(adj_ref[q, near], q, -1) for q in Q_ZERO + back}
    plus, minus = pair_sums(g, [p for p in PAIRS if p in Q_ZERO])
    for i, value in enumerate(still_sums(plus, minus, g[0])):
        out[ROW_LEVEL + i] = value
    for i, q in enumerate(back):
        out[ROW_ADJ + i] = g[q]
        out[ROW_ADJ_FAR + i] = shift_yz(adj_ref[q, far], q, -1)
    out[ROW_BLOCKS] = blocks


def pack_kernel(f_ref, adj_ref, accel_ref, own_ref, to_b, to_a, row):
    accel = read_accel(accel_ref, 0)
    blocks = spread(row, own_ref[...])
    for r in range(ROWS, B_ROWS):
        to_b[r] = jnp.zeros((8, 128), jnp.float32)

    def both(low, high):
        pack(f_ref, adj_ref, low, False, blocks, accel)
        pack(f_ref, adj_ref, high, True, blocks, accel)

    even = is_even()
    pl.when(even)(lambda: both(to_b, to_a))
    pl.when(jnp.logical_not(even))(lambda: both(to_a, to_b))


def boundary(low, message, solid, solid_own, f_next, adj_ref, accel):
    inward, outward = (Q_PLUS, Q_MINUS) if low else (Q_MINUS, Q_PLUS)
    beside, face, layer, behind = (2, 3, 0, 1) if low else (11, 10, 7, 6)
    first = 0 if low else 1

    part = [message[ROW_MOMENTS + i] for i in range(4)]
    for k, motion in enumerate(Z_MOTIONS):
        moved = pltpu.roll(solid, motion % 128, 1) if motion else solid
        away = [moved * message[ROW_TURNED + 3 * k + i] for i in range(3)]
        part = [a - b for a, b in zip(part, away)] + [add_signed(part[3], away[0], -motion)]
    for q in outward:
        value = f_next[q, beside]
        part = [add_signed(kept, value, sign) for kept, sign in zip(part, (1,) + VELOCITIES[q])]
    g = {q: message[ROW_ADJ_FAR + i] for i, q in enumerate(outward)}
    g.update({q: shift_yz(adj_ref[q, layer], q, -1) for q in inward})
    plus, minus = pair_sums(g, Q_PLUS)
    fluid = 1.0 - 2.0 * solid
    still = [message[ROW_LEVEL + i] for i in range(6)]
    rest, pull = adjoint_parts((part[0], part[1:]), *all_sums(still, plus, minus, fluid), accel)
    adj_beside = {}
    for p in Q_PLUS:
        both = pair_adjoint(plus[p], fluid * minus[p], rest, pull, p)
        q = p + 1 if low else p
        adj_beside[q] = shift_yz(both[q - p], q, -1)

    f = {q: f_next[q, face] for q in Q_ZERO + outward}
    for i, q in enumerate(inward):
        value, opposite = message[2 * i + first], message[2 * i + 1 - first]
        f[q] = shift_yz(value + solid * (opposite - value), q, 1)
    g = {q: message[ROW_ADJ + i] for i, q in enumerate(outward)}
    g.update({q: shift_yz(adj_ref[q, layer], q, -1) for q in Q_ZERO})
    g.update({q: shift_yz(adj_ref[q, behind], q, -1) for q in inward})
    density, momentum, _, minus = moments(f)
    odd = odd_parts(density, momentum, minus, accel)
    adj_face = collide_adjoint((density, momentum), g, solid_own, accel)
    adj_face = {q: shift_yz(adj_face[q], q, -1) for q in Q_ZERO + outward}
    return adj_beside, adj_face, sens_terms(g, odd)


def boundary_sens(low, adj_beside, adj_face, odd_ref):
    face, behind = (2, 3) if low else (9, 8)
    total = 0.0
    for q in Q_ZERO:
        if q:
            total = total + adj_face[q] * turned(odd_ref, face, q)
    for q in Q_MINUS if low else Q_PLUS:
        total = total + adj_beside[q] * turned(odd_ref, face, q)
        total = total + adj_face[q] * turned(odd_ref, behind, q)
    return total


def interior_kernel(
    accel_ref,
    f_ref,
    adj_ref,
    from_a,
    from_b,
    own_ref,
    g_out,
    f_next,
    odd_ext,
    mom_out,
    solid_out,
    total_out,
    row,
):
    accel_first = read_accel(accel_ref, 0)
    accel_second = read_accel(accel_ref, 1)
    own = spread(row, own_ref[...])
    solid_own = SOLID_MAX * smooth(from_a[ROW_BLOCKS] + from_b[ROW_BLOCKS], own)
    solid_out[...] = solid_own

    def forward(k, _):
        for half in range(2):
            e = 2 * k + 2 + half
            f = [
                f_ref[q, pl.ds(pl.multiple_of(16 * k, 16), 16), :].astype(jnp.float32)[
                    8 * half : 8 * half + 8
                ]
                for q in range(Q)
            ]
            gray, odd = collide(f, solid_own, accel_first)
            density, momentum, _, _ = moments(f)
            for i, part in enumerate([density] + momentum):
                mom_out[i, e - 2] = part
            for q in range(Q):
                f_next[q, e + 1 + VELOCITIES[q][0]] = shift_yz(gray[q], q, 1)
            for i, p in enumerate(PAIRS):
                odd_ext[i, e] = odd[p]
        return 0

    lax.fori_loop(0, 4, forward, 0, unroll=FORWARD_UNROLL)

    def backward(e, total):
        f = [f_next[q, e + 1] for q in range(Q)]
        g = [shift_yz(adj_ref[q, e - 2 + VELOCITIES[q][0]], q, -1) for q in range(Q)]
        density, momentum, _, minus = moments(f)
        odd = odd_parts(density, momentum, minus, accel_second)
        total = total + sens_terms(g, odd)
        adjoint = collide_adjoint((density, momentum), g, solid_own, accel_second)
        for q in range(Q):
            to = e - VELOCITIES[q][0]
            value = shift_yz(adjoint[q], q, -1)
            g_out[q, to] = value
            if q:
                total = total + value * turned(odd_ext, to, q)
        return total

    total_out[...] = lax.fori_loop(
        3, 9, backward, jnp.zeros((8, 128), jnp.float32), unroll=BACKWARD_UNROLL
    )


def sides_kernel(
    accel_ref,
    adj_ref,
    from_a,
    from_b,
    own_ref,
    solid_ref,
    f_next,
    odd_ext,
    total_ref,
    across_ref,
    within_ref,
    low_out,
    high_out,
    sums_out,
    row,
    past_row,
):
    accel_second = read_accel(accel_ref, 1)
    own = spread(row, own_ref[...])
    row[...] = total_ref[...]
    odd_chip = lax.axis_index("tile") & 2 == 2

    def side(low, message):
        outward = Q_MINUS if low else Q_PLUS
        past = jnp.where(odd_chip == low, within_ref[...], across_ref[...])
        solid = SOLID_MAX * smooth(own + spread(past_row, past), message[ROW_BLOCKS])
        adj_beside, adj_face, sens = boundary(
            low, message, solid, solid_ref[...], f_next, adj_ref, accel_second
        )
        out = low_out if low else high_out
        for i, q in enumerate(Q_ZERO):
            out[i] = adj_face[q]
        for i, q in enumerate(outward):
            out[len(Q_ZERO) + i] = adj_beside[q]
            out[len(Q_ZERO) + len(outward) + i] = adj_face[q]
        row[...] += sens + boundary_sens(low, adj_beside, adj_face, odd_ext)

    def both(low, high):
        side(True, low)
        side(False, high)

    even = is_even()
    pl.when(even)(lambda: both(from_b, from_a))
    pl.when(jnp.logical_not(even))(lambda: both(from_a, from_b))

    total = jnp.broadcast_to(jnp.sum(row[...], axis=0, keepdims=True), (8, 128))
    for step in (1, 2, 4):
        total = total + pltpu.roll(total, 128 - step, 1)
    total = jnp.where(lanes() % BLOCK == 0, total, 0.0)
    sums_out[...] = jnp.broadcast_to(total[0:1][None], sums_out.shape)


def turned(odd_ref, layer, q):
    return -odd_ref[q // 2, layer] if q % 2 else odd_ref[q // 2 - 1, layer]


def start_kernel(accel_ref, solid_ref, g_ref, mom_ref, low_ref, high_ref, out_ref):
    accel = read_accel(accel_ref, 0)
    solid = solid_ref[...]

    def layer(x, changed):
        g = {q: g_ref[q, x + 2] for q in range(Q)}
        g.update(changed)
        momentum = [mom_ref[1 + axis, x] for axis in range(3)]
        adjoint = collide_adjoint((mom_ref[0, x], momentum), g, solid, accel)
        for q in range(Q):
            out_ref[q, x] = adjoint[q]

    def inner(x, _):
        layer(x, {})
        return 0

    lax.fori_loop(2, 6, inner, 0)
    for side, face, behind, outward in ((low_ref, 0, 1, Q_MINUS), (high_ref, 7, 6, Q_PLUS)):
        layer(face, {q: side[i] for i, q in enumerate(Q_ZERO + outward)})
        first = len(Q_ZERO) + len(outward)
        layer(behind, {q: side[first + i] for i, q in enumerate(outward)})


def group_order(cases):
    places = tuple(range(1, GROUP)) + (0,)
    listed = [(place, case) for half in (0, 1) for place in places for case in range(half, cases, 2)]
    listed.remove((0, 0))
    return [(0, 0)] + listed


def place_in_group():
    return (lax.axis_index("tile") - OFFSET) & (GROUP - 1)


def tile_total(sums_ref, cases, tile):
    ranks = [rank for rank, (place, _) in enumerate(group_order(cases)) if place == tile]
    return sum(sums_ref[rank] for rank in ranks)


def end_kernel(cases, sums_ref, out):
    first, last = tile_total(sums_ref, cases, 0), tile_total(sums_ref, cases, GROUP - 1)
    out[...] = jnp.where(place_in_group() == 0, first, last)


def update_kernel(
    cases,
    sums_ref,
    outside_ref,
    design_ref,
    mask_ref,
    first_ref,
    second_ref,
    design_out,
    first_out,
    second_out,
):
    place = place_in_group()
    totals = [tile_total(sums_ref, cases, tile) for tile in range(GROUP)]
    line = [outside_ref[...]] + totals + [outside_ref[...]]
    line = [jnp.broadcast_to(row, (8, 128)) for row in line]

    def pick(shift):
        value = line[shift]
        for k in range(1, GROUP):
            value = jnp.where(place == k, line[k + shift], value)
        return value

    gradient = SOLID_MAX * smooth(pick(0) + pick(2), pick(1))
    spots = jnp.minimum(lanes() * BLOCK, 127)
    gradient = jnp.take_along_axis(gradient, spots, axis=1)[0:1, 0:16]
    gradient = mask_ref[...].astype(jnp.float32) * gradient
    first = BETA_ONE * first_ref[...] + (1.0 - BETA_ONE) * gradient
    second = BETA_TWO * second_ref[...] + (1.0 - BETA_TWO) * gradient * gradient
    stepped = design_ref[...] - LEARN_RATE * (first * (1.0 / BIAS_ONE)) / (
        jnp.sqrt(second * (1.0 / BIAS_TWO)) + ADAM_EPS
    )
    design_out[...] = jnp.clip(stepped, 0.0, 1.0)
    first_out[...] = first
    second_out[...] = second


def tables(tiles, cases):
    run = RUN if tiles % RUN == 0 else tiles

    def device(tile, case):
        return (tile % tiles) * cases + case

    def near(tile, step, case):
        target = tile + step
        crossed = (target // run) != (tile // run)
        return device(target, case ^ 1 if crossed else case)

    found = {name: [] for name in ("chip", "beyond", "across", "within", "ends")}
    for tile in range(tiles):
        step = 1 if tile % 2 else -1
        for case in range(cases):
            here = device(tile, case)
            found["chip"].append((here, device(tile ^ 1, case)))
            found["beyond"].append((here, device(tile + step, case)))
            odd_chip = (tile // 2) % 2
            found["across"].append((here, near(tile, 2 if odd_chip else -2, case)))
            found["within"].append((here, near(tile, -2 if odd_chip else 2, case)))
            place = (tile - OFFSET) % GROUP
            if place == 0:
                found["ends"].append((here, device(tile - 1, case)))
            if place == GROUP - 1:
                found["ends"].append((here, device(tile + 1, case)))
    groups = [
        [device(OFFSET + g * GROUP + place, case) for place, case in group_order(cases)]
        for g in range(tiles // GROUP)
    ]
    return found, groups


VMEM_SPEC = pl.BlockSpec(memory_space=pltpu.VMEM)
HBM_SPEC = pl.BlockSpec(memory_space=pltpu.HBM)
F32 = jnp.float32


def body(
    tiles,
    cases,
    checkpoint,
    adjoint_field,
    accel_table,
    design,
    design_mask,
    first_moment,
    second_moment,
):
    axes = ("tile", "case")
    pairs, groups = tables(tiles, cases)
    f_zero = checkpoint.reshape(Q, 64, 128)
    adjoint = adjoint_field[0]
    flat = [a.reshape(1, 16) for a in (design, design_mask, first_moment, second_moment)]
    params = pltpu.CompilerParams(vmem_limit_bytes=32 * 1024 * 1024)

    def send(value, name):
        return lax.ppermute(value, axes, pairs[name])

    def call(kernel, name, out_shape, in_specs, scratch, *args):
        many = isinstance(out_shape, tuple)
        return pl.pallas_call(
            kernel,
            out_shape=out_shape,
            in_specs=in_specs,
            out_specs=[VMEM_SPEC] * len(out_shape) if many else VMEM_SPEC,
            scratch_shapes=scratch,
            compiler_params=params,
            name=name,
        )(*args)

    def shape(*dims):
        return jax.ShapeDtypeStruct(dims, F32)

    row = pltpu.VMEM((8, 128), F32)
    blocks, accel, *kept, f_zero, adjoint = call(
        load_kernel,
        "load",
        (
            shape(1, 16),
            shape(2, 3, 8, 128),
            shape(1, 16),
            jax.ShapeDtypeStruct((1, 16), jnp.int32),
            shape(1, 16),
            shape(1, 16),
            jax.ShapeDtypeStruct((Q, 64, 128), jnp.bfloat16),
            shape(Q, 8, 8, 128),
        ),
        [HBM_SPEC] * 7,
        [pltpu.SMEM((2, 3), jnp.int32), pltpu.SemaphoreType.DMA((7,))],
        *(
            pltpu.with_memory_space_constraint(a, pltpu.HBM)
            for a in (*flat[:2], accel_table[0], *flat[2:], f_zero, adjoint)
        ),
    )
    to_b, to_a = call(
        pack_kernel,
        "pack_faces",
        (shape(B_ROWS, 8, 128), shape(ROWS, 8, 128)),
        [VMEM_SPEC] * 4,
        [row],
        f_zero,
        adjoint,
        accel,
        blocks,
    )
    from_b = send(to_b, "beyond")
    from_a = send(to_a, "chip")
    within = send(blocks, "within")
    across = send(blocks, "across")
    g_one, f_next, odd, mom, solid, total = call(
        interior_kernel,
        "interior",
        (
            shape(Q, 12, 8, 128),
            shape(Q, 14, 8, 128),
            shape(len(PAIRS), 12, 8, 128),
            shape(4, 8, 8, 128),
            shape(8, 128),
            shape(8, 128),
        ),
        [VMEM_SPEC] * 6,
        [row],
        accel,
        f_zero,
        adjoint,
        from_a,
        from_b,
        blocks,
    )
    face = shape(len(Q_ZERO) + 2 * len(Q_PLUS), 8, 128)
    low, high, sums = call(
        sides_kernel,
        "sides",
        (face, face, shape(GROUP * cases, 1, 128)),
        [VMEM_SPEC] * 11,
        [row, row],
        accel,
        adjoint,
        from_a,
        from_b,
        blocks,
        solid,
        f_next,
        odd,
        total,
        across,
        within,
    )
    sums, low = lax.optimization_barrier((sums, low))
    shared = lax.all_to_all(sums, axes, 0, 0, axis_index_groups=groups, tiled=True)
    start = call(
        start_kernel,
        "adjoint_start",
        shape(Q, 8, 8, 128),
        [VMEM_SPEC] * 6,
        [],
        accel,
        solid,
        g_one,
        mom,
        low,
        high,
    )
    ends = call(
        functools.partial(end_kernel, cases),
        "group_end",
        shape(1, 128),
        [VMEM_SPEC],
        [],
        shared,
    )
    ends, start = lax.optimization_barrier((ends, start))
    outside = send(ends, "ends")
    small = shape(1, 16)
    updated = call(
        functools.partial(update_kernel, cases),
        "update",
        (small, small, small),
        [VMEM_SPEC] * 6,
        [],
        shared,
        outside,
        *kept,
    )
    return (start[None],) + tuple(u.reshape(1, 1, 16) for u in updated)


def solution(mesh):
    placed = (
        P("case", None, "tile", None, None),
        P("case", None, "tile", None, None),
        P("case", None, None),
        P("tile", None, None),
        P("tile", None, None),
        P("tile", None, None),
        P("tile", None, None),
    )
    return jax.shard_map(
        functools.partial(body, mesh.shape["tile"], mesh.shape["case"]),
        mesh=mesh,
        in_specs=placed,
        out_specs=(
            P("case", None, "tile", None, None),
            P("tile", None, None),
            P("tile", None, None),
            P("tile", None, None),
        ),
        check_vma=False,
    )
```

```python
import functools

import jax
import jax.numpy as jnp
import numpy as np
from jax import lax
from jax.experimental import pallas as pl
from jax.experimental.pallas import tpu as pltpu
from jax.sharding import PartitionSpec as P

Q = 19
BLOCK = 8
VELOCITIES = [
    (0, 0, 0),
    (1, 0, 0),
    (-1, 0, 0),
    (0, 1, 0),
    (0, -1, 0),
    (0, 0, 1),
    (0, 0, -1),
    (1, 1, 0),
    (-1, -1, 0),
    (1, -1, 0),
    (-1, 1, 0),
    (1, 0, 1),
    (-1, 0, -1),
    (1, 0, -1),
    (-1, 0, 1),
    (0, 1, 1),
    (0, -1, -1),
    (0, 1, -1),
    (0, -1, 1),
]
W_REST, W_AXIS, W_DIAG = 1.0 / 3.0, 1.0 / 18.0, 1.0 / 36.0
RELAX_RATE = 0.9
SOLID_MAX = 0.5
FACE_WEIGHT = 0.5
ACCEL_SCALE = 400.0
BETA_ONE = 0.9
BETA_TWO = 0.999
LEARN_RATE = 0.2
ADAM_EPS = 1e-08
BIAS_ONE = 1.0 - 0.9**10
BIAS_TWO = 1.0 - 0.999**10

PAIRS = tuple(range(1, Q, 2))
Q_ZERO = [q for q in range(Q) if VELOCITIES[q][0] == 0]
Q_PLUS = [q for q in range(Q) if VELOCITIES[q][0] == 1]
Q_MINUS = [q for q in range(Q) if VELOCITIES[q][0] == -1]
ROW_MOMENTS = 2 * len(Q_PLUS)
ROW_TURNED = ROW_MOMENTS + 4
ROW_LEVEL = ROW_TURNED + 9
ROW_ADJ = ROW_LEVEL + 6
ROW_ADJ_FAR = ROW_ADJ + len(Q_PLUS)
ROW_BLOCKS = ROW_ADJ_FAR + len(Q_PLUS)
ROWS = ROW_BLOCKS + 1
B_ROWS = ROWS + 1
Z_MOTIONS = (0, 1, -1)
RUN = 16
FORWARD_UNROLL = 2
BACKWARD_UNROLL = 6
GROUP = 8
OFFSET = 7


def shift_yz(value, vel_id, direction):
    _, shift_y, shift_z = VELOCITIES[vel_id]
    if shift_y:
        value = pltpu.roll(value, (direction * shift_y) % 8, 0)
    if shift_z:
        value = pltpu.roll(value, (direction * shift_z) % 128, 1)
    return value


def add_signed(total, value, sign):
    if sign == 0:
        return total
    return total + value if sign > 0 else total - value


def along(vector, vel_id):
    total = None
    for part, sign in zip(vector, VELOCITIES[vel_id]):
        if sign == 0:
            continue
        if total is None:
            total = part if sign > 0 else -part
        else:
            total = total + part if sign > 0 else total - part
    return total


def weight(pair):
    return W_AXIS if pair < 7 else W_DIAG


def moments(f):
    plus = {p: f[p] + f[p + 1] for p in PAIRS}
    minus = {p: f[p] - f[p + 1] for p in PAIRS}
    density = f[0]
    for p in PAIRS:
        density = density + plus[p]
    momentum = []
    for axis in range(3):
        total = None
        for p in PAIRS:
            sign = VELOCITIES[p][axis]
            if sign == 0:
                continue
            if total is None:
                total = minus[p]
            else:
                total = total + minus[p] if sign > 0 else total - minus[p]
        momentum.append(total)
    return density, momentum, plus, minus


def odd_parts(density, momentum, minus, accel):
    flow = [3.0 * RELAX_RATE * m + (3.0 * a) * density for m, a in zip(momentum, accel)]
    return {
        p: (1.0 - RELAX_RATE) * minus[p] + (2.0 * weight(p)) * along(flow, p) for p in PAIRS
    }


def collide(f, solid, accel):
    density, momentum, plus, minus = moments(f)
    odd = odd_parts(density, momentum, minus, accel)
    inverse = 1.0 / density
    velocity = [m * inverse for m in momentum]
    speed_sq = sum(m * u for m, u in zip(momentum, velocity))
    base = RELAX_RATE * (density - 1.5 * speed_sq)
    gray = {0: (1.0 - RELAX_RATE) * f[0] + W_REST * base}
    bent = 0.5 - solid
    for p in PAIRS:
        project = along(velocity, p)
        even = 0.5 * (1.0 - RELAX_RATE) * plus[p] + weight(p) * (
            base + (4.5 * RELAX_RATE) * density * (project * project)
        )
        turned = bent * odd[p]
        gray[p] = even + turned
        gray[p + 1] = even - turned
    return gray, odd


def adjoint_parts(f_moments, level, first, second, accel):
    density, momentum = f_moments
    inverse = 1.0 / density
    velocity = [m * inverse for m in momentum]
    bent = [
        sum(second[(min(i, j), max(i, j))] * velocity[j] for j in range(3)) for i in range(3)
    ]
    pull = [
        RELAX_RATE * (3.0 * first[i] + 9.0 * bent[i] - (3.0 * level) * velocity[i])
        for i in range(3)
    ]
    speed_sq = sum(u * u for u in velocity)
    rest = RELAX_RATE * (
        level * (1.0 + 1.5 * speed_sq) - 4.5 * sum(b * u for b, u in zip(bent, velocity))
    )
    return rest + 3.0 * sum(a * b for a, b in zip(accel, first)), pull


def pair_adjoint(plus, minus, rest, pull, pair):
    even = 0.5 * (1.0 - RELAX_RATE) * plus + rest
    odd = 0.5 * (1.0 - RELAX_RATE) * minus + along(pull, pair)
    return even + odd, even - odd


def still_sums(plus, minus, rest):
    diag = W_DIAG * (plus[15] + plus[17])
    axis_y, axis_z = W_AXIS * plus[3], W_AXIS * plus[5]
    return (
        W_REST * rest + axis_y + axis_z + diag,
        axis_y + diag,
        axis_z + diag,
        W_DIAG * (plus[15] - plus[17]),
        W_AXIS * minus[3] + W_DIAG * (minus[15] + minus[17]),
        W_AXIS * minus[5] + W_DIAG * (minus[15] - minus[17]),
    )


def all_sums(still, plus, minus, fluid):
    level, yy, zz, yz, y, z = still
    diag_xy, diag_xz = W_DIAG * (plus[7] + plus[9]), W_DIAG * (plus[11] + plus[13])
    axis_x = W_AXIS * plus[1]
    second = {
        (0, 0): axis_x + diag_xy + diag_xz,
        (1, 1): yy + diag_xy,
        (2, 2): zz + diag_xz,
        (0, 1): W_DIAG * (plus[7] - plus[9]),
        (0, 2): W_DIAG * (plus[11] - plus[13]),
        (1, 2): yz,
    }
    first = [
        fluid * (W_AXIS * minus[1] + W_DIAG * (minus[7] + minus[9] + minus[11] + minus[13])),
        fluid * (y + W_DIAG * (minus[7] - minus[9])),
        fluid * (z + W_DIAG * (minus[11] - minus[13])),
    ]
    return level + axis_x + diag_xy + diag_xz, first, second


def pair_sums(g, pairs):
    return {p: g[p] + g[p + 1] for p in pairs}, {p: g[p] - g[p + 1] for p in pairs}


def collide_adjoint(f_moments, g, solid, accel):
    plus, minus = pair_sums(g, PAIRS)
    fluid = 1.0 - 2.0 * solid
    sums = all_sums(still_sums(plus, minus, g[0]), plus, minus, fluid)
    rest, pull = adjoint_parts(f_moments, *sums, accel)
    out = {0: (1.0 - RELAX_RATE) * g[0] + rest}
    for p in PAIRS:
        out[p], out[p + 1] = pair_adjoint(plus[p], fluid * minus[p], rest, pull, p)
    return out


def sens_terms(g, odd):
    return sum((g[p + 1] - g[p]) * odd[p] for p in PAIRS)


def lanes():
    return lax.broadcasted_iota(jnp.int32, (8, 128), 1)


def read_accel(accel_ref, turn):
    return [accel_ref[turn, axis] for axis in range(3)]


def is_even():
    return lax.axis_index("tile") & 1 == 0


def spread(row, blocks):
    row[...] = jnp.zeros_like(row)
    row[0:1, 0:16] = blocks
    wide = jnp.take_along_axis(row[...], lanes() // BLOCK, axis=1)
    return jnp.broadcast_to(wide[0:1], (8, 128))


def smooth(beside, grid):
    around = beside + 2.0 * grid + pltpu.roll(grid, 8, 1) + pltpu.roll(grid, 120, 1)
    return (grid + FACE_WEIGHT * around) * (1.0 / (1.0 + 6.0 * FACE_WEIGHT))


def read_layer(f_ref, q, x):
    two = f_ref[q, 16 * (x // 2) : 16 * (x // 2) + 16, :].astype(jnp.float32)
    return two[8:16] if x % 2 else two[0:8]


def load_kernel(
    design_hbm,
    mask_hbm,
    accel_hbm,
    first_hbm,
    second_hbm,
    f_hbm,
    adj_hbm,
    blocks_out,
    accel_out,
    design_out,
    mask_out,
    first_out,
    second_out,
    f_out,
    adj_out,
    table,
    sems,
):
    copies = [
        pltpu.make_async_copy(source, target, sems.at[i])
        for i, (source, target) in enumerate(
            (
                (design_hbm, design_out),
                (mask_hbm, mask_out),
                (accel_hbm, table),
                (first_hbm, first_out),
                (second_hbm, second_out),
                (f_hbm, f_out),
                (adj_hbm, adj_out),
            )
        )
    ]
    for copy in copies:
        copy.start()
    for copy in copies[:5]:
        copy.wait()
    blocks_out[...] = design_out[...] * mask_out[...].astype(jnp.float32)
    for turn in range(2):
        for axis in range(3):
            value = table[turn, axis].astype(jnp.float32) * (1.0 / ACCEL_SCALE)
            accel_out[turn, axis] = jnp.full((8, 128), value, jnp.float32)
    for copy in copies[5:]:
        copy.wait()


def pack(f_ref, adj_ref, out, high, blocks, accel):
    near, far = (7, 6) if high else (0, 1)
    onward, back = (Q_PLUS, Q_MINUS) if high else (Q_MINUS, Q_PLUS)
    post, _ = collide([read_layer(f_ref, q, near) for q in range(Q)], 0.0, accel)
    behind, _ = collide([read_layer(f_ref, q, far) for q in range(Q)], 0.0, accel)
    for i, p in enumerate(Q_PLUS):
        out[2 * i] = post[p]
        out[2 * i + 1] = post[p + 1]
    total = [0.0] * 4
    turned_away = {motion: [0.0] * 3 for motion in Z_MOTIONS}
    for q in Q_ZERO + onward:
        layer = behind if q in onward else post
        value = shift_yz(layer[q], q, 1)
        total = [
            add_signed(kept, value, sign) for kept, sign in zip(total, (1,) + VELOCITIES[q])
        ]
        if q:
            value = shift_yz(layer[q] - layer[q + 1 if q % 2 else q - 1], q, 1)
            group = turned_away[VELOCITIES[q][2]]
            signs = (1,) + VELOCITIES[q][:2]
            turned_away[VELOCITIES[q][2]] = [
                add_signed(kept, value, sign) for kept, sign in zip(group, signs)
            ]
    for i in range(4):
        out[ROW_MOMENTS + i] = total[i]
    for k, motion in enumerate(Z_MOTIONS):
        for i in range(3):
            out[ROW_TURNED + 3 * k + i] = turned_away[motion][i]
    g = {q: shift_yz(adj_ref[q, near], q, -1) for q in Q_ZERO + back}
    plus, minus = pair_sums(g, [p for p in PAIRS if p in Q_ZERO])
    for i, value in enumerate(still_sums(plus, minus, g[0])):
        out[ROW_LEVEL + i] = value
    for i, q in enumerate(back):
        out[ROW_ADJ + i] = g[q]
        out[ROW_ADJ_FAR + i] = shift_yz(adj_ref[q, far], q, -1)
    out[ROW_BLOCKS] = blocks


def pack_kernel(f_ref, adj_ref, accel_ref, own_ref, to_b, to_a, row):
    accel = read_accel(accel_ref, 0)
    blocks = spread(row, own_ref[...])
    for r in range(ROWS, B_ROWS):
        to_b[r] = jnp.zeros((8, 128), jnp.float32)

    def both(low, high):
        pack(f_ref, adj_ref, low, False, blocks, accel)
        pack(f_ref, adj_ref, high, True, blocks, accel)

    even = is_even()
    pl.when(even)(lambda: both(to_b, to_a))
    pl.when(jnp.logical_not(even))(lambda: both(to_a, to_b))


def boundary(low, message, solid, solid_own, f_next, adj_ref, accel):
    inward, outward = (Q_PLUS, Q_MINUS) if low else (Q_MINUS, Q_PLUS)
    beside, face, layer, behind = (2, 3, 0, 1) if low else (11, 10, 7, 6)
    first = 0 if low else 1

    part = [message[ROW_MOMENTS + i] for i in range(4)]
    for k, motion in enumerate(Z_MOTIONS):
        moved = pltpu.roll(solid, motion % 128, 1) if motion else solid
        away = [moved * message[ROW_TURNED + 3 * k + i] for i in range(3)]
        part = [a - b for a, b in zip(part, away)] + [add_signed(part[3], away[0], -motion)]
    for q in outward:
        value = f_next[q, beside]
        part = [add_signed(kept, value, sign) for kept, sign in zip(part, (1,) + VELOCITIES[q])]
    g = {q: message[ROW_ADJ_FAR + i] for i, q in enumerate(outward)}
    g.update({q: shift_yz(adj_ref[q, layer], q, -1) for q in inward})
    plus, minus = pair_sums(g, Q_PLUS)
    fluid = 1.0 - 2.0 * solid
    still = [message[ROW_LEVEL + i] for i in range(6)]
    rest, pull = adjoint_parts((part[0], part[1:]), *all_sums(still, plus, minus, fluid), accel)
    adj_beside = {}
    for p in Q_PLUS:
        both = pair_adjoint(plus[p], fluid * minus[p], rest, pull, p)
        q = p + 1 if low else p
        adj_beside[q] = shift_yz(both[q - p], q, -1)

    f = {q: f_next[q, face] for q in Q_ZERO + outward}
    for i, q in enumerate(inward):
        value, opposite = message[2 * i + first], message[2 * i + 1 - first]
        f[q] = shift_yz(value + solid * (opposite - value), q, 1)
    g = {q: message[ROW_ADJ + i] for i, q in enumerate(outward)}
    g.update({q: shift_yz(adj_ref[q, layer], q, -1) for q in Q_ZERO})
    g.update({q: shift_yz(adj_ref[q, behind], q, -1) for q in inward})
    density, momentum, _, minus = moments(f)
    odd = odd_parts(density, momentum, minus, accel)
    adj_face = collide_adjoint((density, momentum), g, solid_own, accel)
    adj_face = {q: shift_yz(adj_face[q], q, -1) for q in Q_ZERO + outward}
    return adj_beside, adj_face, sens_terms(g, odd)


def boundary_sens(low, adj_beside, adj_face, odd_ref):
    face, behind = (2, 3) if low else (9, 8)
    total = 0.0
    for q in Q_ZERO:
        if q:
            total = total + adj_face[q] * turned(odd_ref, face, q)
    for q in Q_MINUS if low else Q_PLUS:
        total = total + adj_beside[q] * turned(odd_ref, face, q)
        total = total + adj_face[q] * turned(odd_ref, behind, q)
    return total


def interior_kernel(
    accel_ref,
    f_ref,
    adj_ref,
    from_a,
    from_b,
    own_ref,
    g_out,
    f_next,
    odd_ext,
    mom_out,
    solid_out,
    total_out,
    row,
):
    accel_first = read_accel(accel_ref, 0)
    accel_second = read_accel(accel_ref, 1)
    own = spread(row, own_ref[...])
    solid_own = SOLID_MAX * smooth(from_a[ROW_BLOCKS] + from_b[ROW_BLOCKS], own)
    solid_out[...] = solid_own

    def forward(k, _):
        for half in range(2):
            e = 2 * k + 2 + half
            f = [
                f_ref[q, pl.ds(pl.multiple_of(16 * k, 16), 16), :].astype(jnp.float32)[
                    8 * half : 8 * half + 8
                ]
                for q in range(Q)
            ]
            gray, odd = collide(f, solid_own, accel_first)
            density, momentum, _, _ = moments(f)
            for i, part in enumerate([density] + momentum):
                mom_out[i, e - 2] = part
            for q in range(Q):
                f_next[q, e + 1 + VELOCITIES[q][0]] = shift_yz(gray[q], q, 1)
            for i, p in enumerate(PAIRS):
                odd_ext[i, e] = odd[p]
        return 0

    lax.fori_loop(0, 4, forward, 0, unroll=FORWARD_UNROLL)

    def backward(e, total):
        f = [f_next[q, e + 1] for q in range(Q)]
        g = [shift_yz(adj_ref[q, e - 2 + VELOCITIES[q][0]], q, -1) for q in range(Q)]
        density, momentum, _, minus = moments(f)
        odd = odd_parts(density, momentum, minus, accel_second)
        total = total + sens_terms(g, odd)
        adjoint = collide_adjoint((density, momentum), g, solid_own, accel_second)
        for q in range(Q):
            to = e - VELOCITIES[q][0]
            value = shift_yz(adjoint[q], q, -1)
            g_out[q, to] = value
            if q:
                total = total + value * turned(odd_ext, to, q)
        return total

    total_out[...] = lax.fori_loop(
        3, 9, backward, jnp.zeros((8, 128), jnp.float32), unroll=BACKWARD_UNROLL
    )


def sides_kernel(
    accel_ref,
    adj_ref,
    from_a,
    from_b,
    own_ref,
    solid_ref,
    f_next,
    odd_ext,
    total_ref,
    across_ref,
    within_ref,
    low_out,
    high_out,
    sums_out,
    row,
    past_row,
):
    accel_second = read_accel(accel_ref, 1)
    own = spread(row, own_ref[...])
    row[...] = total_ref[...]
    odd_chip = lax.axis_index("tile") & 2 == 2

    def side(low, message):
        outward = Q_MINUS if low else Q_PLUS
        past = jnp.where(odd_chip == low, within_ref[...], across_ref[...])
        solid = SOLID_MAX * smooth(own + spread(past_row, past), message[ROW_BLOCKS])
        adj_beside, adj_face, sens = boundary(
            low, message, solid, solid_ref[...], f_next, adj_ref, accel_second
        )
        out = low_out if low else high_out
        for i, q in enumerate(Q_ZERO):
            out[i] = adj_face[q]
        for i, q in enumerate(outward):
            out[len(Q_ZERO) + i] = adj_beside[q]
            out[len(Q_ZERO) + len(outward) + i] = adj_face[q]
        row[...] += sens + boundary_sens(low, adj_beside, adj_face, odd_ext)

    def both(low, high):
        side(True, low)
        side(False, high)

    even = is_even()
    pl.when(even)(lambda: both(from_b, from_a))
    pl.when(jnp.logical_not(even))(lambda: both(from_a, from_b))

    total = jnp.broadcast_to(jnp.sum(row[...], axis=0, keepdims=True), (8, 128))
    for step in (1, 2, 4):
        total = total + pltpu.roll(total, 128 - step, 1)
    total = jnp.where(lanes() % BLOCK == 0, total, 0.0)
    sums_out[...] = jnp.broadcast_to(total[0:1][None], sums_out.shape)


def turned(odd_ref, layer, q):
    return -odd_ref[q // 2, layer] if q % 2 else odd_ref[q // 2 - 1, layer]


def start_kernel(accel_ref, solid_ref, g_ref, mom_ref, low_ref, high_ref, out_ref):
    accel = read_accel(accel_ref, 0)
    solid = solid_ref[...]

    def layer(x, changed):
        g = {q: g_ref[q, x + 2] for q in range(Q)}
        g.update(changed)
        momentum = [mom_ref[1 + axis, x] for axis in range(3)]
        adjoint = collide_adjoint((mom_ref[0, x], momentum), g, solid, accel)
        for q in range(Q):
            out_ref[q, x] = adjoint[q]

    def inner(x, _):
        layer(x, {})
        return 0

    lax.fori_loop(2, 6, inner, 0)
    for side, face, behind, outward in ((low_ref, 0, 1, Q_MINUS), (high_ref, 7, 6, Q_PLUS)):
        layer(face, {q: side[i] for i, q in enumerate(Q_ZERO + outward)})
        first = len(Q_ZERO) + len(outward)
        layer(behind, {q: side[first + i] for i, q in enumerate(outward)})


def group_order(cases):
    places = tuple(range(1, GROUP)) + (0,)
    listed = [(place, case) for half in (0, 1) for place in places for case in range(half, cases, 2)]
    listed.remove((1, 1))
    return [(1, 1)] + listed


def place_in_group():
    return (lax.axis_index("tile") - OFFSET) & (GROUP - 1)


def tile_total(sums_ref, cases, tile):
    ranks = [rank for rank, (place, _) in enumerate(group_order(cases)) if place == tile]
    return sum(sums_ref[rank] for rank in ranks)


def end_kernel(cases, sums_ref, out):
    first, last = tile_total(sums_ref, cases, 0), tile_total(sums_ref, cases, GROUP - 1)
    out[...] = jnp.where(place_in_group() == 0, first, last)


def update_kernel(
    cases,
    sums_ref,
    outside_ref,
    design_ref,
    mask_ref,
    first_ref,
    second_ref,
    design_out,
    first_out,
    second_out,
):
    place = place_in_group()
    totals = [tile_total(sums_ref, cases, tile) for tile in range(GROUP)]
    line = [outside_ref[...]] + totals + [outside_ref[...]]
    line = [jnp.broadcast_to(row, (8, 128)) for row in line]

    def pick(shift):
        value = line[shift]
        for k in range(1, GROUP):
            value = jnp.where(place == k, line[k + shift], value)
        return value

    gradient = SOLID_MAX * smooth(pick(0) + pick(2), pick(1))
    spots = jnp.minimum(lanes() * BLOCK, 127)
    gradient = jnp.take_along_axis(gradient, spots, axis=1)[0:1, 0:16]
    gradient = mask_ref[...].astype(jnp.float32) * gradient
    first = BETA_ONE * first_ref[...] + (1.0 - BETA_ONE) * gradient
    second = BETA_TWO * second_ref[...] + (1.0 - BETA_TWO) * gradient * gradient
    stepped = design_ref[...] - LEARN_RATE * (first * (1.0 / BIAS_ONE)) / (
        jnp.sqrt(second * (1.0 / BIAS_TWO)) + ADAM_EPS
    )
    design_out[...] = jnp.clip(stepped, 0.0, 1.0)
    first_out[...] = first
    second_out[...] = second


def tables(tiles, cases):
    run = RUN if tiles % RUN == 0 else tiles

    def device(tile, case):
        return (tile % tiles) * cases + case

    def near(tile, step, case):
        target = tile + step
        crossed = (target // run) != (tile // run)
        return device(target, case ^ 1 if crossed else case)

    found = {name: [] for name in ("chip", "beyond", "across", "within", "ends")}
    for tile in range(tiles):
        step = 1 if tile % 2 else -1
        for case in range(cases):
            here = device(tile, case)
            found["chip"].append((here, device(tile ^ 1, case)))
            found["beyond"].append((here, device(tile + step, case)))
            odd_chip = (tile // 2) % 2
            found["across"].append((here, near(tile, 2 if odd_chip else -2, case)))
            found["within"].append((here, near(tile, -2 if odd_chip else 2, case)))
            place = (tile - OFFSET) % GROUP
            if place == 0:
                found["ends"].append((here, device(tile - 1, case)))
            if place == GROUP - 1:
                found["ends"].append((here, device(tile + 1, case)))
    groups = [
        [device(OFFSET + g * GROUP + place, case) for place, case in group_order(cases)]
        for g in range(tiles // GROUP)
    ]
    return found, groups


VMEM_SPEC = pl.BlockSpec(memory_space=pltpu.VMEM)
HBM_SPEC = pl.BlockSpec(memory_space=pltpu.HBM)
F32 = jnp.float32


def body(
    tiles,
    cases,
    checkpoint,
    adjoint_field,
    accel_table,
    design,
    design_mask,
    first_moment,
    second_moment,
):
    axes = ("tile", "case")
    pairs, groups = tables(tiles, cases)
    f_zero = checkpoint.reshape(Q, 64, 128)
    adjoint = adjoint_field[0]
    flat = [a.reshape(1, 16) for a in (design, design_mask, first_moment, second_moment)]
    params = pltpu.CompilerParams(vmem_limit_bytes=32 * 1024 * 1024)

    def send(value, name):
        return lax.ppermute(value, axes, pairs[name])

    def call(kernel, name, out_shape, in_specs, scratch, *args):
        many = isinstance(out_shape, tuple)
        return pl.pallas_call(
            kernel,
            out_shape=out_shape,
            in_specs=in_specs,
            out_specs=[VMEM_SPEC] * len(out_shape) if many else VMEM_SPEC,
            scratch_shapes=scratch,
            compiler_params=params,
            name=name,
        )(*args)

    def shape(*dims):
        return jax.ShapeDtypeStruct(dims, F32)

    row = pltpu.VMEM((8, 128), F32)
    blocks, accel, *kept, f_zero, adjoint = call(
        load_kernel,
        "load",
        (
            shape(1, 16),
            shape(2, 3, 8, 128),
            shape(1, 16),
            jax.ShapeDtypeStruct((1, 16), jnp.int32),
            shape(1, 16),
            shape(1, 16),
            jax.ShapeDtypeStruct((Q, 64, 128), jnp.bfloat16),
            shape(Q, 8, 8, 128),
        ),
        [HBM_SPEC] * 7,
        [pltpu.SMEM((2, 3), jnp.int32), pltpu.SemaphoreType.DMA((7,))],
        *(
            pltpu.with_memory_space_constraint(a, pltpu.HBM)
            for a in (*flat[:2], accel_table[0], *flat[2:], f_zero, adjoint)
        ),
    )
    to_b, to_a = call(
        pack_kernel,
        "pack_faces",
        (shape(B_ROWS, 8, 128), shape(ROWS, 8, 128)),
        [VMEM_SPEC] * 4,
        [row],
        f_zero,
        adjoint,
        accel,
        blocks,
    )
    from_b = send(to_b, "beyond")
    from_a = send(to_a, "chip")
    within = send(blocks, "within")
    across = send(blocks, "across")
    g_one, f_next, odd, mom, solid, total = call(
        interior_kernel,
        "interior",
        (
            shape(Q, 12, 8, 128),
            shape(Q, 14, 8, 128),
            shape(len(PAIRS), 12, 8, 128),
            shape(4, 8, 8, 128),
            shape(8, 128),
            shape(8, 128),
        ),
        [VMEM_SPEC] * 6,
        [row],
        accel,
        f_zero,
        adjoint,
        from_a,
        from_b,
        blocks,
    )
    face = shape(len(Q_ZERO) + 2 * len(Q_PLUS), 8, 128)
    low, high, sums = call(
        sides_kernel,
        "sides",
        (face, face, shape(GROUP * cases, 1, 128)),
        [VMEM_SPEC] * 11,
        [row, row],
        accel,
        adjoint,
        from_a,
        from_b,
        blocks,
        solid,
        f_next,
        odd,
        total,
        across,
        within,
    )
    sums, low = lax.optimization_barrier((sums, low))
    shared = lax.all_to_all(sums, axes, 0, 0, axis_index_groups=groups, tiled=True)
    start = call(
        start_kernel,
        "adjoint_start",
        shape(Q, 8, 8, 128),
        [VMEM_SPEC] * 6,
        [],
        accel,
        solid,
        g_one,
        mom,
        low,
        high,
    )
    ends = call(
        functools.partial(end_kernel, cases),
        "group_end",
        shape(1, 128),
        [VMEM_SPEC],
        [],
        shared,
    )
    ends, start = lax.optimization_barrier((ends, start))
    outside = send(ends, "ends")
    small = shape(1, 16)
    updated = call(
        functools.partial(update_kernel, cases),
        "update",
        (small, small, small),
        [VMEM_SPEC] * 6,
        [],
        shared,
        outside,
        *kept,
    )
    return (start[None],) + tuple(u.reshape(1, 1, 16) for u in updated)


def solution(mesh):
    placed = (
        P("case", None, "tile", None, None),
        P("case", None, "tile", None, None),
        P("case", None, None),
        P("tile", None, None),
        P("tile", None, None),
        P("tile", None, None),
        P("tile", None, None),
    )
    return jax.shard_map(
        functools.partial(body, mesh.shape["tile"], mesh.shape["case"]),
        mesh=mesh,
        in_specs=placed,
        out_specs=(
            P("case", None, "tile", None, None),
            P("tile", None, None),
            P("tile", None, None),
            P("tile", None, None),
        ),
        check_vma=False,
    )
```

```python
import functools

import jax
import jax.numpy as jnp
import numpy as np
from jax import lax
from jax.experimental import pallas as pl
from jax.experimental.pallas import tpu as pltpu
from jax.sharding import PartitionSpec as P

Q = 19
BLOCK = 8
VELOCITIES = [
    (0, 0, 0),
    (1, 0, 0),
    (-1, 0, 0),
    (0, 1, 0),
    (0, -1, 0),
    (0, 0, 1),
    (0, 0, -1),
    (1, 1, 0),
    (-1, -1, 0),
    (1, -1, 0),
    (-1, 1, 0),
    (1, 0, 1),
    (-1, 0, -1),
    (1, 0, -1),
    (-1, 0, 1),
    (0, 1, 1),
    (0, -1, -1),
    (0, 1, -1),
    (0, -1, 1),
]
W_REST, W_AXIS, W_DIAG = 1.0 / 3.0, 1.0 / 18.0, 1.0 / 36.0
RELAX_RATE = 0.9
SOLID_MAX = 0.5
FACE_WEIGHT = 0.5
ACCEL_SCALE = 400.0
BETA_ONE = 0.9
BETA_TWO = 0.999
LEARN_RATE = 0.2
ADAM_EPS = 1e-08
BIAS_ONE = 1.0 - 0.9**10
BIAS_TWO = 1.0 - 0.999**10

PAIRS = tuple(range(1, Q, 2))
Q_ZERO = [q for q in range(Q) if VELOCITIES[q][0] == 0]
Q_PLUS = [q for q in range(Q) if VELOCITIES[q][0] == 1]
Q_MINUS = [q for q in range(Q) if VELOCITIES[q][0] == -1]
ROW_MOMENTS = 2 * len(Q_PLUS)
ROW_TURNED = ROW_MOMENTS + 4
ROW_LEVEL = ROW_TURNED + 9
ROW_ADJ = ROW_LEVEL + 6
ROW_ADJ_FAR = ROW_ADJ + len(Q_PLUS)
ROW_BLOCKS = ROW_ADJ_FAR + len(Q_PLUS)
ROWS = ROW_BLOCKS + 1
B_ROWS = ROWS + 1
Z_MOTIONS = (0, 1, -1)
RUN = 16
FORWARD_UNROLL = 2
BACKWARD_UNROLL = 6
GROUP = 4
OFFSET = 3


def shift_yz(value, vel_id, direction):
    _, shift_y, shift_z = VELOCITIES[vel_id]
    if shift_y:
        value = pltpu.roll(value, (direction * shift_y) % 8, 0)
    if shift_z:
        value = pltpu.roll(value, (direction * shift_z) % 128, 1)
    return value


def add_signed(total, value, sign):
    if sign == 0:
        return total
    return total + value if sign > 0 else total - value


def along(vector, vel_id):
    total = None
    for part, sign in zip(vector, VELOCITIES[vel_id]):
        if sign == 0:
            continue
        if total is None:
            total = part if sign > 0 else -part
        else:
            total = total + part if sign > 0 else total - part
    return total


def weight(pair):
    return W_AXIS if pair < 7 else W_DIAG


def moments(f):
    plus = {p: f[p] + f[p + 1] for p in PAIRS}
    minus = {p: f[p] - f[p + 1] for p in PAIRS}
    density = f[0]
    for p in PAIRS:
        density = density + plus[p]
    momentum = []
    for axis in range(3):
        total = None
        for p in PAIRS:
            sign = VELOCITIES[p][axis]
            if sign == 0:
                continue
            if total is None:
                total = minus[p]
            else:
                total = total + minus[p] if sign > 0 else total - minus[p]
        momentum.append(total)
    return density, momentum, plus, minus


def odd_parts(density, momentum, minus, accel):
    flow = [3.0 * RELAX_RATE * m + (3.0 * a) * density for m, a in zip(momentum, accel)]
    return {
        p: (1.0 - RELAX_RATE) * minus[p] + (2.0 * weight(p)) * along(flow, p) for p in PAIRS
    }


def collide(f, solid, accel):
    density, momentum, plus, minus = moments(f)
    odd = odd_parts(density, momentum, minus, accel)
    inverse = 1.0 / density
    velocity = [m * inverse for m in momentum]
    speed_sq = sum(m * u for m, u in zip(momentum, velocity))
    base = RELAX_RATE * (density - 1.5 * speed_sq)
    gray = {0: (1.0 - RELAX_RATE) * f[0] + W_REST * base}
    bent = 0.5 - solid
    for p in PAIRS:
        project = along(velocity, p)
        even = 0.5 * (1.0 - RELAX_RATE) * plus[p] + weight(p) * (
            base + (4.5 * RELAX_RATE) * density * (project * project)
        )
        turned = bent * odd[p]
        gray[p] = even + turned
        gray[p + 1] = even - turned
    return gray, odd


def adjoint_parts(f_moments, level, first, second, accel):
    density, momentum = f_moments
    inverse = 1.0 / density
    velocity = [m * inverse for m in momentum]
    bent = [
        sum(second[(min(i, j), max(i, j))] * velocity[j] for j in range(3)) for i in range(3)
    ]
    pull = [
        RELAX_RATE * (3.0 * first[i] + 9.0 * bent[i] - (3.0 * level) * velocity[i])
        for i in range(3)
    ]
    speed_sq = sum(u * u for u in velocity)
    rest = RELAX_RATE * (
        level * (1.0 + 1.5 * speed_sq) - 4.5 * sum(b * u for b, u in zip(bent, velocity))
    )
    return rest + 3.0 * sum(a * b for a, b in zip(accel, first)), pull


def pair_adjoint(plus, minus, rest, pull, pair):
    even = 0.5 * (1.0 - RELAX_RATE) * plus + rest
    odd = 0.5 * (1.0 - RELAX_RATE) * minus + along(pull, pair)
    return even + odd, even - odd


def still_sums(plus, minus, rest):
    diag = W_DIAG * (plus[15] + plus[17])
    axis_y, axis_z = W_AXIS * plus[3], W_AXIS * plus[5]
    return (
        W_REST * rest + axis_y + axis_z + diag,
        axis_y + diag,
        axis_z + diag,
        W_DIAG * (plus[15] - plus[17]),
        W_AXIS * minus[3] + W_DIAG * (minus[15] + minus[17]),
        W_AXIS * minus[5] + W_DIAG * (minus[15] - minus[17]),
    )


def all_sums(still, plus, minus, fluid):
    level, yy, zz, yz, y, z = still
    diag_xy, diag_xz = W_DIAG * (plus[7] + plus[9]), W_DIAG * (plus[11] + plus[13])
    axis_x = W_AXIS * plus[1]
    second = {
        (0, 0): axis_x + diag_xy + diag_xz,
        (1, 1): yy + diag_xy,
        (2, 2): zz + diag_xz,
        (0, 1): W_DIAG * (plus[7] - plus[9]),
        (0, 2): W_DIAG * (plus[11] - plus[13]),
        (1, 2): yz,
    }
    first = [
        fluid * (W_AXIS * minus[1] + W_DIAG * (minus[7] + minus[9] + minus[11] + minus[13])),
        fluid * (y + W_DIAG * (minus[7] - minus[9])),
        fluid * (z + W_DIAG * (minus[11] - minus[13])),
    ]
    return level + axis_x + diag_xy + diag_xz, first, second


def pair_sums(g, pairs):
    return {p: g[p] + g[p + 1] for p in pairs}, {p: g[p] - g[p + 1] for p in pairs}


def collide_adjoint(f_moments, g, solid, accel):
    plus, minus = pair_sums(g, PAIRS)
    fluid = 1.0 - 2.0 * solid
    sums = all_sums(still_sums(plus, minus, g[0]), plus, minus, fluid)
    rest, pull = adjoint_parts(f_moments, *sums, accel)
    out = {0: (1.0 - RELAX_RATE) * g[0] + rest}
    for p in PAIRS:
        out[p], out[p + 1] = pair_adjoint(plus[p], fluid * minus[p], rest, pull, p)
    return out


def sens_terms(g, odd):
    return sum((g[p + 1] - g[p]) * odd[p] for p in PAIRS)


def lanes():
    return lax.broadcasted_iota(jnp.int32, (8, 128), 1)


def read_accel(accel_ref, turn):
    return [accel_ref[turn, axis] for axis in range(3)]


def is_even():
    return lax.axis_index("tile") & 1 == 0


def spread(row, blocks):
    row[...] = jnp.zeros_like(row)
    row[0:1, 0:16] = blocks
    wide = jnp.take_along_axis(row[...], lanes() // BLOCK, axis=1)
    return jnp.broadcast_to(wide[0:1], (8, 128))


def smooth(beside, grid):
    around = beside + 2.0 * grid + pltpu.roll(grid, 8, 1) + pltpu.roll(grid, 120, 1)
    return (grid + FACE_WEIGHT * around) * (1.0 / (1.0 + 6.0 * FACE_WEIGHT))


def read_layer(f_ref, q, x):
    two = f_ref[q, 16 * (x // 2) : 16 * (x // 2) + 16, :].astype(jnp.float32)
    return two[8:16] if x % 2 else two[0:8]


def load_kernel(
    design_hbm,
    mask_hbm,
    accel_hbm,
    first_hbm,
    second_hbm,
    f_hbm,
    adj_hbm,
    blocks_out,
    accel_out,
    design_out,
    mask_out,
    first_out,
    second_out,
    f_out,
    adj_out,
    table,
    sems,
):
    copies = [
        pltpu.make_async_copy(source, target, sems.at[i])
        for i, (source, target) in enumerate(
            (
                (design_hbm, design_out),
                (mask_hbm, mask_out),
                (accel_hbm, table),
                (first_hbm, first_out),
                (second_hbm, second_out),
                (f_hbm, f_out),
                (adj_hbm, adj_out),
            )
        )
    ]
    for copy in copies:
        copy.start()
    for copy in copies[:5]:
        copy.wait()
    blocks_out[...] = design_out[...] * mask_out[...].astype(jnp.float32)
    for turn in range(2):
        for axis in range(3):
            value = table[turn, axis].astype(jnp.float32) * (1.0 / ACCEL_SCALE)
            accel_out[turn, axis] = jnp.full((8, 128), value, jnp.float32)
    for copy in copies[5:]:
        copy.wait()


def pack(f_ref, adj_ref, out, high, blocks, accel):
    near, far = (7, 6) if high else (0, 1)
    onward, back = (Q_PLUS, Q_MINUS) if high else (Q_MINUS, Q_PLUS)
    post, _ = collide([read_layer(f_ref, q, near) for q in range(Q)], 0.0, accel)
    behind, _ = collide([read_layer(f_ref, q, far) for q in range(Q)], 0.0, accel)
    for i, p in enumerate(Q_PLUS):
        out[2 * i] = post[p]
        out[2 * i + 1] = post[p + 1]
    total = [0.0] * 4
    turned_away = {motion: [0.0] * 3 for motion in Z_MOTIONS}
    for q in Q_ZERO + onward:
        layer = behind if q in onward else post
        value = shift_yz(layer[q], q, 1)
        total = [
            add_signed(kept, value, sign) for kept, sign in zip(total, (1,) + VELOCITIES[q])
        ]
        if q:
            value = shift_yz(layer[q] - layer[q + 1 if q % 2 else q - 1], q, 1)
            group = turned_away[VELOCITIES[q][2]]
            signs = (1,) + VELOCITIES[q][:2]
            turned_away[VELOCITIES[q][2]] = [
                add_signed(kept, value, sign) for kept, sign in zip(group, signs)
            ]
    for i in range(4):
        out[ROW_MOMENTS + i] = total[i]
    for k, motion in enumerate(Z_MOTIONS):
        for i in range(3):
            out[ROW_TURNED + 3 * k + i] = turned_away[motion][i]
    g = {q: shift_yz(adj_ref[q, near], q, -1) for q in Q_ZERO + back}
    plus, minus = pair_sums(g, [p for p in PAIRS if p in Q_ZERO])
    for i, value in enumerate(still_sums(plus, minus, g[0])):
        out[ROW_LEVEL + i] = value
    for i, q in enumerate(back):
        out[ROW_ADJ + i] = g[q]
        out[ROW_ADJ_FAR + i] = shift_yz(adj_ref[q, far], q, -1)
    out[ROW_BLOCKS] = blocks


def pack_kernel(f_ref, adj_ref, accel_ref, own_ref, to_b, to_a, row):
    accel = read_accel(accel_ref, 0)
    blocks = spread(row, own_ref[...])
    for r in range(ROWS, B_ROWS):
        to_b[r] = jnp.zeros((8, 128), jnp.float32)

    def both(low, high):
        pack(f_ref, adj_ref, low, False, blocks, accel)
        pack(f_ref, adj_ref, high, True, blocks, accel)

    even = is_even()
    pl.when(even)(lambda: both(to_b, to_a))
    pl.when(jnp.logical_not(even))(lambda: both(to_a, to_b))


def boundary(low, message, solid, solid_own, f_next, adj_ref, accel):
    inward, outward = (Q_PLUS, Q_MINUS) if low else (Q_MINUS, Q_PLUS)
    beside, face, layer, behind = (2, 3, 0, 1) if low else (11, 10, 7, 6)
    first = 0 if low else 1

    part = [message[ROW_MOMENTS + i] for i in range(4)]
    for k, motion in enumerate(Z_MOTIONS):
        moved = pltpu.roll(solid, motion % 128, 1) if motion else solid
        away = [moved * message[ROW_TURNED + 3 * k + i] for i in range(3)]
        part = [a - b for a, b in zip(part, away)] + [add_signed(part[3], away[0], -motion)]
    for q in outward:
        value = f_next[q, beside]
        part = [add_signed(kept, value, sign) for kept, sign in zip(part, (1,) + VELOCITIES[q])]
    g = {q: message[ROW_ADJ_FAR + i] for i, q in enumerate(outward)}
    g.update({q: shift_yz(adj_ref[q, layer], q, -1) for q in inward})
    plus, minus = pair_sums(g, Q_PLUS)
    fluid = 1.0 - 2.0 * solid
    still = [message[ROW_LEVEL + i] for i in range(6)]
    rest, pull = adjoint_parts((part[0], part[1:]), *all_sums(still, plus, minus, fluid), accel)
    adj_beside = {}
    for p in Q_PLUS:
        both = pair_adjoint(plus[p], fluid * minus[p], rest, pull, p)
        q = p + 1 if low else p
        adj_beside[q] = shift_yz(both[q - p], q, -1)

    f = {q: f_next[q, face] for q in Q_ZERO + outward}
    for i, q in enumerate(inward):
        value, opposite = message[2 * i + first], message[2 * i + 1 - first]
        f[q] = shift_yz(value + solid * (opposite - value), q, 1)
    g = {q: message[ROW_ADJ + i] for i, q in enumerate(outward)}
    g.update({q: shift_yz(adj_ref[q, layer], q, -1) for q in Q_ZERO})
    g.update({q: shift_yz(adj_ref[q, behind], q, -1) for q in inward})
    density, momentum, _, minus = moments(f)
    odd = odd_parts(density, momentum, minus, accel)
    adj_face = collide_adjoint((density, momentum), g, solid_own, accel)
    adj_face = {q: shift_yz(adj_face[q], q, -1) for q in Q_ZERO + outward}
    return adj_beside, adj_face, sens_terms(g, odd)


def boundary_sens(low, adj_beside, adj_face, odd_ref):
    face, behind = (2, 3) if low else (9, 8)
    total = 0.0
    for q in Q_ZERO:
        if q:
            total = total + adj_face[q] * turned(odd_ref, face, q)
    for q in Q_MINUS if low else Q_PLUS:
        total = total + adj_beside[q] * turned(odd_ref, face, q)
        total = total + adj_face[q] * turned(odd_ref, behind, q)
    return total


def interior_kernel(
    accel_ref,
    f_ref,
    adj_ref,
    from_a,
    from_b,
    own_ref,
    g_out,
    f_next,
    odd_ext,
    mom_out,
    solid_out,
    total_out,
    row,
):
    accel_first = read_accel(accel_ref, 0)
    accel_second = read_accel(accel_ref, 1)
    own = spread(row, own_ref[...])
    solid_own = SOLID_MAX * smooth(from_a[ROW_BLOCKS] + from_b[ROW_BLOCKS], own)
    solid_out[...] = solid_own

    def forward(k, _):
        for half in range(2):
            e = 2 * k + 2 + half
            f = [
                f_ref[q, pl.ds(pl.multiple_of(16 * k, 16), 16), :].astype(jnp.float32)[
                    8 * half : 8 * half + 8
                ]
                for q in range(Q)
            ]
            gray, odd = collide(f, solid_own, accel_first)
            density, momentum, _, _ = moments(f)
            for i, part in enumerate([density] + momentum):
                mom_out[i, e - 2] = part
            for q in range(Q):
                f_next[q, e + 1 + VELOCITIES[q][0]] = shift_yz(gray[q], q, 1)
            for i, p in enumerate(PAIRS):
                odd_ext[i, e] = odd[p]
        return 0

    lax.fori_loop(0, 4, forward, 0, unroll=FORWARD_UNROLL)

    def backward(e, total):
        f = [f_next[q, e + 1] for q in range(Q)]
        g = [shift_yz(adj_ref[q, e - 2 + VELOCITIES[q][0]], q, -1) for q in range(Q)]
        density, momentum, _, minus = moments(f)
        odd = odd_parts(density, momentum, minus, accel_second)
        total = total + sens_terms(g, odd)
        adjoint = collide_adjoint((density, momentum), g, solid_own, accel_second)
        for q in range(Q):
            to = e - VELOCITIES[q][0]
            value = shift_yz(adjoint[q], q, -1)
            g_out[q, to] = value
            if q:
                total = total + value * turned(odd_ext, to, q)
        return total

    total_out[...] = lax.fori_loop(
        3, 9, backward, jnp.zeros((8, 128), jnp.float32), unroll=BACKWARD_UNROLL
    )


def sides_kernel(
    accel_ref,
    adj_ref,
    from_a,
    from_b,
    own_ref,
    solid_ref,
    f_next,
    odd_ext,
    total_ref,
    across_ref,
    within_ref,
    low_out,
    high_out,
    sums_out,
    row,
    past_row,
):
    accel_second = read_accel(accel_ref, 1)
    own = spread(row, own_ref[...])
    row[...] = total_ref[...]
    odd_chip = lax.axis_index("tile") & 2 == 2

    def side(low, message):
        outward = Q_MINUS if low else Q_PLUS
        past = jnp.where(odd_chip == low, within_ref[...], across_ref[...])
        solid = SOLID_MAX * smooth(own + spread(past_row, past), message[ROW_BLOCKS])
        adj_beside, adj_face, sens = boundary(
            low, message, solid, solid_ref[...], f_next, adj_ref, accel_second
        )
        out = low_out if low else high_out
        for i, q in enumerate(Q_ZERO):
            out[i] = adj_face[q]
        for i, q in enumerate(outward):
            out[len(Q_ZERO) + i] = adj_beside[q]
            out[len(Q_ZERO) + len(outward) + i] = adj_face[q]
        row[...] += sens + boundary_sens(low, adj_beside, adj_face, odd_ext)

    def both(low, high):
        side(True, low)
        side(False, high)

    even = is_even()
    pl.when(even)(lambda: both(from_b, from_a))
    pl.when(jnp.logical_not(even))(lambda: both(from_a, from_b))

    total = jnp.broadcast_to(jnp.sum(row[...], axis=0, keepdims=True), (8, 128))
    for step in (1, 2, 4):
        total = total + pltpu.roll(total, 128 - step, 1)
    total = jnp.where(lanes() % BLOCK == 0, total, 0.0)
    sums_out[...] = jnp.broadcast_to(total[0:1][None], sums_out.shape)


def turned(odd_ref, layer, q):
    return -odd_ref[q // 2, layer] if q % 2 else odd_ref[q // 2 - 1, layer]


def start_kernel(accel_ref, solid_ref, g_ref, mom_ref, low_ref, high_ref, out_ref):
    accel = read_accel(accel_ref, 0)
    solid = solid_ref[...]

    def layer(x, changed):
        g = {q: g_ref[q, x + 2] for q in range(Q)}
        g.update(changed)
        momentum = [mom_ref[1 + axis, x] for axis in range(3)]
        adjoint = collide_adjoint((mom_ref[0, x], momentum), g, solid, accel)
        for q in range(Q):
            out_ref[q, x] = adjoint[q]

    def inner(x, _):
        layer(x, {})
        return 0

    lax.fori_loop(2, 6, inner, 0)
    for side, face, behind, outward in ((low_ref, 0, 1, Q_MINUS), (high_ref, 7, 6, Q_PLUS)):
        layer(face, {q: side[i] for i, q in enumerate(Q_ZERO + outward)})
        first = len(Q_ZERO) + len(outward)
        layer(behind, {q: side[first + i] for i, q in enumerate(outward)})


def group_order(cases):
    places = (2, 1) + tuple(range(3, GROUP)) + (0,)
    listed = [(place, case) for half in (0, 1) for place in places for case in range(half, cases, 2)]
    listed.remove((3, 1))
    return [(3, 1)] + listed


def place_in_group():
    return (lax.axis_index("tile") - OFFSET) & (GROUP - 1)


def tile_total(sums_ref, cases, tile):
    ranks = [rank for rank, (place, _) in enumerate(group_order(cases)) if place == tile]
    return sum(sums_ref[rank] for rank in ranks)


def end_kernel(cases, sums_ref, out):
    first, last = tile_total(sums_ref, cases, 0), tile_total(sums_ref, cases, GROUP - 1)
    out[...] = jnp.where(place_in_group() == 0, first, last)


def update_kernel(
    cases,
    sums_ref,
    outside_ref,
    design_ref,
    mask_ref,
    first_ref,
    second_ref,
    design_out,
    first_out,
    second_out,
):
    place = place_in_group()
    totals = [tile_total(sums_ref, cases, tile) for tile in range(GROUP)]
    line = [outside_ref[...]] + totals + [outside_ref[...]]
    line = [jnp.broadcast_to(row, (8, 128)) for row in line]

    def pick(shift):
        value = line[shift]
        for k in range(1, GROUP):
            value = jnp.where(place == k, line[k + shift], value)
        return value

    gradient = SOLID_MAX * smooth(pick(0) + pick(2), pick(1))
    spots = jnp.minimum(lanes() * BLOCK, 127)
    gradient = jnp.take_along_axis(gradient, spots, axis=1)[0:1, 0:16]
    gradient = mask_ref[...].astype(jnp.float32) * gradient
    first = BETA_ONE * first_ref[...] + (1.0 - BETA_ONE) * gradient
    second = BETA_TWO * second_ref[...] + (1.0 - BETA_TWO) * gradient * gradient
    stepped = design_ref[...] - LEARN_RATE * (first * (1.0 / BIAS_ONE)) / (
        jnp.sqrt(second * (1.0 / BIAS_TWO)) + ADAM_EPS
    )
    design_out[...] = jnp.clip(stepped, 0.0, 1.0)
    first_out[...] = first
    second_out[...] = second


def tables(tiles, cases):
    run = RUN if tiles % RUN == 0 else tiles

    def device(tile, case):
        return (tile % tiles) * cases + case

    def near(tile, step, case):
        target = tile + step
        crossed = (target // run) != (tile // run)
        return device(target, case ^ 1 if crossed else case)

    found = {name: [] for name in ("chip", "beyond", "across", "within", "ends")}
    for tile in range(tiles):
        step = 1 if tile % 2 else -1
        for case in range(cases):
            here = device(tile, case)
            found["chip"].append((here, device(tile ^ 1, case)))
            found["beyond"].append((here, device(tile + step, case)))
            odd_chip = (tile // 2) % 2
            found["across"].append((here, near(tile, 2 if odd_chip else -2, case)))
            found["within"].append((here, near(tile, -2 if odd_chip else 2, case)))
            place = (tile - OFFSET) % GROUP
            if place == 0:
                found["ends"].append((here, device(tile - 1, case)))
            if place == GROUP - 1:
                found["ends"].append((here, device(tile + 1, case)))
    groups = [
        [device(OFFSET + g * GROUP + place, case) for place, case in group_order(cases)]
        for g in range(tiles // GROUP)
    ]
    return found, groups


VMEM_SPEC = pl.BlockSpec(memory_space=pltpu.VMEM)
HBM_SPEC = pl.BlockSpec(memory_space=pltpu.HBM)
F32 = jnp.float32


def body(
    tiles,
    cases,
    checkpoint,
    adjoint_field,
    accel_table,
    design,
    design_mask,
    first_moment,
    second_moment,
):
    axes = ("tile", "case")
    pairs, groups = tables(tiles, cases)
    f_zero = checkpoint.reshape(Q, 64, 128)
    adjoint = adjoint_field[0]
    flat = [a.reshape(1, 16) for a in (design, design_mask, first_moment, second_moment)]
    params = pltpu.CompilerParams(vmem_limit_bytes=32 * 1024 * 1024)

    def send(value, name):
        return lax.ppermute(value, axes, pairs[name])

    def call(kernel, name, out_shape, in_specs, scratch, *args):
        many = isinstance(out_shape, tuple)
        return pl.pallas_call(
            kernel,
            out_shape=out_shape,
            in_specs=in_specs,
            out_specs=[VMEM_SPEC] * len(out_shape) if many else VMEM_SPEC,
            scratch_shapes=scratch,
            compiler_params=params,
            name=name,
        )(*args)

    def shape(*dims):
        return jax.ShapeDtypeStruct(dims, F32)

    row = pltpu.VMEM((8, 128), F32)
    blocks, accel, *kept, f_zero, adjoint = call(
        load_kernel,
        "load",
        (
            shape(1, 16),
            shape(2, 3, 8, 128),
            shape(1, 16),
            jax.ShapeDtypeStruct((1, 16), jnp.int32),
            shape(1, 16),
            shape(1, 16),
            jax.ShapeDtypeStruct((Q, 64, 128), jnp.bfloat16),
            shape(Q, 8, 8, 128),
        ),
        [HBM_SPEC] * 7,
        [pltpu.SMEM((2, 3), jnp.int32), pltpu.SemaphoreType.DMA((7,))],
        *(
            pltpu.with_memory_space_constraint(a, pltpu.HBM)
            for a in (*flat[:2], accel_table[0], *flat[2:], f_zero, adjoint)
        ),
    )
    to_b, to_a = call(
        pack_kernel,
        "pack_faces",
        (shape(B_ROWS, 8, 128), shape(ROWS, 8, 128)),
        [VMEM_SPEC] * 4,
        [row],
        f_zero,
        adjoint,
        accel,
        blocks,
    )
    from_b = send(to_b, "beyond")
    from_a = send(to_a, "chip")
    within = send(blocks, "within")
    across = send(blocks, "across")
    g_one, f_next, odd, mom, solid, total = call(
        interior_kernel,
        "interior",
        (
            shape(Q, 12, 8, 128),
            shape(Q, 14, 8, 128),
            shape(len(PAIRS), 12, 8, 128),
            shape(4, 8, 8, 128),
            shape(8, 128),
            shape(8, 128),
        ),
        [VMEM_SPEC] * 6,
        [row],
        accel,
        f_zero,
        adjoint,
        from_a,
        from_b,
        blocks,
    )
    face = shape(len(Q_ZERO) + 2 * len(Q_PLUS), 8, 128)
    low, high, sums = call(
        sides_kernel,
        "sides",
        (face, face, shape(GROUP * cases, 1, 128)),
        [VMEM_SPEC] * 11,
        [row, row],
        accel,
        adjoint,
        from_a,
        from_b,
        blocks,
        solid,
        f_next,
        odd,
        total,
        across,
        within,
    )
    sums, low = lax.optimization_barrier((sums, low))
    shared = lax.all_to_all(sums, axes, 0, 0, axis_index_groups=groups, tiled=True)
    start = call(
        start_kernel,
        "adjoint_start",
        shape(Q, 8, 8, 128),
        [VMEM_SPEC] * 6,
        [],
        accel,
        solid,
        g_one,
        mom,
        low,
        high,
    )
    ends = call(
        functools.partial(end_kernel, cases),
        "group_end",
        shape(1, 128),
        [VMEM_SPEC],
        [],
        shared,
    )
    ends, start = lax.optimization_barrier((ends, start))
    outside = send(ends, "ends")
    small = shape(1, 16)
    updated = call(
        functools.partial(update_kernel, cases),
        "update",
        (small, small, small),
        [VMEM_SPEC] * 6,
        [],
        shared,
        outside,
        *kept,
    )
    return (start[None],) + tuple(u.reshape(1, 1, 16) for u in updated)


def solution(mesh):
    placed = (
        P("case", None, "tile", None, None),
        P("case", None, "tile", None, None),
        P("case", None, None),
        P("tile", None, None),
        P("tile", None, None),
        P("tile", None, None),
        P("tile", None, None),
    )
    return jax.shard_map(
        functools.partial(body, mesh.shape["tile"], mesh.shape["case"]),
        mesh=mesh,
        in_specs=placed,
        out_specs=(
            P("case", None, "tile", None, None),
            P("tile", None, None),
            P("tile", None, None),
            P("tile", None, None),
        ),
        check_vma=False,
    )
```

```python
import functools

import jax
import jax.numpy as jnp
import numpy as np
from jax import lax
from jax.experimental import pallas as pl
from jax.experimental.pallas import tpu as pltpu
from jax.sharding import PartitionSpec as P

Q = 19
BLOCK = 8
VELOCITIES = [
    (0, 0, 0),
    (1, 0, 0),
    (-1, 0, 0),
    (0, 1, 0),
    (0, -1, 0),
    (0, 0, 1),
    (0, 0, -1),
    (1, 1, 0),
    (-1, -1, 0),
    (1, -1, 0),
    (-1, 1, 0),
    (1, 0, 1),
    (-1, 0, -1),
    (1, 0, -1),
    (-1, 0, 1),
    (0, 1, 1),
    (0, -1, -1),
    (0, 1, -1),
    (0, -1, 1),
]
W_REST, W_AXIS, W_DIAG = 1.0 / 3.0, 1.0 / 18.0, 1.0 / 36.0
RELAX_RATE = 0.9
SOLID_MAX = 0.5
FACE_WEIGHT = 0.5
ACCEL_SCALE = 400.0
BETA_ONE = 0.9
BETA_TWO = 0.999
LEARN_RATE = 0.2
ADAM_EPS = 1e-08
BIAS_ONE = 1.0 - 0.9**10
BIAS_TWO = 1.0 - 0.999**10

PAIRS = tuple(range(1, Q, 2))
Q_ZERO = [q for q in range(Q) if VELOCITIES[q][0] == 0]
Q_PLUS = [q for q in range(Q) if VELOCITIES[q][0] == 1]
Q_MINUS = [q for q in range(Q) if VELOCITIES[q][0] == -1]
ROW_MOMENTS = 2 * len(Q_PLUS)
ROW_TURNED = ROW_MOMENTS + 4
ROW_LEVEL = ROW_TURNED + 9
ROW_ADJ = ROW_LEVEL + 6
ROW_ADJ_FAR = ROW_ADJ + len(Q_PLUS)
ROW_BLOCKS = ROW_ADJ_FAR + len(Q_PLUS)
ROWS = ROW_BLOCKS + 1
B_ROWS = ROWS + 1
Z_MOTIONS = (0, 1, -1)
RUN = 16
FORWARD_UNROLL = 2
BACKWARD_UNROLL = 6
GROUP = 4
OFFSET = 3


def shift_yz(value, vel_id, direction):
    _, shift_y, shift_z = VELOCITIES[vel_id]
    if shift_y:
        value = pltpu.roll(value, (direction * shift_y) % 8, 0)
    if shift_z:
        value = pltpu.roll(value, (direction * shift_z) % 128, 1)
    return value


def add_signed(total, value, sign):
    if sign == 0:
        return total
    return total + value if sign > 0 else total - value


def along(vector, vel_id):
    total = None
    for part, sign in zip(vector, VELOCITIES[vel_id]):
        if sign == 0:
            continue
        if total is None:
            total = part if sign > 0 else -part
        else:
            total = total + part if sign > 0 else total - part
    return total


def weight(pair):
    return W_AXIS if pair < 7 else W_DIAG


def moments(f):
    plus = {p: f[p] + f[p + 1] for p in PAIRS}
    minus = {p: f[p] - f[p + 1] for p in PAIRS}
    density = f[0]
    for p in PAIRS:
        density = density + plus[p]
    momentum = []
    for axis in range(3):
        total = None
        for p in PAIRS:
            sign = VELOCITIES[p][axis]
            if sign == 0:
                continue
            if total is None:
                total = minus[p]
            else:
                total = total + minus[p] if sign > 0 else total - minus[p]
        momentum.append(total)
    return density, momentum, plus, minus


def odd_parts(density, momentum, minus, accel):
    flow = [3.0 * RELAX_RATE * m + (3.0 * a) * density for m, a in zip(momentum, accel)]
    return {
        p: (1.0 - RELAX_RATE) * minus[p] + (2.0 * weight(p)) * along(flow, p) for p in PAIRS
    }


def collide(f, solid, accel):
    density, momentum, plus, minus = moments(f)
    odd = odd_parts(density, momentum, minus, accel)
    inverse = 1.0 / density
    velocity = [m * inverse for m in momentum]
    speed_sq = sum(m * u for m, u in zip(momentum, velocity))
    base = RELAX_RATE * (density - 1.5 * speed_sq)
    gray = {0: (1.0 - RELAX_RATE) * f[0] + W_REST * base}
    bent = 0.5 - solid
    for p in PAIRS:
        project = along(velocity, p)
        even = 0.5 * (1.0 - RELAX_RATE) * plus[p] + weight(p) * (
            base + (4.5 * RELAX_RATE) * density * (project * project)
        )
        turned = bent * odd[p]
        gray[p] = even + turned
        gray[p + 1] = even - turned
    return gray, odd


def adjoint_parts(f_moments, level, first, second, accel):
    density, momentum = f_moments
    inverse = 1.0 / density
    velocity = [m * inverse for m in momentum]
    bent = [
        sum(second[(min(i, j), max(i, j))] * velocity[j] for j in range(3)) for i in range(3)
    ]
    pull = [
        RELAX_RATE * (3.0 * first[i] + 9.0 * bent[i] - (3.0 * level) * velocity[i])
        for i in range(3)
    ]
    speed_sq = sum(u * u for u in velocity)
    rest = RELAX_RATE * (
        level * (1.0 + 1.5 * speed_sq) - 4.5 * sum(b * u for b, u in zip(bent, velocity))
    )
    return rest + 3.0 * sum(a * b for a, b in zip(accel, first)), pull


def pair_adjoint(plus, minus, rest, pull, pair):
    even = 0.5 * (1.0 - RELAX_RATE) * plus + rest
    odd = 0.5 * (1.0 - RELAX_RATE) * minus + along(pull, pair)
    return even + odd, even - odd


def still_sums(plus, minus, rest):
    diag = W_DIAG * (plus[15] + plus[17])
    axis_y, axis_z = W_AXIS * plus[3], W_AXIS * plus[5]
    return (
        W_REST * rest + axis_y + axis_z + diag,
        axis_y + diag,
        axis_z + diag,
        W_DIAG * (plus[15] - plus[17]),
        W_AXIS * minus[3] + W_DIAG * (minus[15] + minus[17]),
        W_AXIS * minus[5] + W_DIAG * (minus[15] - minus[17]),
    )


def all_sums(still, plus, minus, fluid):
    level, yy, zz, yz, y, z = still
    diag_xy, diag_xz = W_DIAG * (plus[7] + plus[9]), W_DIAG * (plus[11] + plus[13])
    axis_x = W_AXIS * plus[1]
    second = {
        (0, 0): axis_x + diag_xy + diag_xz,
        (1, 1): yy + diag_xy,
        (2, 2): zz + diag_xz,
        (0, 1): W_DIAG * (plus[7] - plus[9]),
        (0, 2): W_DIAG * (plus[11] - plus[13]),
        (1, 2): yz,
    }
    first = [
        fluid * (W_AXIS * minus[1] + W_DIAG * (minus[7] + minus[9] + minus[11] + minus[13])),
        fluid * (y + W_DIAG * (minus[7] - minus[9])),
        fluid * (z + W_DIAG * (minus[11] - minus[13])),
    ]
    return level + axis_x + diag_xy + diag_xz, first, second


def pair_sums(g, pairs):
    return {p: g[p] + g[p + 1] for p in pairs}, {p: g[p] - g[p + 1] for p in pairs}


def collide_adjoint(f_moments, g, solid, accel):
    plus, minus = pair_sums(g, PAIRS)
    fluid = 1.0 - 2.0 * solid
    sums = all_sums(still_sums(plus, minus, g[0]), plus, minus, fluid)
    rest, pull = adjoint_parts(f_moments, *sums, accel)
    out = {0: (1.0 - RELAX_RATE) * g[0] + rest}
    for p in PAIRS:
        out[p], out[p + 1] = pair_adjoint(plus[p], fluid * minus[p], rest, pull, p)
    return out


def sens_terms(g, odd):
    return sum((g[p + 1] - g[p]) * odd[p] for p in PAIRS)


def lanes():
    return lax.broadcasted_iota(jnp.int32, (8, 128), 1)


def read_accel(accel_ref, turn):
    return [accel_ref[turn, axis] for axis in range(3)]


def is_even():
    return lax.axis_index("tile") & 1 == 0


def spread(row, blocks):
    row[...] = jnp.zeros_like(row)
    row[0:1, 0:16] = blocks
    wide = jnp.take_along_axis(row[...], lanes() // BLOCK, axis=1)
    return jnp.broadcast_to(wide[0:1], (8, 128))


def smooth(beside, grid):
    around = beside + 2.0 * grid + pltpu.roll(grid, 8, 1) + pltpu.roll(grid, 120, 1)
    return (grid + FACE_WEIGHT * around) * (1.0 / (1.0 + 6.0 * FACE_WEIGHT))


def read_layer(f_ref, q, x):
    two = f_ref[q, 16 * (x // 2) : 16 * (x // 2) + 16, :].astype(jnp.float32)
    return two[8:16] if x % 2 else two[0:8]


def load_kernel(
    design_hbm,
    mask_hbm,
    accel_hbm,
    first_hbm,
    second_hbm,
    f_hbm,
    adj_hbm,
    blocks_out,
    accel_out,
    design_out,
    mask_out,
    first_out,
    second_out,
    f_out,
    adj_out,
    table,
    sems,
):
    copies = [
        pltpu.make_async_copy(source, target, sems.at[i])
        for i, (source, target) in enumerate(
            (
                (design_hbm, design_out),
                (mask_hbm, mask_out),
                (accel_hbm, table),
                (first_hbm, first_out),
                (second_hbm, second_out),
                (f_hbm, f_out),
                (adj_hbm, adj_out),
            )
        )
    ]
    for copy in copies:
        copy.start()
    for copy in copies[:5]:
        copy.wait()
    blocks_out[...] = design_out[...] * mask_out[...].astype(jnp.float32)
    for turn in range(2):
        for axis in range(3):
            value = table[turn, axis].astype(jnp.float32) * (1.0 / ACCEL_SCALE)
            accel_out[turn, axis] = jnp.full((8, 128), value, jnp.float32)
    for copy in copies[5:]:
        copy.wait()


def pack(f_ref, adj_ref, out, high, blocks, accel):
    near, far = (7, 6) if high else (0, 1)
    onward, back = (Q_PLUS, Q_MINUS) if high else (Q_MINUS, Q_PLUS)
    post, _ = collide([read_layer(f_ref, q, near) for q in range(Q)], 0.0, accel)
    behind, _ = collide([read_layer(f_ref, q, far) for q in range(Q)], 0.0, accel)
    for i, p in enumerate(Q_PLUS):
        out[2 * i] = post[p]
        out[2 * i + 1] = post[p + 1]
    total = [0.0] * 4
    turned_away = {motion: [0.0] * 3 for motion in Z_MOTIONS}
    for q in Q_ZERO + onward:
        layer = behind if q in onward else post
        value = shift_yz(layer[q], q, 1)
        total = [
            add_signed(kept, value, sign) for kept, sign in zip(total, (1,) + VELOCITIES[q])
        ]
        if q:
            value = shift_yz(layer[q] - layer[q + 1 if q % 2 else q - 1], q, 1)
            group = turned_away[VELOCITIES[q][2]]
            signs = (1,) + VELOCITIES[q][:2]
            turned_away[VELOCITIES[q][2]] = [
                add_signed(kept, value, sign) for kept, sign in zip(group, signs)
            ]
    for i in range(4):
        out[ROW_MOMENTS + i] = total[i]
    for k, motion in enumerate(Z_MOTIONS):
        for i in range(3):
            out[ROW_TURNED + 3 * k + i] = turned_away[motion][i]
    g = {q: shift_yz(adj_ref[q, near], q, -1) for q in Q_ZERO + back}
    plus, minus = pair_sums(g, [p for p in PAIRS if p in Q_ZERO])
    for i, value in enumerate(still_sums(plus, minus, g[0])):
        out[ROW_LEVEL + i] = value
    for i, q in enumerate(back):
        out[ROW_ADJ + i] = g[q]
        out[ROW_ADJ_FAR + i] = shift_yz(adj_ref[q, far], q, -1)
    out[ROW_BLOCKS] = blocks


def pack_kernel(f_ref, adj_ref, accel_ref, own_ref, to_b, to_a, row):
    accel = read_accel(accel_ref, 0)
    blocks = spread(row, own_ref[...])
    for r in range(ROWS, B_ROWS):
        to_b[r] = jnp.zeros((8, 128), jnp.float32)

    def both(low, high):
        pack(f_ref, adj_ref, low, False, blocks, accel)
        pack(f_ref, adj_ref, high, True, blocks, accel)

    even = is_even()
    pl.when(even)(lambda: both(to_b, to_a))
    pl.when(jnp.logical_not(even))(lambda: both(to_a, to_b))


def enter_kernel(*refs):
    *loaded, to_b, to_a, table, sems, row = refs
    load_kernel(*loaded, table, sems)
    blocks, accel, *_, f_out, adj_out = loaded[7:]
    pack_kernel(f_out, adj_out, accel, blocks, to_b, to_a, row)


def boundary(low, message, solid, solid_own, f_next, adj_ref, accel):
    inward, outward = (Q_PLUS, Q_MINUS) if low else (Q_MINUS, Q_PLUS)
    beside, face, layer, behind = (2, 3, 0, 1) if low else (11, 10, 7, 6)
    first = 0 if low else 1

    part = [message[ROW_MOMENTS + i] for i in range(4)]
    for k, motion in enumerate(Z_MOTIONS):
        moved = pltpu.roll(solid, motion % 128, 1) if motion else solid
        away = [moved * message[ROW_TURNED + 3 * k + i] for i in range(3)]
        part = [a - b for a, b in zip(part, away)] + [add_signed(part[3], away[0], -motion)]
    for q in outward:
        value = f_next[q, beside]
        part = [add_signed(kept, value, sign) for kept, sign in zip(part, (1,) + VELOCITIES[q])]
    g = {q: message[ROW_ADJ_FAR + i] for i, q in enumerate(outward)}
    g.update({q: shift_yz(adj_ref[q, layer], q, -1) for q in inward})
    plus, minus = pair_sums(g, Q_PLUS)
    fluid = 1.0 - 2.0 * solid
    still = [message[ROW_LEVEL + i] for i in range(6)]
    rest, pull = adjoint_parts((part[0], part[1:]), *all_sums(still, plus, minus, fluid), accel)
    adj_beside = {}
    for p in Q_PLUS:
        both = pair_adjoint(plus[p], fluid * minus[p], rest, pull, p)
        q = p + 1 if low else p
        adj_beside[q] = shift_yz(both[q - p], q, -1)

    f = {q: f_next[q, face] for q in Q_ZERO + outward}
    for i, q in enumerate(inward):
        value, opposite = message[2 * i + first], message[2 * i + 1 - first]
        f[q] = shift_yz(value + solid * (opposite - value), q, 1)
    g = {q: message[ROW_ADJ + i] for i, q in enumerate(outward)}
    g.update({q: shift_yz(adj_ref[q, layer], q, -1) for q in Q_ZERO})
    g.update({q: shift_yz(adj_ref[q, behind], q, -1) for q in inward})
    density, momentum, _, minus = moments(f)
    odd = odd_parts(density, momentum, minus, accel)
    adj_face = collide_adjoint((density, momentum), g, solid_own, accel)
    adj_face = {q: shift_yz(adj_face[q], q, -1) for q in Q_ZERO + outward}
    return adj_beside, adj_face, sens_terms(g, odd)


def boundary_sens(low, adj_beside, adj_face, odd_ref):
    face, behind = (2, 3) if low else (9, 8)
    total = 0.0
    for q in Q_ZERO:
        if q:
            total = total + adj_face[q] * turned(odd_ref, face, q)
    for q in Q_MINUS if low else Q_PLUS:
        total = total + adj_beside[q] * turned(odd_ref, face, q)
        total = total + adj_face[q] * turned(odd_ref, behind, q)
    return total


def interior_kernel(
    accel_ref,
    f_ref,
    adj_ref,
    from_a,
    from_b,
    own_ref,
    g_out,
    f_next,
    odd_ext,
    mom_out,
    solid_out,
    total_out,
    row,
):
    accel_first = read_accel(accel_ref, 0)
    accel_second = read_accel(accel_ref, 1)
    own = spread(row, own_ref[...])
    solid_own = SOLID_MAX * smooth(from_a[ROW_BLOCKS] + from_b[ROW_BLOCKS], own)
    solid_out[...] = solid_own

    def forward(k, _):
        for half in range(2):
            e = 2 * k + 2 + half
            f = [
                f_ref[q, pl.ds(pl.multiple_of(16 * k, 16), 16), :].astype(jnp.float32)[
                    8 * half : 8 * half + 8
                ]
                for q in range(Q)
            ]
            gray, odd = collide(f, solid_own, accel_first)
            density, momentum, _, _ = moments(f)
            for i, part in enumerate([density] + momentum):
                mom_out[i, e - 2] = part
            for q in range(Q):
                f_next[q, e + 1 + VELOCITIES[q][0]] = shift_yz(gray[q], q, 1)
            for i, p in enumerate(PAIRS):
                odd_ext[i, e] = odd[p]
        return 0

    lax.fori_loop(0, 4, forward, 0, unroll=FORWARD_UNROLL)

    def backward(e, total):
        f = [f_next[q, e + 1] for q in range(Q)]
        g = [shift_yz(adj_ref[q, e - 2 + VELOCITIES[q][0]], q, -1) for q in range(Q)]
        density, momentum, _, minus = moments(f)
        odd = odd_parts(density, momentum, minus, accel_second)
        total = total + sens_terms(g, odd)
        adjoint = collide_adjoint((density, momentum), g, solid_own, accel_second)
        for q in range(Q):
            to = e - VELOCITIES[q][0]
            value = shift_yz(adjoint[q], q, -1)
            g_out[q, to] = value
            if q:
                total = total + value * turned(odd_ext, to, q)
        return total

    total_out[...] = lax.fori_loop(
        3, 9, backward, jnp.zeros((8, 128), jnp.float32), unroll=BACKWARD_UNROLL
    )


def sides_kernel(
    accel_ref,
    adj_ref,
    from_a,
    from_b,
    own_ref,
    solid_ref,
    f_next,
    odd_ext,
    total_ref,
    across_ref,
    within_ref,
    low_out,
    high_out,
    sums_out,
    row,
    past_row,
):
    accel_second = read_accel(accel_ref, 1)
    own = spread(row, own_ref[...])
    row[...] = total_ref[...]
    odd_chip = lax.axis_index("tile") & 2 == 2

    def side(low, message):
        outward = Q_MINUS if low else Q_PLUS
        past = jnp.where(odd_chip == low, within_ref[...], across_ref[...])
        solid = SOLID_MAX * smooth(own + spread(past_row, past), message[ROW_BLOCKS])
        adj_beside, adj_face, sens = boundary(
            low, message, solid, solid_ref[...], f_next, adj_ref, accel_second
        )
        out = low_out if low else high_out
        for i, q in enumerate(Q_ZERO):
            out[i] = adj_face[q]
        for i, q in enumerate(outward):
            out[len(Q_ZERO) + i] = adj_beside[q]
            out[len(Q_ZERO) + len(outward) + i] = adj_face[q]
        row[...] += sens + boundary_sens(low, adj_beside, adj_face, odd_ext)

    def both(low, high):
        side(True, low)
        side(False, high)

    even = is_even()
    pl.when(even)(lambda: both(from_b, from_a))
    pl.when(jnp.logical_not(even))(lambda: both(from_a, from_b))

    total = jnp.broadcast_to(jnp.sum(row[...], axis=0, keepdims=True), (8, 128))
    for step in (1, 2, 4):
        total = total + pltpu.roll(total, 128 - step, 1)
    total = jnp.where(lanes() % BLOCK == 0, total, 0.0)
    sums_out[...] = jnp.broadcast_to(total[0:1][None], sums_out.shape)


def turned(odd_ref, layer, q):
    return -odd_ref[q // 2, layer] if q % 2 else odd_ref[q // 2 - 1, layer]


def start_kernel(accel_ref, solid_ref, g_ref, mom_ref, low_ref, high_ref, out_ref):
    accel = read_accel(accel_ref, 0)
    solid = solid_ref[...]

    def layer(x, changed):
        g = {q: g_ref[q, x + 2] for q in range(Q)}
        g.update(changed)
        momentum = [mom_ref[1 + axis, x] for axis in range(3)]
        adjoint = collide_adjoint((mom_ref[0, x], momentum), g, solid, accel)
        for q in range(Q):
            out_ref[q, x] = adjoint[q]

    def inner(x, _):
        layer(x, {})
        return 0

    lax.fori_loop(2, 6, inner, 0)
    for side, face, behind, outward in ((low_ref, 0, 1, Q_MINUS), (high_ref, 7, 6, Q_PLUS)):
        layer(face, {q: side[i] for i, q in enumerate(Q_ZERO + outward)})
        first = len(Q_ZERO) + len(outward)
        layer(behind, {q: side[first + i] for i, q in enumerate(outward)})


def group_order(cases):
    places = (2, 1) + tuple(range(3, GROUP)) + (0,)
    listed = [(place, case) for half in (0, 1) for place in places for case in range(half, cases, 2)]
    listed.remove((3, 1))
    return [(3, 1)] + listed


def place_in_group():
    return (lax.axis_index("tile") - OFFSET) & (GROUP - 1)


def tile_total(sums_ref, cases, tile):
    ranks = [rank for rank, (place, _) in enumerate(group_order(cases)) if place == tile]
    return sum(sums_ref[rank] for rank in ranks)


def end_kernel(cases, sums_ref, out):
    first, last = tile_total(sums_ref, cases, 0), tile_total(sums_ref, cases, GROUP - 1)
    out[...] = jnp.where(place_in_group() == 0, first, last)


def update_kernel(
    cases,
    sums_ref,
    outside_ref,
    design_ref,
    mask_ref,
    first_ref,
    second_ref,
    design_out,
    first_out,
    second_out,
):
    place = place_in_group()
    totals = [tile_total(sums_ref, cases, tile) for tile in range(GROUP)]
    line = [outside_ref[...]] + totals + [outside_ref[...]]
    line = [jnp.broadcast_to(row, (8, 128)) for row in line]

    def pick(shift):
        value = line[shift]
        for k in range(1, GROUP):
            value = jnp.where(place == k, line[k + shift], value)
        return value

    gradient = SOLID_MAX * smooth(pick(0) + pick(2), pick(1))
    spots = jnp.minimum(lanes() * BLOCK, 127)
    gradient = jnp.take_along_axis(gradient, spots, axis=1)[0:1, 0:16]
    gradient = mask_ref[...].astype(jnp.float32) * gradient
    first = BETA_ONE * first_ref[...] + (1.0 - BETA_ONE) * gradient
    second = BETA_TWO * second_ref[...] + (1.0 - BETA_TWO) * gradient * gradient
    stepped = design_ref[...] - LEARN_RATE * (first * (1.0 / BIAS_ONE)) / (
        jnp.sqrt(second * (1.0 / BIAS_TWO)) + ADAM_EPS
    )
    design_out[...] = jnp.clip(stepped, 0.0, 1.0)
    first_out[...] = first
    second_out[...] = second


def tables(tiles, cases):
    run = RUN if tiles % RUN == 0 else tiles

    def device(tile, case):
        return (tile % tiles) * cases + case

    def near(tile, step, case):
        target = tile + step
        crossed = (target // run) != (tile // run)
        return device(target, case ^ 1 if crossed else case)

    found = {name: [] for name in ("chip", "beyond", "across", "within", "ends")}
    for tile in range(tiles):
        step = 1 if tile % 2 else -1
        for case in range(cases):
            here = device(tile, case)
            found["chip"].append((here, device(tile ^ 1, case)))
            found["beyond"].append((here, device(tile + step, case)))
            odd_chip = (tile // 2) % 2
            found["across"].append((here, near(tile, 2 if odd_chip else -2, case)))
            found["within"].append((here, near(tile, -2 if odd_chip else 2, case)))
            place = (tile - OFFSET) % GROUP
            if place == 0:
                found["ends"].append((here, device(tile - 1, case)))
            if place == GROUP - 1:
                found["ends"].append((here, device(tile + 1, case)))
    groups = [
        [device(OFFSET + g * GROUP + place, case) for place, case in group_order(cases)]
        for g in range(tiles // GROUP)
    ]
    return found, groups


VMEM_SPEC = pl.BlockSpec(memory_space=pltpu.VMEM)
HBM_SPEC = pl.BlockSpec(memory_space=pltpu.HBM)
F32 = jnp.float32


def body(
    tiles,
    cases,
    checkpoint,
    adjoint_field,
    accel_table,
    design,
    design_mask,
    first_moment,
    second_moment,
):
    axes = ("tile", "case")
    pairs, groups = tables(tiles, cases)
    f_zero = checkpoint.reshape(Q, 64, 128)
    adjoint = adjoint_field[0]
    flat = [a.reshape(1, 16) for a in (design, design_mask, first_moment, second_moment)]
    params = pltpu.CompilerParams(vmem_limit_bytes=32 * 1024 * 1024)

    def send(value, name):
        return lax.ppermute(value, axes, pairs[name])

    def call(kernel, name, out_shape, in_specs, scratch, *args):
        many = isinstance(out_shape, tuple)
        return pl.pallas_call(
            kernel,
            out_shape=out_shape,
            in_specs=in_specs,
            out_specs=[VMEM_SPEC] * len(out_shape) if many else VMEM_SPEC,
            scratch_shapes=scratch,
            compiler_params=params,
            name=name,
        )(*args)

    def shape(*dims):
        return jax.ShapeDtypeStruct(dims, F32)

    row = pltpu.VMEM((8, 128), F32)
    blocks, accel, *kept, f_zero, adjoint, to_b, to_a = call(
        enter_kernel,
        "load_and_pack",
        (
            shape(1, 16),
            shape(2, 3, 8, 128),
            shape(1, 16),
            jax.ShapeDtypeStruct((1, 16), jnp.int32),
            shape(1, 16),
            shape(1, 16),
            jax.ShapeDtypeStruct((Q, 64, 128), jnp.bfloat16),
            shape(Q, 8, 8, 128),
            shape(B_ROWS, 8, 128),
            shape(ROWS, 8, 128),
        ),
        [HBM_SPEC] * 7,
        [pltpu.SMEM((2, 3), jnp.int32), pltpu.SemaphoreType.DMA((7,)), row],
        *(
            pltpu.with_memory_space_constraint(a, pltpu.HBM)
            for a in (*flat[:2], accel_table[0], *flat[2:], f_zero, adjoint)
        ),
    )
    from_b = send(to_b, "beyond")
    from_a = send(to_a, "chip")
    within = send(blocks, "within")
    across = send(blocks, "across")
    g_one, f_next, odd, mom, solid, total = call(
        interior_kernel,
        "interior",
        (
            shape(Q, 12, 8, 128),
            shape(Q, 14, 8, 128),
            shape(len(PAIRS), 12, 8, 128),
            shape(4, 8, 8, 128),
            shape(8, 128),
            shape(8, 128),
        ),
        [VMEM_SPEC] * 6,
        [row],
        accel,
        f_zero,
        adjoint,
        from_a,
        from_b,
        blocks,
    )
    face = shape(len(Q_ZERO) + 2 * len(Q_PLUS), 8, 128)
    low, high, sums = call(
        sides_kernel,
        "sides",
        (face, face, shape(GROUP * cases, 1, 128)),
        [VMEM_SPEC] * 11,
        [row, row],
        accel,
        adjoint,
        from_a,
        from_b,
        blocks,
        solid,
        f_next,
        odd,
        total,
        across,
        within,
    )
    sums, low = lax.optimization_barrier((sums, low))
    shared = lax.all_to_all(sums, axes, 0, 0, axis_index_groups=groups, tiled=True)
    start = call(
        start_kernel,
        "adjoint_start",
        shape(Q, 8, 8, 128),
        [VMEM_SPEC] * 6,
        [],
        accel,
        solid,
        g_one,
        mom,
        low,
        high,
    )
    ends = call(
        functools.partial(end_kernel, cases),
        "group_end",
        shape(1, 128),
        [VMEM_SPEC],
        [],
        shared,
    )
    ends, start = lax.optimization_barrier((ends, start))
    outside = send(ends, "ends")
    small = shape(1, 16)
    updated = call(
        functools.partial(update_kernel, cases),
        "update",
        (small, small, small),
        [VMEM_SPEC] * 6,
        [],
        shared,
        outside,
        *kept,
    )
    return (start[None],) + tuple(u.reshape(1, 1, 16) for u in updated)


def solution(mesh):
    placed = (
        P("case", None, "tile", None, None),
        P("case", None, "tile", None, None),
        P("case", None, None),
        P("tile", None, None),
        P("tile", None, None),
        P("tile", None, None),
        P("tile", None, None),
    )
    return jax.shard_map(
        functools.partial(body, mesh.shape["tile"], mesh.shape["case"]),
        mesh=mesh,
        in_specs=placed,
        out_specs=(
            P("case", None, "tile", None, None),
            P("tile", None, None),
            P("tile", None, None),
            P("tile", None, None),
        ),
        check_vma=False,
    )
```

```python
import functools

import jax
import jax.numpy as jnp
import numpy as np
from jax import lax
from jax.experimental import pallas as pl
from jax.experimental.pallas import tpu as pltpu
from jax.sharding import PartitionSpec as P

Q = 19
BLOCK = 8
VELOCITIES = [
    (0, 0, 0),
    (1, 0, 0),
    (-1, 0, 0),
    (0, 1, 0),
    (0, -1, 0),
    (0, 0, 1),
    (0, 0, -1),
    (1, 1, 0),
    (-1, -1, 0),
    (1, -1, 0),
    (-1, 1, 0),
    (1, 0, 1),
    (-1, 0, -1),
    (1, 0, -1),
    (-1, 0, 1),
    (0, 1, 1),
    (0, -1, -1),
    (0, 1, -1),
    (0, -1, 1),
]
W_REST, W_AXIS, W_DIAG = 1.0 / 3.0, 1.0 / 18.0, 1.0 / 36.0
RELAX_RATE = 0.9
SOLID_MAX = 0.5
FACE_WEIGHT = 0.5
ACCEL_SCALE = 400.0
BETA_ONE = 0.9
BETA_TWO = 0.999
LEARN_RATE = 0.2
ADAM_EPS = 1e-08
BIAS_ONE = 1.0 - 0.9**10
BIAS_TWO = 1.0 - 0.999**10

PAIRS = tuple(range(1, Q, 2))
Q_ZERO = [q for q in range(Q) if VELOCITIES[q][0] == 0]
Q_PLUS = [q for q in range(Q) if VELOCITIES[q][0] == 1]
Q_MINUS = [q for q in range(Q) if VELOCITIES[q][0] == -1]
ROW_MOMENTS = 2 * len(Q_PLUS)
ROW_TURNED = ROW_MOMENTS + 4
ROW_LEVEL = ROW_TURNED + 9
ROW_ADJ = ROW_LEVEL + 6
ROW_ADJ_FAR = ROW_ADJ + len(Q_PLUS)
ROW_BLOCKS = ROW_ADJ_FAR + len(Q_PLUS)
ROWS = ROW_BLOCKS + 1
B_ROWS = ROWS + 1
Z_MOTIONS = (0, 1, -1)
RUN = 16
FORWARD_UNROLL = 2
BACKWARD_UNROLL = 6
GROUP = 4
OFFSET = 3


def shift_yz(value, vel_id, direction):
    _, shift_y, shift_z = VELOCITIES[vel_id]
    if shift_y:
        value = pltpu.roll(value, (direction * shift_y) % 8, 0)
    if shift_z:
        value = pltpu.roll(value, (direction * shift_z) % 128, 1)
    return value


def add_signed(total, value, sign):
    if sign == 0:
        return total
    return total + value if sign > 0 else total - value


def along(vector, vel_id):
    total = None
    for part, sign in zip(vector, VELOCITIES[vel_id]):
        if sign == 0:
            continue
        if total is None:
            total = part if sign > 0 else -part
        else:
            total = total + part if sign > 0 else total - part
    return total


def weight(pair):
    return W_AXIS if pair < 7 else W_DIAG


def moments(f):
    plus = {p: f[p] + f[p + 1] for p in PAIRS}
    minus = {p: f[p] - f[p + 1] for p in PAIRS}
    density = f[0]
    for p in PAIRS:
        density = density + plus[p]
    momentum = []
    for axis in range(3):
        total = None
        for p in PAIRS:
            sign = VELOCITIES[p][axis]
            if sign == 0:
                continue
            if total is None:
                total = minus[p]
            else:
                total = total + minus[p] if sign > 0 else total - minus[p]
        momentum.append(total)
    return density, momentum, plus, minus


def odd_parts(density, momentum, minus, accel):
    flow = [3.0 * RELAX_RATE * m + (3.0 * a) * density for m, a in zip(momentum, accel)]
    return {
        p: (1.0 - RELAX_RATE) * minus[p] + (2.0 * weight(p)) * along(flow, p) for p in PAIRS
    }


def collide(f, solid, accel):
    density, momentum, plus, minus = moments(f)
    odd = odd_parts(density, momentum, minus, accel)
    inverse = 1.0 / density
    velocity = [m * inverse for m in momentum]
    speed_sq = sum(m * u for m, u in zip(momentum, velocity))
    base = RELAX_RATE * (density - 1.5 * speed_sq)
    gray = {0: (1.0 - RELAX_RATE) * f[0] + W_REST * base}
    bent = 0.5 - solid
    for p in PAIRS:
        project = along(velocity, p)
        even = 0.5 * (1.0 - RELAX_RATE) * plus[p] + weight(p) * (
            base + (4.5 * RELAX_RATE) * density * (project * project)
        )
        turned = bent * odd[p]
        gray[p] = even + turned
        gray[p + 1] = even - turned
    return gray, odd


def adjoint_parts(f_moments, level, first, second, accel):
    density, momentum = f_moments
    inverse = 1.0 / density
    velocity = [m * inverse for m in momentum]
    bent = [
        sum(second[(min(i, j), max(i, j))] * velocity[j] for j in range(3)) for i in range(3)
    ]
    pull = [
        RELAX_RATE * (3.0 * first[i] + 9.0 * bent[i] - (3.0 * level) * velocity[i])
        for i in range(3)
    ]
    speed_sq = sum(u * u for u in velocity)
    rest = RELAX_RATE * (
        level * (1.0 + 1.5 * speed_sq) - 4.5 * sum(b * u for b, u in zip(bent, velocity))
    )
    return rest + 3.0 * sum(a * b for a, b in zip(accel, first)), pull


def pair_adjoint(plus, minus, rest, pull, pair):
    even = 0.5 * (1.0 - RELAX_RATE) * plus + rest
    odd = 0.5 * (1.0 - RELAX_RATE) * minus + along(pull, pair)
    return even + odd, even - odd


def still_sums(plus, minus, rest):
    diag = W_DIAG * (plus[15] + plus[17])
    axis_y, axis_z = W_AXIS * plus[3], W_AXIS * plus[5]
    return (
        W_REST * rest + axis_y + axis_z + diag,
        axis_y + diag,
        axis_z + diag,
        W_DIAG * (plus[15] - plus[17]),
        W_AXIS * minus[3] + W_DIAG * (minus[15] + minus[17]),
        W_AXIS * minus[5] + W_DIAG * (minus[15] - minus[17]),
    )


def all_sums(still, plus, minus, fluid):
    level, yy, zz, yz, y, z = still
    diag_xy, diag_xz = W_DIAG * (plus[7] + plus[9]), W_DIAG * (plus[11] + plus[13])
    axis_x = W_AXIS * plus[1]
    second = {
        (0, 0): axis_x + diag_xy + diag_xz,
        (1, 1): yy + diag_xy,
        (2, 2): zz + diag_xz,
        (0, 1): W_DIAG * (plus[7] - plus[9]),
        (0, 2): W_DIAG * (plus[11] - plus[13]),
        (1, 2): yz,
    }
    first = [
        fluid * (W_AXIS * minus[1] + W_DIAG * (minus[7] + minus[9] + minus[11] + minus[13])),
        fluid * (y + W_DIAG * (minus[7] - minus[9])),
        fluid * (z + W_DIAG * (minus[11] - minus[13])),
    ]
    return level + axis_x + diag_xy + diag_xz, first, second


def pair_sums(g, pairs):
    return {p: g[p] + g[p + 1] for p in pairs}, {p: g[p] - g[p + 1] for p in pairs}


def collide_adjoint(f_moments, g, solid, accel):
    plus, minus = pair_sums(g, PAIRS)
    fluid = 1.0 - 2.0 * solid
    sums = all_sums(still_sums(plus, minus, g[0]), plus, minus, fluid)
    rest, pull = adjoint_parts(f_moments, *sums, accel)
    out = {0: (1.0 - RELAX_RATE) * g[0] + rest}
    for p in PAIRS:
        out[p], out[p + 1] = pair_adjoint(plus[p], fluid * minus[p], rest, pull, p)
    return out


def sens_terms(g, odd):
    return sum((g[p + 1] - g[p]) * odd[p] for p in PAIRS)


def lanes():
    return lax.broadcasted_iota(jnp.int32, (8, 128), 1)


def read_accel(accel_ref, turn):
    return [accel_ref[turn, axis] for axis in range(3)]


def is_even():
    return lax.axis_index("tile") & 1 == 0


def spread(row, blocks):
    row[...] = jnp.zeros_like(row)
    row[0:1, 0:16] = blocks
    wide = jnp.take_along_axis(row[...], lanes() // BLOCK, axis=1)
    return jnp.broadcast_to(wide[0:1], (8, 128))


def smooth(beside, grid):
    around = beside + 2.0 * grid + pltpu.roll(grid, 8, 1) + pltpu.roll(grid, 120, 1)
    return (grid + FACE_WEIGHT * around) * (1.0 / (1.0 + 6.0 * FACE_WEIGHT))


def read_layer(f_ref, q, x):
    two = f_ref[q, 16 * (x // 2) : 16 * (x // 2) + 16, :].astype(jnp.float32)
    return two[8:16] if x % 2 else two[0:8]


def load_kernel(
    design_hbm,
    mask_hbm,
    accel_hbm,
    first_hbm,
    second_hbm,
    f_hbm,
    adj_hbm,
    blocks_out,
    accel_out,
    design_out,
    mask_out,
    first_out,
    second_out,
    f_out,
    adj_out,
    table,
    sems,
):
    copies = [
        pltpu.make_async_copy(source, target, sems.at[i])
        for i, (source, target) in enumerate(
            (
                (design_hbm, design_out),
                (mask_hbm, mask_out),
                (accel_hbm, table),
                (first_hbm, first_out),
                (second_hbm, second_out),
                (f_hbm, f_out),
                (adj_hbm, adj_out),
            )
        )
    ]
    for copy in copies[5:] + copies[:5]:
        copy.start()
    for copy in copies[:5]:
        copy.wait()
    blocks_out[...] = design_out[...] * mask_out[...].astype(jnp.float32)
    for turn in range(2):
        for axis in range(3):
            value = table[turn, axis].astype(jnp.float32) * (1.0 / ACCEL_SCALE)
            accel_out[turn, axis] = jnp.full((8, 128), value, jnp.float32)
    for copy in copies[5:]:
        copy.wait()


def pack(f_ref, adj_ref, out, high, blocks, accel):
    near, far = (7, 6) if high else (0, 1)
    onward, back = (Q_PLUS, Q_MINUS) if high else (Q_MINUS, Q_PLUS)
    post, _ = collide([read_layer(f_ref, q, near) for q in range(Q)], 0.0, accel)
    behind, _ = collide([read_layer(f_ref, q, far) for q in range(Q)], 0.0, accel)
    for i, p in enumerate(Q_PLUS):
        out[2 * i] = post[p]
        out[2 * i + 1] = post[p + 1]
    total = [0.0] * 4
    turned_away = {motion: [0.0] * 3 for motion in Z_MOTIONS}
    for q in Q_ZERO + onward:
        layer = behind if q in onward else post
        value = shift_yz(layer[q], q, 1)
        total = [
            add_signed(kept, value, sign) for kept, sign in zip(total, (1,) + VELOCITIES[q])
        ]
        if q:
            value = shift_yz(layer[q] - layer[q + 1 if q % 2 else q - 1], q, 1)
            group = turned_away[VELOCITIES[q][2]]
            signs = (1,) + VELOCITIES[q][:2]
            turned_away[VELOCITIES[q][2]] = [
                add_signed(kept, value, sign) for kept, sign in zip(group, signs)
            ]
    for i in range(4):
        out[ROW_MOMENTS + i] = total[i]
    for k, motion in enumerate(Z_MOTIONS):
        for i in range(3):
            out[ROW_TURNED + 3 * k + i] = turned_away[motion][i]
    g = {q: shift_yz(adj_ref[q, near], q, -1) for q in Q_ZERO + back}
    plus, minus = pair_sums(g, [p for p in PAIRS if p in Q_ZERO])
    for i, value in enumerate(still_sums(plus, minus, g[0])):
        out[ROW_LEVEL + i] = value
    for i, q in enumerate(back):
        out[ROW_ADJ + i] = g[q]
        out[ROW_ADJ_FAR + i] = shift_yz(adj_ref[q, far], q, -1)
    out[ROW_BLOCKS] = blocks


def pack_kernel(f_ref, adj_ref, accel_ref, own_ref, to_b, to_a, row):
    accel = read_accel(accel_ref, 0)
    blocks = spread(row, own_ref[...])
    for r in range(ROWS, B_ROWS):
        to_b[r] = jnp.zeros((8, 128), jnp.float32)

    def both(low, high):
        pack(f_ref, adj_ref, low, False, blocks, accel)
        pack(f_ref, adj_ref, high, True, blocks, accel)

    even = is_even()
    pl.when(even)(lambda: both(to_b, to_a))
    pl.when(jnp.logical_not(even))(lambda: both(to_a, to_b))


def enter_kernel(*refs):
    *loaded, to_b, to_a, table, sems, row = refs
    load_kernel(*loaded, table, sems)
    blocks, accel, *_, f_out, adj_out = loaded[7:]
    pack_kernel(f_out, adj_out, accel, blocks, to_b, to_a, row)


def boundary(low, message, solid, solid_own, f_next, adj_ref, accel):
    inward, outward = (Q_PLUS, Q_MINUS) if low else (Q_MINUS, Q_PLUS)
    beside, face, layer, behind = (2, 3, 0, 1) if low else (11, 10, 7, 6)
    first = 0 if low else 1

    part = [message[ROW_MOMENTS + i] for i in range(4)]
    for k, motion in enumerate(Z_MOTIONS):
        moved = pltpu.roll(solid, motion % 128, 1) if motion else solid
        away = [moved * message[ROW_TURNED + 3 * k + i] for i in range(3)]
        part = [a - b for a, b in zip(part, away)] + [add_signed(part[3], away[0], -motion)]
    for q in outward:
        value = f_next[q, beside]
        part = [add_signed(kept, value, sign) for kept, sign in zip(part, (1,) + VELOCITIES[q])]
    g = {q: message[ROW_ADJ_FAR + i] for i, q in enumerate(outward)}
    g.update({q: shift_yz(adj_ref[q, layer], q, -1) for q in inward})
    plus, minus = pair_sums(g, Q_PLUS)
    fluid = 1.0 - 2.0 * solid
    still = [message[ROW_LEVEL + i] for i in range(6)]
    rest, pull = adjoint_parts((part[0], part[1:]), *all_sums(still, plus, minus, fluid), accel)
    adj_beside = {}
    for p in Q_PLUS:
        both = pair_adjoint(plus[p], fluid * minus[p], rest, pull, p)
        q = p + 1 if low else p
        adj_beside[q] = shift_yz(both[q - p], q, -1)

    f = {q: f_next[q, face] for q in Q_ZERO + outward}
    for i, q in enumerate(inward):
        value, opposite = message[2 * i + first], message[2 * i + 1 - first]
        f[q] = shift_yz(value + solid * (opposite - value), q, 1)
    g = {q: message[ROW_ADJ + i] for i, q in enumerate(outward)}
    g.update({q: shift_yz(adj_ref[q, layer], q, -1) for q in Q_ZERO})
    g.update({q: shift_yz(adj_ref[q, behind], q, -1) for q in inward})
    density, momentum, _, minus = moments(f)
    odd = odd_parts(density, momentum, minus, accel)
    adj_face = collide_adjoint((density, momentum), g, solid_own, accel)
    adj_face = {q: shift_yz(adj_face[q], q, -1) for q in Q_ZERO + outward}
    return adj_beside, adj_face, sens_terms(g, odd)


def boundary_sens(low, adj_beside, adj_face, odd_ref):
    face, behind = (2, 3) if low else (9, 8)
    total = 0.0
    for q in Q_ZERO:
        if q:
            total = total + adj_face[q] * turned(odd_ref, face, q)
    for q in Q_MINUS if low else Q_PLUS:
        total = total + adj_beside[q] * turned(odd_ref, face, q)
        total = total + adj_face[q] * turned(odd_ref, behind, q)
    return total


def interior_kernel(
    accel_ref,
    f_ref,
    adj_ref,
    from_a,
    from_b,
    own_ref,
    g_out,
    f_next,
    odd_ext,
    mom_out,
    solid_out,
    total_out,
    row,
):
    accel_first = read_accel(accel_ref, 0)
    accel_second = read_accel(accel_ref, 1)
    own = spread(row, own_ref[...])
    solid_own = SOLID_MAX * smooth(from_a[ROW_BLOCKS] + from_b[ROW_BLOCKS], own)
    solid_out[...] = solid_own

    def forward(k, _):
        for half in range(2):
            e = 2 * k + 2 + half
            f = [
                f_ref[q, pl.ds(pl.multiple_of(16 * k, 16), 16), :].astype(jnp.float32)[
                    8 * half : 8 * half + 8
                ]
                for q in range(Q)
            ]
            gray, odd = collide(f, solid_own, accel_first)
            density, momentum, _, _ = moments(f)
            for i, part in enumerate([density] + momentum):
                mom_out[i, e - 2] = part
            for q in range(Q):
                f_next[q, e + 1 + VELOCITIES[q][0]] = shift_yz(gray[q], q, 1)
            for i, p in enumerate(PAIRS):
                odd_ext[i, e] = odd[p]
        return 0

    lax.fori_loop(0, 4, forward, 0, unroll=FORWARD_UNROLL)

    def backward(e, total):
        f = [f_next[q, e + 1] for q in range(Q)]
        g = [shift_yz(adj_ref[q, e - 2 + VELOCITIES[q][0]], q, -1) for q in range(Q)]
        density, momentum, _, minus = moments(f)
        odd = odd_parts(density, momentum, minus, accel_second)
        total = total + sens_terms(g, odd)
        adjoint = collide_adjoint((density, momentum), g, solid_own, accel_second)
        for q in range(Q):
            to = e - VELOCITIES[q][0]
            value = shift_yz(adjoint[q], q, -1)
            g_out[q, to] = value
            if q:
                total = total + value * turned(odd_ext, to, q)
        return total

    total_out[...] = lax.fori_loop(
        3, 9, backward, jnp.zeros((8, 128), jnp.float32), unroll=BACKWARD_UNROLL
    )


def sides_kernel(
    accel_ref,
    adj_ref,
    from_a,
    from_b,
    own_ref,
    solid_ref,
    f_next,
    odd_ext,
    total_ref,
    across_ref,
    within_ref,
    low_out,
    high_out,
    sums_out,
    row,
    past_row,
):
    accel_second = read_accel(accel_ref, 1)
    own = spread(row, own_ref[...])
    row[...] = total_ref[...]
    odd_chip = lax.axis_index("tile") & 2 == 2

    def side(low, message):
        outward = Q_MINUS if low else Q_PLUS
        past = jnp.where(odd_chip == low, within_ref[...], across_ref[...])
        solid = SOLID_MAX * smooth(own + spread(past_row, past), message[ROW_BLOCKS])
        adj_beside, adj_face, sens = boundary(
            low, message, solid, solid_ref[...], f_next, adj_ref, accel_second
        )
        out = low_out if low else high_out
        for i, q in enumerate(Q_ZERO):
            out[i] = adj_face[q]
        for i, q in enumerate(outward):
            out[len(Q_ZERO) + i] = adj_beside[q]
            out[len(Q_ZERO) + len(outward) + i] = adj_face[q]
        row[...] += sens + boundary_sens(low, adj_beside, adj_face, odd_ext)

    def both(low, high):
        side(True, low)
        side(False, high)

    even = is_even()
    pl.when(even)(lambda: both(from_b, from_a))
    pl.when(jnp.logical_not(even))(lambda: both(from_a, from_b))

    total = jnp.broadcast_to(jnp.sum(row[...], axis=0, keepdims=True), (8, 128))
    for step in (1, 2, 4):
        total = total + pltpu.roll(total, 128 - step, 1)
    total = jnp.where(lanes() % BLOCK == 0, total, 0.0)
    sums_out[...] = jnp.broadcast_to(total[0:1][None], sums_out.shape)


def turned(odd_ref, layer, q):
    return -odd_ref[q // 2, layer] if q % 2 else odd_ref[q // 2 - 1, layer]


def start_kernel(accel_ref, solid_ref, g_ref, mom_ref, low_ref, high_ref, out_ref):
    accel = read_accel(accel_ref, 0)
    solid = solid_ref[...]

    def layer(x, changed):
        g = {q: g_ref[q, x + 2] for q in range(Q)}
        g.update(changed)
        momentum = [mom_ref[1 + axis, x] for axis in range(3)]
        adjoint = collide_adjoint((mom_ref[0, x], momentum), g, solid, accel)
        for q in range(Q):
            out_ref[q, x] = adjoint[q]

    def inner(x, _):
        layer(x, {})
        return 0

    lax.fori_loop(2, 6, inner, 0)
    for side, face, behind, outward in ((low_ref, 0, 1, Q_MINUS), (high_ref, 7, 6, Q_PLUS)):
        layer(face, {q: side[i] for i, q in enumerate(Q_ZERO + outward)})
        first = len(Q_ZERO) + len(outward)
        layer(behind, {q: side[first + i] for i, q in enumerate(outward)})


def group_order(cases):
    places = (2, 1) + tuple(range(3, GROUP)) + (0,)
    listed = [(place, case) for half in (0, 1) for place in places for case in range(half, cases, 2)]
    listed.remove((3, 1))
    return [(3, 1)] + listed


def place_in_group():
    return (lax.axis_index("tile") - OFFSET) & (GROUP - 1)


def tile_total(sums_ref, cases, tile):
    ranks = [rank for rank, (place, _) in enumerate(group_order(cases)) if place == tile]
    return sum(sums_ref[rank] for rank in ranks)


def end_kernel(cases, sums_ref, out):
    first, last = tile_total(sums_ref, cases, 0), tile_total(sums_ref, cases, GROUP - 1)
    out[...] = jnp.where(place_in_group() == 0, first, last)


def update_kernel(
    cases,
    sums_ref,
    outside_ref,
    design_ref,
    mask_ref,
    first_ref,
    second_ref,
    design_out,
    first_out,
    second_out,
):
    place = place_in_group()
    totals = [tile_total(sums_ref, cases, tile) for tile in range(GROUP)]
    line = [outside_ref[...]] + totals + [outside_ref[...]]
    line = [jnp.broadcast_to(row, (8, 128)) for row in line]

    def pick(shift):
        value = line[shift]
        for k in range(1, GROUP):
            value = jnp.where(place == k, line[k + shift], value)
        return value

    gradient = SOLID_MAX * smooth(pick(0) + pick(2), pick(1))
    spots = jnp.minimum(lanes() * BLOCK, 127)
    gradient = jnp.take_along_axis(gradient, spots, axis=1)[0:1, 0:16]
    gradient = mask_ref[...].astype(jnp.float32) * gradient
    first = BETA_ONE * first_ref[...] + (1.0 - BETA_ONE) * gradient
    second = BETA_TWO * second_ref[...] + (1.0 - BETA_TWO) * gradient * gradient
    stepped = design_ref[...] - LEARN_RATE * (first * (1.0 / BIAS_ONE)) / (
        jnp.sqrt(second * (1.0 / BIAS_TWO)) + ADAM_EPS
    )
    design_out[...] = jnp.clip(stepped, 0.0, 1.0)
    first_out[...] = first
    second_out[...] = second


def tables(tiles, cases):
    run = RUN if tiles % RUN == 0 else tiles

    def device(tile, case):
        return (tile % tiles) * cases + case

    def near(tile, step, case):
        target = tile + step
        crossed = (target // run) != (tile // run)
        return device(target, case ^ 1 if crossed else case)

    found = {name: [] for name in ("chip", "beyond", "across", "within", "ends")}
    for tile in range(tiles):
        step = 1 if tile % 2 else -1
        for case in range(cases):
            here = device(tile, case)
            found["chip"].append((here, device(tile ^ 1, case)))
            found["beyond"].append((here, device(tile + step, case)))
            odd_chip = (tile // 2) % 2
            found["across"].append((here, near(tile, 2 if odd_chip else -2, case)))
            found["within"].append((here, near(tile, -2 if odd_chip else 2, case)))
            place = (tile - OFFSET) % GROUP
            if place == 0:
                found["ends"].append((here, device(tile - 1, case)))
            if place == GROUP - 1:
                found["ends"].append((here, device(tile + 1, case)))
    groups = [
        [device(OFFSET + g * GROUP + place, case) for place, case in group_order(cases)]
        for g in range(tiles // GROUP)
    ]
    return found, groups


VMEM_SPEC = pl.BlockSpec(memory_space=pltpu.VMEM)
HBM_SPEC = pl.BlockSpec(memory_space=pltpu.HBM)
F32 = jnp.float32


def body(
    tiles,
    cases,
    checkpoint,
    adjoint_field,
    accel_table,
    design,
    design_mask,
    first_moment,
    second_moment,
):
    axes = ("tile", "case")
    pairs, groups = tables(tiles, cases)
    f_zero = checkpoint.reshape(Q, 64, 128)
    adjoint = adjoint_field[0]
    flat = [a.reshape(1, 16) for a in (design, design_mask, first_moment, second_moment)]
    params = pltpu.CompilerParams(vmem_limit_bytes=32 * 1024 * 1024)

    def send(value, name):
        return lax.ppermute(value, axes, pairs[name])

    def call(kernel, name, out_shape, in_specs, scratch, *args):
        many = isinstance(out_shape, tuple)
        return pl.pallas_call(
            kernel,
            out_shape=out_shape,
            in_specs=in_specs,
            out_specs=[VMEM_SPEC] * len(out_shape) if many else VMEM_SPEC,
            scratch_shapes=scratch,
            compiler_params=params,
            name=name,
        )(*args)

    def shape(*dims):
        return jax.ShapeDtypeStruct(dims, F32)

    row = pltpu.VMEM((8, 128), F32)
    blocks, accel, *kept, f_zero, adjoint, to_b, to_a = call(
        enter_kernel,
        "load_and_pack",
        (
            shape(1, 16),
            shape(2, 3, 8, 128),
            shape(1, 16),
            jax.ShapeDtypeStruct((1, 16), jnp.int32),
            shape(1, 16),
            shape(1, 16),
            jax.ShapeDtypeStruct((Q, 64, 128), jnp.bfloat16),
            shape(Q, 8, 8, 128),
            shape(B_ROWS, 8, 128),
            shape(ROWS, 8, 128),
        ),
        [HBM_SPEC] * 7,
        [pltpu.SMEM((2, 3), jnp.int32), pltpu.SemaphoreType.DMA((7,)), row],
        *(
            pltpu.with_memory_space_constraint(a, pltpu.HBM)
            for a in (*flat[:2], accel_table[0], *flat[2:], f_zero, adjoint)
        ),
    )
    from_b = send(to_b, "beyond")
    from_a = send(to_a, "chip")
    within = send(blocks, "within")
    across = send(blocks, "across")
    g_one, f_next, odd, mom, solid, total = call(
        interior_kernel,
        "interior",
        (
            shape(Q, 12, 8, 128),
            shape(Q, 14, 8, 128),
            shape(len(PAIRS), 12, 8, 128),
            shape(4, 8, 8, 128),
            shape(8, 128),
            shape(8, 128),
        ),
        [VMEM_SPEC] * 6,
        [row],
        accel,
        f_zero,
        adjoint,
        from_a,
        from_b,
        blocks,
    )
    face = shape(len(Q_ZERO) + 2 * len(Q_PLUS), 8, 128)
    low, high, sums = call(
        sides_kernel,
        "sides",
        (face, face, shape(GROUP * cases, 1, 128)),
        [VMEM_SPEC] * 11,
        [row, row],
        accel,
        adjoint,
        from_a,
        from_b,
        blocks,
        solid,
        f_next,
        odd,
        total,
        across,
        within,
    )
    sums, low = lax.optimization_barrier((sums, low))
    shared = lax.all_to_all(sums, axes, 0, 0, axis_index_groups=groups, tiled=True)
    start = call(
        start_kernel,
        "adjoint_start",
        shape(Q, 8, 8, 128),
        [VMEM_SPEC] * 6,
        [],
        accel,
        solid,
        g_one,
        mom,
        low,
        high,
    )
    ends = call(
        functools.partial(end_kernel, cases),
        "group_end",
        shape(1, 128),
        [VMEM_SPEC],
        [],
        shared,
    )
    ends, start = lax.optimization_barrier((ends, start))
    outside = send(ends, "ends")
    small = shape(1, 16)
    updated = call(
        functools.partial(update_kernel, cases),
        "update",
        (small, small, small),
        [VMEM_SPEC] * 6,
        [],
        shared,
        outside,
        *kept,
    )
    return (start[None],) + tuple(u.reshape(1, 1, 16) for u in updated)


def solution(mesh):
    placed = (
        P("case", None, "tile", None, None),
        P("case", None, "tile", None, None),
        P("case", None, None),
        P("tile", None, None),
        P("tile", None, None),
        P("tile", None, None),
        P("tile", None, None),
    )
    return jax.shard_map(
        functools.partial(body, mesh.shape["tile"], mesh.shape["case"]),
        mesh=mesh,
        in_specs=placed,
        out_specs=(
            P("case", None, "tile", None, None),
            P("tile", None, None),
            P("tile", None, None),
            P("tile", None, None),
        ),
        check_vma=False,
    )
```
